32 devices in a mesh: ctx: 8 (over z, y), tp: 4 (over x, core).
Axes of the slice: x: 2, y: 2, z: 4, core: 2. Of those that a mesh axis runs over, the one named last changes fastest.
Arguments:
- gate_in: bfloat16 [1024, 4096], P('ctx', 'tp'), may hold values from -250 to 250, as said below
- conv_in: bfloat16 [1024, 4096], P('ctx', 'tp'), may hold values from -6 to 6
- value_in: bfloat16 [1024, 4096], P('ctx', 'tp'), may hold values from -6 to 6
- filter_taps: float32 [128, 4096], P(None, 'tp'), may hold values from -0.5 to 0.5
- norm_gain: float32 [4096], P('tp'), may hold values from 0.1 to 1.9
- qkv_weight: bfloat16 [4096, 3, 2048], P(None, None, 'tp'), may hold values from -0.5 to 0.5
Outputs:
- attended: bfloat16 [1024, 2048], P('ctx', 'tp')
The draws below stay inside these ranges and needn't reach their ends.
Inputs may be any that keep to these rules, and one draw needn't show every extreme that they name: `gate_in`: gate values; channels and bases carry different scales.
All inputs are finite; a program needn't handle non-finite values.
Results may differ from the reference program's by a relative error of at most 0.027.
Values may be sent and summed in bfloat16 or wider, within the bound.
No kernel may reach another device: no remote copies, remote signals or barrier semaphores. Data moves between devices by JAX's collectives and lax.ppermute only.
A program may use at most 192 MiB of HBM per device.

```python
import math
import jax
import jax.numpy as jnp
from jax import lax

D = 4096
FILTER = 128
HEAD_DIM = 128
HEADS = 16
LENGTH = 1024


def draw_gate_in(key, part):
    first, second = jax.random.split(key, 2)
    base = jnp.clip(jax.random.normal(first, (LENGTH, D), jnp.float32), -6.0, 6.0)
    channel_scale = jnp.exp(jnp.log(10.0) * jnp.arange(D, dtype=jnp.float32) / D)
    row_scale = jnp.exp(jnp.log(10.0) * jax.random.uniform(second, (LENGTH, 1), jnp.float32))
    return (base * channel_scale[None, :] * row_scale / 2.5).astype(jnp.bfloat16)


def draw_qkv_weight(key, part):
    first = jax.random.fold_in(key, 0)
    width = HEADS * HEAD_DIM
    base = jnp.clip(jax.random.normal(first, (D, 3, width), jnp.float32), -6.0, 6.0) * D ** (-0.5)
    base = jnp.clip(base, -0.5, 0.5)
    return base.astype(jnp.bfloat16)


def shard_levels(own_key, extent, shards, least, high):
    level = 1.0
    for position, parts in shards:
        heights = jax.random.uniform(jax.random.fold_in(jax.random.fold_in(own_key, 6), position), (parts,), jnp.float32, least / len(shards), high / len(shards))
        level = level * jnp.repeat(jnp.exp(heights), extent[position] // parts).reshape((-1,) + (1,) * (len(extent) - 1 - position))
    return level


def normal_values(key, dims, spread, bound, pieces=(), kind=jnp.bfloat16):
    values = jax.random.normal(key, dims, jnp.float32) * spread
    if len(pieces) > 0:
        values = shard_levels(key, dims, pieces, -0.22, 0.18) * values
    return jnp.clip(values, min=-bound, max=bound).astype(kind)


def setup_inputs(seed: int = 0) -> dict:
    arg_keys = jax.random.split(jax.random.key(seed), 7)
    return {
        "gate_in": draw_gate_in(jax.random.fold_in(arg_keys[6], 71), 0),
        "conv_in": normal_values(arg_keys[1], (LENGTH, D), 1.0, 6.0, ((0, 8), (1, 4))),
        "value_in": normal_values(arg_keys[2], (LENGTH, D), 1.0, 6.0, ((0, 8), (1, 4))),
        "filter_taps": normal_values(arg_keys[3], (FILTER, D), FILTER ** -0.5, 0.5, ((1, 4),), jnp.float32),
        "norm_gain": jnp.clip(1.0 + 0.18 * jax.random.normal(arg_keys[4], (D,), jnp.float32), 0.1, 1.9),
        "qkv_weight": draw_qkv_weight(jax.random.fold_in(arg_keys[6], 71), 0),
    }


def causal_filter(full, taps):
    span = taps.shape[0]
    channels = full.shape[1]
    group = math.gcd(channels, 64)
    nblocks = full.shape[0] // span
    blocks = full.reshape(nblocks, span, channels)
    diff = jnp.arange(span, dtype=jnp.int32)[:, None] - jnp.arange(span, dtype=jnp.int32)[None, :]
    cur_idx = jnp.clip(diff, 0, span - 1)
    prev_idx = jnp.clip(diff + span, 0, span - 1)

    def one_group(start):
        tgroup = lax.dynamic_slice_in_dim(taps, start, group, 1)
        tcur = jnp.where((diff >= 0)[:, :, None], tgroup[cur_idx], 0.0)
        tprev = jnp.where((diff < 0)[:, :, None], tgroup[prev_idx], 0.0)
        bgroup = lax.dynamic_slice_in_dim(blocks, start, group, 2)
        out = jnp.einsum('bsc,isc->bic', bgroup[1:], tcur, precision=lax.Precision.HIGHEST)
        out = out + jnp.einsum('bsc,isc->bic', bgroup[:-1], tprev, precision=lax.Precision.HIGHEST)
        return out
    starts = (jnp.arange(channels // group) * group).astype(jnp.int32)
    result = lax.map(one_group, starts)
    return result.transpose(1, 2, 0, 3).reshape((nblocks - 1) * span, channels)

def reference(gate_in, conv_in, value_in, filter_taps, norm_gain, qkv_weight):
    mixed = (conv_in.astype(jnp.float32) * value_in.astype(jnp.float32)).astype(jnp.bfloat16)
    mixed = lax.optimization_barrier(mixed).astype(jnp.float32)
    full = jnp.concatenate([jnp.zeros((FILTER, D), jnp.float32), mixed], axis=0)
    filtered = causal_filter(full, filter_taps)
    hyena = (gate_in.astype(jnp.float32) * filtered).astype(jnp.bfloat16)
    hyena = lax.optimization_barrier(hyena).astype(jnp.float32)
    msq = lax.optimization_barrier(jnp.mean(hyena * hyena, axis=1))
    normed = (hyena * lax.rsqrt(msq + 1e-06)[:, None] * norm_gain[None, :]).astype(jnp.bfloat16)
    flat = qkv_weight.reshape(D, 3 * HEADS * HEAD_DIM)
    proj = jnp.dot(normed, flat, preferred_element_type=jnp.float32).astype(jnp.bfloat16)
    proj = proj.reshape(LENGTH, 3, HEADS, HEAD_DIM)
    query = proj[:, 0].astype(jnp.float32)
    key = proj[:, 1].astype(jnp.float32)
    value = proj[:, 2].astype(jnp.float32)
    block = math.gcd(LENGTH, 128)
    key_pos = jnp.arange(LENGTH, dtype=jnp.int32)
    scale = 1.0 / math.sqrt(HEAD_DIM)

    def attend(start):
        qblock = lax.dynamic_slice_in_dim(query, start, block, 0)
        qpos = start + jnp.arange(block, dtype=jnp.int32)
        scores = jnp.einsum('qhd,khd->hqk', qblock, key) * scale
        allowed = (qpos[:, None] >= key_pos[None, :])[None]
        scores = jnp.where(allowed, scores, -1e+30)
        rowmax = lax.optimization_barrier(jnp.max(scores, axis=2, keepdims=True))
        expo = jnp.where(allowed, jnp.exp(scores - rowmax), 0.0)
        total = lax.optimization_barrier(jnp.sum(expo, axis=2))
        weights = expo.astype(jnp.bfloat16).astype(jnp.float32)
        out = jnp.einsum('hqk,khd->qhd', weights, value) / total.T[:, :, None]
        return out.astype(jnp.bfloat16)
    starts = (jnp.arange(LENGTH // block) * block).astype(jnp.int32)
    blocks = lax.map(attend, starts)
    return blocks.reshape(LENGTH, HEADS * HEAD_DIM)
```

```python
import functools
import math

import jax
import jax.numpy as jnp
from jax import lax
from jax.experimental import pallas as pl
from jax.experimental.pallas import tpu as pltpu
from jax.sharding import PartitionSpec as P

HEAD_DIM = 128
LANES = 128
SLAB = 8
SPAN_OUT = 16
SPAN_IN = 8
EPS = 1e-06
BF16 = jnp.bfloat16
F32 = jnp.float32
VMEM = pl.BlockSpec(memory_space=pltpu.VMEM)


def to_slabs(source, target, first, rows):
    for group in range(SLAB):
        target[pl.ds(first * SLAB + group, rows, stride=SLAB), :] = source[
            :, group * LANES : (group + 1) * LANES
        ].astype(F32)


def slab(ref, index):
    return ref[pl.ds(pl.multiple_of(index * SLAB, SLAB), SLAB), :]


def add_taps(sums, x_ref, tap_ref, x_first, tap_first):
    taps = [slab(tap_ref, tap_first + d) for d in range(1 - SPAN_IN, SPAN_OUT)]
    sums = list(sums)
    for b in range(SPAN_IN):
        x = slab(x_ref, x_first + b)
        for a in range(SPAN_OUT):
            sums[a] = sums[a] + taps[a - b + SPAN_IN - 1] * x
    return tuple(sums)


def own_kernel(rows, span, mixed_ref, taps_ref, sums_ref, tap_ref, x_ref):
    tap_ref[pl.ds(0, SPAN_OUT * SLAB), :] = jnp.zeros((SPAN_OUT * SLAB, LANES), F32)
    tap_ref[pl.ds((SPAN_OUT + span) * SLAB, SPAN_OUT * SLAB), :] = jnp.zeros(
        (SPAN_OUT * SLAB, LANES), F32
    )
    to_slabs(taps_ref, tap_ref, SPAN_OUT, span)
    to_slabs(mixed_ref, x_ref, 0, rows)

    def block(t, _):
        def step(s, sums):
            return add_taps(
                sums, x_ref, tap_ref, s * SPAN_IN, SPAN_OUT + t * SPAN_OUT - s * SPAN_IN
            )

        sums = lax.fori_loop(
            0,
            (t + 1) * (SPAN_OUT // SPAN_IN),
            step,
            tuple(jnp.zeros((SLAB, LANES), F32) for _ in range(SPAN_OUT)),
        )
        for a in range(SPAN_OUT):
            sums_ref[
                pl.ds(pl.multiple_of((t * SPAN_OUT + a) * SLAB, SLAB), SLAB), :
            ] = sums[a]
        return 0

    lax.fori_loop(0, rows // SPAN_OUT, block, 0)


def rim_kernel(rows, span, rim_ref, sums_ref, tap_ref, gate_ref, hyena_ref, x_ref, full_ref):
    to_slabs(rim_ref, x_ref, 0, rows)

    def block(t, _):
        def step(s, sums):
            return add_taps(
                sums, x_ref, tap_ref, s * SPAN_IN, SPAN_OUT + rows + t * SPAN_OUT - s * SPAN_IN
            )

        sums = lax.fori_loop(
            t * (SPAN_OUT // SPAN_IN),
            rows // SPAN_IN,
            step,
            tuple(slab(sums_ref, t * SPAN_OUT + a) for a in range(SPAN_OUT)),
        )
        for a in range(SPAN_OUT):
            full_ref[
                pl.ds(pl.multiple_of((t * SPAN_OUT + a) * SLAB, SLAB), SLAB), :
            ] = sums[a]
        return 0

    lax.fori_loop(0, rows // SPAN_OUT, block, 0)
    for group in range(SLAB):
        lanes = slice(group * LANES, (group + 1) * LANES)
        hyena_ref[:, lanes] = (
            gate_ref[:, lanes].astype(F32) * full_ref[pl.ds(group, rows, stride=SLAB), :]
        ).astype(BF16)


def own_part(mixed, taps):
    rows, span = mixed.shape[0], taps.shape[0]
    return pl.pallas_call(
        functools.partial(own_kernel, rows, span),
        out_shape=(
            jax.ShapeDtypeStruct((rows * SLAB, LANES), F32),
            jax.ShapeDtypeStruct(((span + 2 * SPAN_OUT) * SLAB, LANES), F32),
        ),
        in_specs=[VMEM] * 2,
        out_specs=(VMEM, VMEM),
        scratch_shapes=[pltpu.VMEM((rows * SLAB, LANES), F32)],
        compiler_params=pltpu.CompilerParams(vmem_limit_bytes=16 << 20),
        cost_estimate=pl.CostEstimate(
            flops=rows * span * SLAB * LANES, bytes_accessed=1 << 21, transcendentals=0
        ),
        name="fir_own_rows",
    )(mixed, taps)


def rim_part(rim, sums, taps, gate):
    rows = gate.shape[0]
    span = taps.shape[0] // SLAB - 2 * SPAN_OUT
    return pl.pallas_call(
        functools.partial(rim_kernel, rows, span),
        out_shape=jax.ShapeDtypeStruct((rows, SLAB * LANES), BF16),
        in_specs=[VMEM] * 4,
        out_specs=VMEM,
        scratch_shapes=[pltpu.VMEM((rows * SLAB, LANES), F32)] * 2,
        compiler_params=pltpu.CompilerParams(vmem_limit_bytes=16 << 20),
        cost_estimate=pl.CostEstimate(
            flops=rows * span * SLAB * LANES, bytes_accessed=1 << 21, transcendentals=0
        ),
        name="fir_rim_rows",
    )(rim, sums, taps, gate)


def hyena_of(gate, mixed, rim, taps):
    rows, channels = gate.shape
    wide = SLAB * LANES
    pieces = []
    for first in range(0, channels, wide):
        cut = slice(first, min(first + wide, channels))

        def widened(value):
            part = value[:, cut]
            return jnp.pad(part, ((0, 0), (0, wide - part.shape[1])))

        sums, slabs = own_part(widened(mixed), widened(taps))
        piece = rim_part(widened(rim), sums, slabs, widened(gate))
        pieces.append(piece[:, : cut.stop - cut.start])
    return pieces[0] if len(pieces) == 1 else jnp.concatenate(pieces, axis=1)


def project(blocks, offsets, gain_ref, weight_ref, acc_ref, ssq_ref, me):
    width = weight_ref.shape[2]
    for block_ref, offset in zip(blocks, offsets):
        owner = jnp.bitwise_xor(me, offset)
        channels = block_ref.shape[1]
        hyena = block_ref[...].astype(F32)
        squares = hyena * hyena
        total = ssq_ref[...]
        for first in range(0, channels, LANES):
            total = total + squares[:, first : first + LANES]
        ssq_ref[...] = total
        scaled = (hyena * gain_ref[pl.ds(owner, 1), :]).astype(BF16)
        start = pl.multiple_of(owner * channels, channels)
        for which in range(3):
            acc_ref[:, which * width : (which + 1) * width] += jnp.dot(
                scaled,
                weight_ref[which, pl.ds(start, channels), :],
                preferred_element_type=F32,
            )


def first_kernel(offsets, me_ref, *refs):
    n = len(offsets)
    blocks, (gain_ref, weight_ref, acc_ref, ssq_ref) = refs[:n], refs[n:]
    acc_ref[...] = jnp.zeros_like(acc_ref)
    ssq_ref[...] = jnp.zeros_like(ssq_ref)
    project(blocks, offsets, gain_ref, weight_ref, acc_ref, ssq_ref, me_ref[0])


def last_kernel(offsets, model, me_ref, *refs):
    n = len(offsets)
    blocks, (gain_ref, weight_ref, acc_in, ssq_in), rest = refs[:n], refs[n : n + 4], refs[n + 4 :]
    outs, (acc_ref, ssq_ref) = rest[:-2], rest[-2:]
    acc_ref[...] = acc_in[...]
    ssq_ref[...] = ssq_in[...]
    project(blocks, offsets, gain_ref, weight_ref, acc_ref, ssq_ref, me_ref[0])
    msq = jnp.sum(ssq_ref[...], axis=1, keepdims=True) / model
    scale = lax.rsqrt(msq + EPS)
    rows = acc_ref.shape[0]
    width = weight_ref.shape[2]
    for k, out in enumerate(outs):
        head = jnp.bitwise_xor(me_ref[1], k)
        for which in range(3):
            lanes = pl.ds(pl.multiple_of(which * width + head * HEAD_DIM, LANES), HEAD_DIM)
            out[which * rows : (which + 1) * rows, :] = (acc_ref[:, lanes] * scale).astype(BF16)


def qkv_messages(mine, others, gain, weight, spot, model):
    rows = mine[0][1].shape[0]
    width = weight.shape[2]
    smem = pl.BlockSpec(memory_space=pltpu.SMEM)
    params = pltpu.CompilerParams(vmem_limit_bytes=24 << 20)
    acc_shape = jax.ShapeDtypeStruct((rows, 3 * width), F32)
    ssq_shape = jax.ShapeDtypeStruct((rows, LANES), F32)

    def cost(blocks):
        macs = len(blocks) * rows * blocks[0][1].shape[1] * 3 * width
        return pl.CostEstimate(
            flops=2 * macs, bytes_accessed=2 * macs // rows + (2 << 20), transcendentals=0
        )

    acc, ssq = pl.pallas_call(
        functools.partial(first_kernel, tuple(o for o, _ in mine)),
        out_shape=(acc_shape, ssq_shape),
        in_specs=[smem] + [VMEM] * (len(mine) + 2),
        out_specs=(VMEM, VMEM),
        compiler_params=params,
        cost_estimate=cost(mine),
        name="qkv_first_blocks",
    )(spot, *[b for _, b in mine], gain, weight)
    heads = width // HEAD_DIM
    return pl.pallas_call(
        functools.partial(last_kernel, tuple(o for o, _ in others), model),
        out_shape=tuple(
            jax.ShapeDtypeStruct((3 * rows, HEAD_DIM), BF16) for _ in range(heads)
        ),
        in_specs=[smem] + [VMEM] * (len(others) + 4),
        out_specs=tuple(VMEM for _ in range(heads)),
        scratch_shapes=[pltpu.VMEM(acc_shape.shape, F32), pltpu.VMEM(ssq_shape.shape, F32)],
        compiler_params=params,
        cost_estimate=cost(others),
        name="qkv_last_blocks",
    )(spot, *[b for _, b in others], gain, weight, acc, ssq)


def attend_kernel(rows, count, spot_ref, *refs):
    mine, theirs = refs[:count], refs[count : 2 * count]
    outs = refs[2 * count : 3 * count]
    key_ref, value_ref = refs[3 * count :]
    z, c = spot_ref[1], spot_ref[3]
    for k in range(count):
        for part, held in enumerate((mine[k], theirs[k])):
            spot = (k * 2 + part) * rows
            key_ref[spot : spot + rows, :] = held[rows : 2 * rows, :]
            value_ref[spot : spot + rows, :] = held[2 * rows : 3 * rows, :]
    total_rows = 2 * count * rows
    within = lax.broadcasted_iota(jnp.int32, (1, total_rows), 1)
    place = within // rows
    key_pos = (
        2 * jnp.bitwise_xor(place // 2, z) + jnp.bitwise_xor(place % 2, c)
    ) * rows + within % rows
    scale = 1.0 / math.sqrt(HEAD_DIM)
    for k in range(count):
        first = (2 * jnp.bitwise_xor(z, k) + c) * rows
        query_pos = first + lax.broadcasted_iota(jnp.int32, (rows, 1), 0)
        scores = (
            lax.dot_general(
                mine[k][:rows, :],
                key_ref[...],
                (((1,), (1,)), ((), ())),
                preferred_element_type=F32,
            )
            * scale
        )
        allowed = query_pos >= key_pos
        scores = jnp.where(allowed, scores, -1e30)
        top = jnp.max(scores, axis=1, keepdims=True)
        expo = jnp.exp(scores - top)
        total = jnp.sum(expo, axis=1, keepdims=True)
        summed = jnp.dot(expo.astype(BF16), value_ref[...], preferred_element_type=F32)
        outs[k][...] = (summed / total).astype(BF16)


def attend(mine, theirs, spot):
    count = len(mine)
    rows = mine[0].shape[0] // 3
    return pl.pallas_call(
        functools.partial(attend_kernel, rows, count),
        out_shape=tuple(jax.ShapeDtypeStruct((rows, HEAD_DIM), BF16) for _ in range(count)),
        in_specs=[pl.BlockSpec(memory_space=pltpu.SMEM)] + [VMEM] * (2 * count),
        out_specs=tuple(VMEM for _ in range(count)),
        scratch_shapes=[pltpu.VMEM((2 * count * rows, HEAD_DIM), BF16)] * 2,
        compiler_params=pltpu.CompilerParams(vmem_limit_bytes=24 << 20),
        name="attention",
    )(spot, *mine, *theirs)


def join_kernel(spot_ref, *refs):
    blocks, out = refs[:-1], refs[-1]
    for k, block in enumerate(blocks):
        head = jnp.bitwise_xor(spot_ref[1], k)
        out[:, pl.ds(pl.multiple_of(head * HEAD_DIM, LANES), HEAD_DIM)] = block[...]


def join(blocks, spot):
    rows = blocks[0].shape[0]
    return pl.pallas_call(
        join_kernel,
        out_shape=jax.ShapeDtypeStruct((rows, len(blocks) * HEAD_DIM), BF16),
        in_specs=[pl.BlockSpec(memory_space=pltpu.SMEM)] + [VMEM] * len(blocks),
        out_specs=VMEM,
        name="join_heads",
    )(spot, *blocks)


def gathered_attention(message, heads, rows):
    parts = jnp.stack([m.reshape(3, rows, HEAD_DIM) for m in message], axis=2)
    query, keys, values = parts[0], parts[1], parts[2]
    keys = lax.all_gather(keys, "ctx", axis=0, tiled=True)
    values = lax.all_gather(values, "ctx", axis=0, tiled=True)
    query_pos = lax.axis_index("ctx") * rows + jnp.arange(rows, dtype=jnp.int32)
    key_pos = jnp.arange(keys.shape[0], dtype=jnp.int32)
    scores = jnp.einsum("qhd,khd->hqk", query, keys, preferred_element_type=F32)
    allowed = (query_pos[:, None] >= key_pos[None, :])[None]
    scores = jnp.where(allowed, scores / math.sqrt(HEAD_DIM), -1e30)
    expo = jnp.where(allowed, jnp.exp(scores - jnp.max(scores, axis=2, keepdims=True)), 0.0)
    total = jnp.sum(expo, axis=2)
    summed = jnp.einsum("hqk,khd->qhd", expo.astype(BF16), values, preferred_element_type=F32)
    return (summed / total.T[:, :, None]).astype(BF16).reshape(rows, heads * HEAD_DIM)


def body(gate_in, conv_in, value_in, filter_taps, norm_gain, qkv_weight):
    rows, channels = gate_in.shape
    ctx, tp = lax.axis_size("ctx"), lax.axis_size("tp")
    at_ctx, at_tp = lax.axis_index("ctx"), lax.axis_index("tp")
    weight = jnp.transpose(qkv_weight, (1, 0, 2))
    heads = weight.shape[2] // HEAD_DIM
    model = weight.shape[1]
    chip_per_head = heads * 2 == ctx and heads & (heads - 1) == 0
    at_z = at_ctx // 2 if chip_per_head else jnp.zeros_like(at_ctx)
    spot = jnp.stack([at_tp, at_z, at_ctx % 2, at_tp % 2]).astype(jnp.int32)

    gain = lax.all_gather(norm_gain, "tp", axis=0)
    mixed = (conv_in.astype(F32) * value_in.astype(F32)).astype(BF16)
    rim = lax.ppermute(mixed, "ctx", [(i, i + 1) for i in range(ctx - 1)])
    hyena = hyena_of(gate_in, mixed, rim, filter_taps)

    def swapped(value, by):
        return lax.ppermute(value, "tp", [(i, i ^ by) for i in range(tp)])

    far = []
    by = tp // 2
    while by > 1:
        far = far + [(o ^ by, swapped(b, by)) for o, b in [(0, hyena)] + far]
        by //= 2
    mine = [(0, hyena), (1, swapped(hyena, 1))]
    others = far + [(o ^ 1, swapped(b, 1)) for o, b in far]
    messages = qkv_messages(mine, others, gain, weight, spot, model)
    if not chip_per_head:
        return gathered_attention(messages, heads, rows)

    def routed(value, k):
        pairs = []
        for z in range(ctx // 2):
            for y in range(2):
                for x in range(tp // 2):
                    for c in range(2):
                        source = (2 * z + y) * tp + 2 * x + c
                        pairs.append((source, (2 * (z ^ k) + c) * tp + 2 * x + y))
        return lax.ppermute(value, ("ctx", "tp"), pairs)

    held = [routed(messages[k], k) for k in range(heads)]
    theirs = [swapped(value, 1) for value in held]
    parts = attend(held, theirs, spot)
    return join([routed(parts[k], k) for k in range(heads)], spot)


def solution(mesh):
    placed = (
        P("ctx", "tp"),
        P("ctx", "tp"),
        P("ctx", "tp"),
        P(None, "tp"),
        P("tp"),
        P(None, None, "tp"),
    )
    return jax.shard_map(
        body, mesh=mesh, in_specs=placed, out_specs=P("ctx", "tp"), check_vma=False
    )
```

```python
import functools
import math

import jax
import jax.numpy as jnp
from jax import lax
from jax.experimental import pallas as pl
from jax.experimental.pallas import tpu as pltpu
from jax.sharding import PartitionSpec as P

HEAD_DIM = 128
LANES = 128
SLAB = 8
SPAN_OUT = 16
SPAN_IN = 8
EPS = 1e-06
BF16 = jnp.bfloat16
F32 = jnp.float32
VMEM = pl.BlockSpec(memory_space=pltpu.VMEM)


def to_slabs(source, target, first, rows):
    for group in range(SLAB):
        target[pl.ds(first * SLAB + group, rows, stride=SLAB), :] = source[
            :, group * LANES : (group + 1) * LANES
        ].astype(F32)


def slab(ref, index):
    return ref[pl.ds(pl.multiple_of(index * SLAB, SLAB), SLAB), :]


def add_taps(sums, x_ref, tap_ref, x_first, tap_first):
    taps = [slab(tap_ref, tap_first + d) for d in range(1 - SPAN_IN, SPAN_OUT)]
    sums = list(sums)
    for b in range(SPAN_IN):
        x = slab(x_ref, x_first + b)
        for a in range(SPAN_OUT):
            sums[a] = sums[a] + taps[a - b + SPAN_IN - 1] * x
    return tuple(sums)


def own_kernel(
    rows,
    span,
    mixed_ref,
    taps_hbm,
    gate_hbm,
    weight_hbm,
    sums_ref,
    tap_ref,
    gate_ref,
    weight_ref,
    x_ref,
    taps_ref,
    sems,
):
    copies = [
        pltpu.make_async_copy(taps_hbm, taps_ref, sems.at[0]),
        pltpu.make_async_copy(gate_hbm, gate_ref, sems.at[1]),
        pltpu.make_async_copy(weight_hbm, weight_ref, sems.at[2]),
    ]
    for copy in copies:
        copy.start()
    tap_ref[pl.ds(0, SPAN_OUT * SLAB), :] = jnp.zeros((SPAN_OUT * SLAB, LANES), F32)
    tap_ref[pl.ds((SPAN_OUT + span) * SLAB, SPAN_OUT * SLAB), :] = jnp.zeros(
        (SPAN_OUT * SLAB, LANES), F32
    )
    to_slabs(mixed_ref, x_ref, 0, rows)
    copies[0].wait()
    to_slabs(taps_ref, tap_ref, SPAN_OUT, span)

    def block(t, _):
        def step(s, sums):
            return add_taps(
                sums, x_ref, tap_ref, s * SPAN_IN, SPAN_OUT + t * SPAN_OUT - s * SPAN_IN
            )

        sums = lax.fori_loop(
            0,
            (t + 1) * (SPAN_OUT // SPAN_IN),
            step,
            tuple(jnp.zeros((SLAB, LANES), F32) for _ in range(SPAN_OUT)),
        )
        for a in range(SPAN_OUT):
            sums_ref[
                pl.ds(pl.multiple_of((t * SPAN_OUT + a) * SLAB, SLAB), SLAB), :
            ] = sums[a]
        return 0

    lax.fori_loop(0, rows // SPAN_OUT, block, 0)
    for copy in copies[1:]:
        copy.wait()


def rim_kernel(rows, span, rim_ref, sums_ref, tap_ref, gate_ref, gain_ref, sent_ref, x_ref, full_ref):
    to_slabs(rim_ref, x_ref, 0, rows)

    def block(t, _):
        def step(s, sums):
            return add_taps(
                sums, x_ref, tap_ref, s * SPAN_IN, SPAN_OUT + rows + t * SPAN_OUT - s * SPAN_IN
            )

        sums = lax.fori_loop(
            t * (SPAN_OUT // SPAN_IN),
            rows // SPAN_IN,
            step,
            tuple(slab(sums_ref, t * SPAN_OUT + a) for a in range(SPAN_OUT)),
        )
        for a in range(SPAN_OUT):
            full_ref[
                pl.ds(pl.multiple_of((t * SPAN_OUT + a) * SLAB, SLAB), SLAB), :
            ] = sums[a]
        return 0

    lax.fori_loop(0, rows // SPAN_OUT, block, 0)
    squares = jnp.zeros((rows, LANES), F32)
    for group in range(SLAB):
        lanes = slice(group * LANES, (group + 1) * LANES)
        hyena = (
            gate_ref[:, lanes].astype(F32) * full_ref[pl.ds(group, rows, stride=SLAB), :]
        ).astype(BF16).astype(F32)
        squares = squares + hyena * hyena
        sent_ref[:, lanes] = (hyena * gain_ref[:, lanes]).astype(BF16)
    total = jnp.sum(squares, axis=1, keepdims=True)
    pieces = []
    for _ in range(3):
        pieces.append(total.astype(BF16).astype(F32))
        total = total - pieces[-1]
    lane = lax.broadcasted_iota(jnp.int32, (rows, LANES), 1)
    row = jnp.zeros((rows, LANES), F32)
    for place, piece in enumerate(pieces):
        row = jnp.where(lane == place, piece, row)
    sent_ref[:, SLAB * LANES :] = row.astype(BF16)


def own_part(mixed, taps, gate, weight):
    rows, span = mixed.shape[0], taps.shape[0]
    wide = SLAB * LANES
    hbm = pl.BlockSpec(memory_space=pltpu.HBM)
    return pl.pallas_call(
        functools.partial(own_kernel, rows, span),
        out_shape=(
            jax.ShapeDtypeStruct((rows * SLAB, LANES), F32),
            jax.ShapeDtypeStruct(((span + 2 * SPAN_OUT) * SLAB, LANES), F32),
            jax.ShapeDtypeStruct(gate.shape, BF16),
            jax.ShapeDtypeStruct(weight.shape, BF16),
        ),
        in_specs=[VMEM, hbm, hbm, hbm],
        out_specs=(VMEM, VMEM, VMEM, VMEM),
        scratch_shapes=[
            pltpu.VMEM((rows * SLAB, LANES), F32),
            pltpu.VMEM((span, wide), F32),
            pltpu.SemaphoreType.DMA((3,)),
        ],
        compiler_params=pltpu.CompilerParams(vmem_limit_bytes=32 << 20),
        cost_estimate=pl.CostEstimate(
            flops=rows * span * wide, bytes_accessed=12 << 20, transcendentals=0
        ),
        name="fir_own_rows",
    )(mixed, taps, gate, weight)


def rim_part(rim, sums, taps, gate, gain):
    rows = gate.shape[0]
    wide = SLAB * LANES
    span = taps.shape[0] // SLAB - 2 * SPAN_OUT
    return pl.pallas_call(
        functools.partial(rim_kernel, rows, span),
        out_shape=jax.ShapeDtypeStruct((rows, wide + LANES), BF16),
        in_specs=[VMEM] * 5,
        out_specs=VMEM,
        scratch_shapes=[pltpu.VMEM((rows * SLAB, LANES), F32)] * 2,
        compiler_params=pltpu.CompilerParams(vmem_limit_bytes=16 << 20),
        cost_estimate=pl.CostEstimate(
            flops=rows * span * wide, bytes_accessed=1 << 21, transcendentals=0
        ),
        name="fir_rim_rows",
    )(rim, sums, taps, gate, gain)


def project(blocks, offsets, weight_ref, acc_ref, ssq_ref, me):
    width = weight_ref.shape[2]
    for block_ref, offset in zip(blocks, offsets):
        owner = jnp.bitwise_xor(me, offset)
        channels = block_ref.shape[1] - LANES
        ssq_ref[...] += block_ref[:, channels:].astype(F32)
        start = pl.multiple_of(owner * channels, channels)
        for which in range(3):
            acc_ref[:, which * width : (which + 1) * width] += jnp.dot(
                block_ref[:, :channels],
                weight_ref[which, pl.ds(start, channels), :],
                preferred_element_type=F32,
            )


def first_kernel(offsets, me_ref, *refs):
    n = len(offsets)
    blocks, (weight_ref, acc_ref, ssq_ref) = refs[:n], refs[n:]
    acc_ref[...] = jnp.zeros_like(acc_ref)
    ssq_ref[...] = jnp.zeros_like(ssq_ref)
    project(blocks, offsets, weight_ref, acc_ref, ssq_ref, me_ref[0])


def last_kernel(offsets, model, me_ref, *refs):
    n = len(offsets)
    blocks, (weight_ref, acc_in, ssq_in), rest = refs[:n], refs[n : n + 3], refs[n + 3 :]
    outs, (acc_ref, ssq_ref) = rest[:-2], rest[-2:]
    acc_ref[...] = acc_in[...]
    ssq_ref[...] = ssq_in[...]
    project(blocks, offsets, weight_ref, acc_ref, ssq_ref, me_ref[0])
    msq = jnp.sum(ssq_ref[...], axis=1, keepdims=True) / model
    scale = lax.rsqrt(msq + EPS)
    rows = acc_ref.shape[0]
    width = weight_ref.shape[2]
    for k, out in enumerate(outs):
        head = jnp.bitwise_xor(me_ref[1], k)
        for which in range(3):
            lanes = pl.ds(pl.multiple_of(which * width + head * HEAD_DIM, LANES), HEAD_DIM)
            out[which * rows : (which + 1) * rows, :] = (acc_ref[:, lanes] * scale).astype(BF16)


def qkv_messages(mine, others, weight, spot, model):
    rows = mine[0][1].shape[0]
    width = weight.shape[2]
    smem = pl.BlockSpec(memory_space=pltpu.SMEM)
    params = pltpu.CompilerParams(vmem_limit_bytes=24 << 20)
    acc_shape = jax.ShapeDtypeStruct((rows, 3 * width), F32)
    ssq_shape = jax.ShapeDtypeStruct((rows, LANES), F32)

    def cost(blocks):
        macs = len(blocks) * rows * blocks[0][1].shape[1] * 3 * width
        return pl.CostEstimate(
            flops=2 * macs, bytes_accessed=2 * macs // rows + (2 << 20), transcendentals=0
        )

    acc, ssq = pl.pallas_call(
        functools.partial(first_kernel, tuple(o for o, _ in mine)),
        out_shape=(acc_shape, ssq_shape),
        in_specs=[smem] + [VMEM] * (len(mine) + 1),
        out_specs=(VMEM, VMEM),
        compiler_params=params,
        cost_estimate=cost(mine),
        name="qkv_first_blocks",
    )(spot, *[b for _, b in mine], weight)
    heads = width // HEAD_DIM
    return pl.pallas_call(
        functools.partial(last_kernel, tuple(o for o, _ in others), model),
        out_shape=tuple(
            jax.ShapeDtypeStruct((3 * rows, HEAD_DIM), BF16) for _ in range(heads)
        ),
        in_specs=[smem] + [VMEM] * (len(others) + 3),
        out_specs=tuple(VMEM for _ in range(heads)),
        scratch_shapes=[pltpu.VMEM(acc_shape.shape, F32), pltpu.VMEM(ssq_shape.shape, F32)],
        compiler_params=params,
        cost_estimate=cost(others),
        name="qkv_last_blocks",
    )(spot, *[b for _, b in others], weight, acc, ssq)


def attend_kernel(rows, count, spot_ref, *refs):
    mine, theirs = refs[:count], refs[count : 2 * count]
    outs = refs[2 * count : 3 * count]
    key_ref, value_ref = refs[3 * count :]
    z, c = spot_ref[1], spot_ref[3]
    for k in range(count):
        for part, held in enumerate((mine[k], theirs[k])):
            spot = (k * 2 + part) * rows
            key_ref[spot : spot + rows, :] = held[rows : 2 * rows, :]
            value_ref[spot : spot + rows, :] = held[2 * rows : 3 * rows, :]
    total_rows = 2 * count * rows
    within = lax.broadcasted_iota(jnp.int32, (1, total_rows), 1)
    place = within // rows
    key_pos = (
        2 * jnp.bitwise_xor(place // 2, z) + jnp.bitwise_xor(place % 2, c)
    ) * rows + within % rows
    scale = 1.0 / math.sqrt(HEAD_DIM)
    for k in range(count):
        first = (2 * jnp.bitwise_xor(z, k) + c) * rows
        query_pos = first + lax.broadcasted_iota(jnp.int32, (rows, 1), 0)
        scores = (
            lax.dot_general(
                mine[k][:rows, :],
                key_ref[...],
                (((1,), (1,)), ((), ())),
                preferred_element_type=F32,
            )
            * scale
        )
        allowed = query_pos >= key_pos
        scores = jnp.where(allowed, scores, -1e30)
        top = jnp.max(scores, axis=1, keepdims=True)
        expo = jnp.exp(scores - top)
        total = jnp.sum(expo, axis=1, keepdims=True)
        summed = jnp.dot(expo.astype(BF16), value_ref[...], preferred_element_type=F32)
        outs[k][...] = (summed / total).astype(BF16)


def attend(mine, theirs, spot):
    count = len(mine)
    rows = mine[0].shape[0] // 3
    return pl.pallas_call(
        functools.partial(attend_kernel, rows, count),
        out_shape=tuple(jax.ShapeDtypeStruct((rows, HEAD_DIM), BF16) for _ in range(count)),
        in_specs=[pl.BlockSpec(memory_space=pltpu.SMEM)] + [VMEM] * (2 * count),
        out_specs=tuple(VMEM for _ in range(count)),
        scratch_shapes=[pltpu.VMEM((2 * count * rows, HEAD_DIM), BF16)] * 2,
        compiler_params=pltpu.CompilerParams(vmem_limit_bytes=24 << 20),
        name="attention",
    )(spot, *mine, *theirs)


def join_kernel(spot_ref, *refs):
    blocks, out = refs[:-1], refs[-1]
    for k, block in enumerate(blocks):
        head = jnp.bitwise_xor(spot_ref[1], k)
        out[:, pl.ds(pl.multiple_of(head * HEAD_DIM, LANES), HEAD_DIM)] = block[...]


def join(blocks, spot):
    rows = blocks[0].shape[0]
    return pl.pallas_call(
        join_kernel,
        out_shape=jax.ShapeDtypeStruct((rows, len(blocks) * HEAD_DIM), BF16),
        in_specs=[pl.BlockSpec(memory_space=pltpu.SMEM)] + [VMEM] * len(blocks),
        out_specs=VMEM,
        compiler_params=pltpu.CompilerParams(vmem_limit_bytes=4 << 20),
        name="join_heads",
    )(spot, *blocks)


def gathered_attention(message, heads, rows):
    parts = jnp.stack([m.reshape(3, rows, HEAD_DIM) for m in message], axis=2)
    query, keys, values = parts[0], parts[1], parts[2]
    keys = lax.all_gather(keys, "ctx", axis=0, tiled=True)
    values = lax.all_gather(values, "ctx", axis=0, tiled=True)
    query_pos = lax.axis_index("ctx") * rows + jnp.arange(rows, dtype=jnp.int32)
    key_pos = jnp.arange(keys.shape[0], dtype=jnp.int32)
    scores = jnp.einsum("qhd,khd->hqk", query, keys, preferred_element_type=F32)
    allowed = (query_pos[:, None] >= key_pos[None, :])[None]
    scores = jnp.where(allowed, scores / math.sqrt(HEAD_DIM), -1e30)
    expo = jnp.where(allowed, jnp.exp(scores - jnp.max(scores, axis=2, keepdims=True)), 0.0)
    total = jnp.sum(expo, axis=2)
    summed = jnp.einsum("hqk,khd->qhd", expo.astype(BF16), values, preferred_element_type=F32)
    return (summed / total.T[:, :, None]).astype(BF16).reshape(rows, heads * HEAD_DIM)


def body(gate_in, conv_in, value_in, filter_taps, norm_gain, qkv_weight):
    rows, channels = gate_in.shape
    ctx, tp = lax.axis_size("ctx"), lax.axis_size("tp")
    at_ctx, at_tp = lax.axis_index("ctx"), lax.axis_index("tp")
    weight = jnp.transpose(qkv_weight, (1, 0, 2))
    heads = weight.shape[2] // HEAD_DIM
    model = weight.shape[1]
    chip_per_head = heads * 2 == ctx and heads & (heads - 1) == 0
    at_z = at_ctx // 2 if chip_per_head else jnp.zeros_like(at_ctx)
    spot = jnp.stack([at_tp, at_z, at_ctx % 2, at_tp % 2]).astype(jnp.int32)

    mixed = (conv_in.astype(F32) * value_in.astype(F32)).astype(BF16)
    rim = lax.ppermute(mixed, "ctx", [(i, i + 1) for i in range(ctx - 1)])
    wide = SLAB * LANES

    def widened(value):
        return jnp.pad(value, ((0, 0), (0, wide - channels))) if channels < wide else value

    sums, taps, gate, weight = own_part(
        widened(mixed), widened(filter_taps), widened(gate_in), weight
    )
    sent = rim_part(widened(rim), sums, taps, gate, widened(norm_gain[None]))
    if channels < wide:
        sent = jnp.concatenate([sent[:, :channels], sent[:, wide:]], axis=1)

    def swapped(value, by):
        return lax.ppermute(value, "tp", [(i, i ^ by) for i in range(tp)])

    far = []
    by = tp // 2
    while by > 1:
        far = far + [(o ^ by, swapped(b, by)) for o, b in [(0, sent)] + far]
        by //= 2
    mine = [(0, sent), (1, swapped(sent, 1))]
    others = far + [(o ^ 1, swapped(b, 1)) for o, b in far]
    messages = qkv_messages(mine, others, weight, spot, model)
    if not chip_per_head:
        return gathered_attention(messages, heads, rows)

    def routed(value, k):
        pairs = []
        for z in range(ctx // 2):
            for y in range(2):
                for x in range(tp // 2):
                    for c in range(2):
                        source = (2 * z + y) * tp + 2 * x + c
                        pairs.append((source, (2 * (z ^ k) + c) * tp + 2 * x + y))
        return lax.ppermute(value, ("ctx", "tp"), pairs)

    held = [routed(messages[k], k) for k in range(heads)]
    theirs = [swapped(value, 1) for value in held]
    parts = attend(held, theirs, spot)
    return join([routed(parts[k], k) for k in range(heads)], spot)


def solution(mesh):
    placed = (
        P("ctx", "tp"),
        P("ctx", "tp"),
        P("ctx", "tp"),
        P(None, "tp"),
        P("tp"),
        P(None, None, "tp"),
    )
    return jax.shard_map(
        body, mesh=mesh, in_specs=placed, out_specs=P("ctx", "tp"), check_vma=False
    )
```

```python
import functools
import math

import jax
import jax.numpy as jnp
from jax import lax
from jax.experimental import pallas as pl
from jax.experimental.pallas import tpu as pltpu
from jax.sharding import PartitionSpec as P

HEAD_DIM = 128
LANES = 128
SLAB = 8
SPAN_OUT = 16
SPAN_IN = 8
EPS = 1e-06
BF16 = jnp.bfloat16
F32 = jnp.float32
VMEM = pl.BlockSpec(memory_space=pltpu.VMEM)


def to_slabs(source, target, first, rows):
    for group in range(SLAB):
        target[pl.ds(first * SLAB + group, rows, stride=SLAB), :] = source[
            :, group * LANES : (group + 1) * LANES
        ].astype(F32)


def slab(ref, index):
    return ref[pl.ds(pl.multiple_of(index * SLAB, SLAB), SLAB), :]


def add_taps(sums, x_ref, tap_ref, x_first, tap_first):
    taps = [slab(tap_ref, tap_first + d) for d in range(1 - SPAN_IN, SPAN_OUT)]
    sums = list(sums)
    for b in range(SPAN_IN):
        x = slab(x_ref, x_first + b)
        for a in range(SPAN_OUT):
            sums[a] = sums[a] + taps[a - b + SPAN_IN - 1] * x
    return tuple(sums)


def own_kernel(
    rows,
    span,
    mixed_ref,
    taps_hbm,
    gate_hbm,
    weight_hbm,
    sums_ref,
    tap_ref,
    gate_ref,
    weight_ref,
    x_ref,
    taps_ref,
    sems,
):
    copies = [
        pltpu.make_async_copy(taps_hbm, taps_ref, sems.at[0]),
        pltpu.make_async_copy(gate_hbm, gate_ref, sems.at[1]),
        pltpu.make_async_copy(weight_hbm, weight_ref, sems.at[2]),
    ]
    for copy in copies:
        copy.start()
    tap_ref[pl.ds(0, SPAN_OUT * SLAB), :] = jnp.zeros((SPAN_OUT * SLAB, LANES), F32)
    tap_ref[pl.ds((SPAN_OUT + span) * SLAB, SPAN_OUT * SLAB), :] = jnp.zeros(
        (SPAN_OUT * SLAB, LANES), F32
    )
    to_slabs(mixed_ref, x_ref, 0, rows)
    copies[0].wait()
    to_slabs(taps_ref, tap_ref, SPAN_OUT, span)

    def block(t, _):
        def step(s, sums):
            return add_taps(
                sums, x_ref, tap_ref, s * SPAN_IN, SPAN_OUT + t * SPAN_OUT - s * SPAN_IN
            )

        sums = lax.fori_loop(
            0,
            (t + 1) * (SPAN_OUT // SPAN_IN),
            step,
            tuple(jnp.zeros((SLAB, LANES), F32) for _ in range(SPAN_OUT)),
        )
        for a in range(SPAN_OUT):
            sums_ref[
                pl.ds(pl.multiple_of((t * SPAN_OUT + a) * SLAB, SLAB), SLAB), :
            ] = sums[a]
        return 0

    lax.fori_loop(0, rows // SPAN_OUT, block, 0)
    for copy in copies[1:]:
        copy.wait()


def rim_kernel(rows, span, rim_ref, sums_ref, tap_ref, gate_ref, gain_ref, sent_ref, x_ref, full_ref):
    to_slabs(rim_ref, x_ref, 0, rows)

    def block(t, _):
        def step(s, sums):
            return add_taps(
                sums, x_ref, tap_ref, s * SPAN_IN, SPAN_OUT + rows + t * SPAN_OUT - s * SPAN_IN
            )

        sums = lax.fori_loop(
            t * (SPAN_OUT // SPAN_IN),
            rows // SPAN_IN,
            step,
            tuple(slab(sums_ref, t * SPAN_OUT + a) for a in range(SPAN_OUT)),
        )
        for a in range(SPAN_OUT):
            full_ref[
                pl.ds(pl.multiple_of((t * SPAN_OUT + a) * SLAB, SLAB), SLAB), :
            ] = sums[a]
        return 0

    lax.fori_loop(0, rows // SPAN_OUT, block, 0)
    squares = jnp.zeros((rows, LANES), F32)
    for group in range(SLAB):
        lanes = slice(group * LANES, (group + 1) * LANES)
        hyena = (
            gate_ref[:, lanes].astype(F32) * full_ref[pl.ds(group, rows, stride=SLAB), :]
        ).astype(BF16).astype(F32)
        squares = squares + hyena * hyena
        sent_ref[:, lanes] = (hyena * gain_ref[:, lanes]).astype(BF16)
    total = jnp.sum(squares, axis=1, keepdims=True)
    pieces = []
    for _ in range(3):
        pieces.append(total.astype(BF16).astype(F32))
        total = total - pieces[-1]
    lane = lax.broadcasted_iota(jnp.int32, (rows, LANES), 1)
    row = jnp.zeros((rows, LANES), F32)
    for place, piece in enumerate(pieces):
        row = jnp.where(lane == place, piece, row)
    sent_ref[:, SLAB * LANES :] = row.astype(BF16)


def own_part(mixed, taps, gate, weight):
    rows, span = mixed.shape[0], taps.shape[0]
    wide = SLAB * LANES
    hbm = pl.BlockSpec(memory_space=pltpu.HBM)
    return pl.pallas_call(
        functools.partial(own_kernel, rows, span),
        out_shape=(
            jax.ShapeDtypeStruct((rows * SLAB, LANES), F32),
            jax.ShapeDtypeStruct(((span + 2 * SPAN_OUT) * SLAB, LANES), F32),
            jax.ShapeDtypeStruct(gate.shape, BF16),
            jax.ShapeDtypeStruct(weight.shape, BF16),
        ),
        in_specs=[VMEM, hbm, hbm, hbm],
        out_specs=(VMEM, VMEM, VMEM, VMEM),
        scratch_shapes=[
            pltpu.VMEM((rows * SLAB, LANES), F32),
            pltpu.VMEM((span, wide), F32),
            pltpu.SemaphoreType.DMA((3,)),
        ],
        compiler_params=pltpu.CompilerParams(vmem_limit_bytes=32 << 20),
        cost_estimate=pl.CostEstimate(
            flops=rows * span * wide, bytes_accessed=12 << 20, transcendentals=0
        ),
        name="fir_own_rows",
    )(mixed, taps, gate, weight)


def rim_part(rim, sums, taps, gate, gain):
    rows = gate.shape[0]
    wide = SLAB * LANES
    span = taps.shape[0] // SLAB - 2 * SPAN_OUT
    return pl.pallas_call(
        functools.partial(rim_kernel, rows, span),
        out_shape=jax.ShapeDtypeStruct((rows, wide + LANES), BF16),
        in_specs=[VMEM] * 5,
        out_specs=VMEM,
        scratch_shapes=[pltpu.VMEM((rows * SLAB, LANES), F32)] * 2,
        compiler_params=pltpu.CompilerParams(vmem_limit_bytes=16 << 20),
        cost_estimate=pl.CostEstimate(
            flops=rows * span * wide, bytes_accessed=1 << 21, transcendentals=0
        ),
        name="fir_rim_rows",
    )(rim, sums, taps, gate, gain)


def project(blocks, offsets, weight_ref, acc_ref, ssq_ref, me):
    width = weight_ref.shape[2]
    for block_ref, offset in zip(blocks, offsets):
        owner = jnp.bitwise_xor(me, offset)
        channels = block_ref.shape[1] - LANES
        ssq_ref[...] += block_ref[:, channels:].astype(F32)
        start = pl.multiple_of(owner * channels, channels)
        for which in range(3):
            acc_ref[:, which * width : (which + 1) * width] += jnp.dot(
                block_ref[:, :channels],
                weight_ref[which, pl.ds(start, channels), :],
                preferred_element_type=F32,
            )


def first_kernel(offsets, *refs):
    n = len(offsets)
    blocks, (weight_ref, acc_ref, ssq_ref) = refs[:n], refs[n:]
    acc_ref[...] = jnp.zeros_like(acc_ref)
    ssq_ref[...] = jnp.zeros_like(ssq_ref)
    project(blocks, offsets, weight_ref, acc_ref, ssq_ref, lax.axis_index("tp"))


def last_kernel(offsets, model, spread, *refs):
    n = len(offsets)
    blocks, (weight_ref, acc_in, ssq_in), rest = refs[:n], refs[n : n + 3], refs[n + 3 :]
    outs, (acc_ref, ssq_ref) = rest[:-2], rest[-2:]
    acc_ref[...] = acc_in[...]
    ssq_ref[...] = ssq_in[...]
    project(blocks, offsets, weight_ref, acc_ref, ssq_ref, lax.axis_index("tp"))
    msq = jnp.sum(ssq_ref[...], axis=1, keepdims=True) / model
    scale = lax.rsqrt(msq + EPS)
    rows = acc_ref.shape[0]
    width = weight_ref.shape[2]
    for k, out in enumerate(outs):
        head = jnp.bitwise_xor(lax.axis_index("ctx") // 2, k) if spread else k
        for which in range(3):
            lanes = pl.ds(pl.multiple_of(which * width + head * HEAD_DIM, LANES), HEAD_DIM)
            out[which * rows : (which + 1) * rows, :] = (acc_ref[:, lanes] * scale).astype(BF16)


def qkv_messages(mine, others, weight, model, spread):
    rows = mine[0][1].shape[0]
    width = weight.shape[2]
    params = pltpu.CompilerParams(vmem_limit_bytes=24 << 20)
    acc_shape = jax.ShapeDtypeStruct((rows, 3 * width), F32)
    ssq_shape = jax.ShapeDtypeStruct((rows, LANES), F32)

    def cost(blocks):
        macs = len(blocks) * rows * blocks[0][1].shape[1] * 3 * width
        return pl.CostEstimate(
            flops=2 * macs, bytes_accessed=2 * macs // rows + (2 << 20), transcendentals=0
        )

    acc, ssq = pl.pallas_call(
        functools.partial(first_kernel, tuple(o for o, _ in mine)),
        out_shape=(acc_shape, ssq_shape),
        in_specs=[VMEM] * (len(mine) + 1),
        out_specs=(VMEM, VMEM),
        compiler_params=params,
        cost_estimate=cost(mine),
        name="qkv_first_blocks",
    )(*[b for _, b in mine], weight)
    heads = width // HEAD_DIM
    return pl.pallas_call(
        functools.partial(last_kernel, tuple(o for o, _ in others), model, spread),
        out_shape=tuple(
            jax.ShapeDtypeStruct((3 * rows, HEAD_DIM), BF16) for _ in range(heads)
        ),
        in_specs=[VMEM] * (len(others) + 3),
        out_specs=tuple(VMEM for _ in range(heads)),
        scratch_shapes=[pltpu.VMEM(acc_shape.shape, F32), pltpu.VMEM(ssq_shape.shape, F32)],
        compiler_params=params,
        cost_estimate=cost(others),
        name="qkv_last_blocks",
    )(*[b for _, b in others], weight, acc, ssq)


def attend_kernel(rows, count, *refs):
    mine, theirs = refs[:count], refs[count : 2 * count]
    outs = refs[2 * count : 3 * count]
    key_ref, value_ref = refs[3 * count :]
    z, c = lax.axis_index("ctx") // 2, lax.axis_index("tp") % 2
    for k in range(count):
        for part, held in enumerate((mine[k], theirs[k])):
            spot = (k * 2 + part) * rows
            key_ref[spot : spot + rows, :] = held[rows : 2 * rows, :]
            value_ref[spot : spot + rows, :] = held[2 * rows : 3 * rows, :]
    total_rows = 2 * count * rows
    within = lax.broadcasted_iota(jnp.int32, (1, total_rows), 1)
    place = within // rows
    key_pos = (
        2 * jnp.bitwise_xor(place // 2, z) + jnp.bitwise_xor(place % 2, c)
    ) * rows + within % rows
    scale = 1.0 / math.sqrt(HEAD_DIM)
    for k in range(count):
        first = (2 * jnp.bitwise_xor(z, k) + c) * rows
        query_pos = first + lax.broadcasted_iota(jnp.int32, (rows, 1), 0)
        scores = (
            lax.dot_general(
                mine[k][:rows, :],
                key_ref[...],
                (((1,), (1,)), ((), ())),
                preferred_element_type=F32,
            )
            * scale
        )
        allowed = query_pos >= key_pos
        scores = jnp.where(allowed, scores, -1e30)
        top = jnp.max(scores, axis=1, keepdims=True)
        expo = jnp.exp(scores - top)
        total = jnp.sum(expo, axis=1, keepdims=True)
        summed = jnp.dot(expo.astype(BF16), value_ref[...], preferred_element_type=F32)
        outs[k][...] = (summed / total).astype(BF16)


def attend(mine, theirs):
    count = len(mine)
    rows = mine[0].shape[0] // 3
    return pl.pallas_call(
        functools.partial(attend_kernel, rows, count),
        out_shape=tuple(jax.ShapeDtypeStruct((rows, HEAD_DIM), BF16) for _ in range(count)),
        in_specs=[VMEM] * (2 * count),
        out_specs=tuple(VMEM for _ in range(count)),
        scratch_shapes=[pltpu.VMEM((2 * count * rows, HEAD_DIM), BF16)] * 2,
        compiler_params=pltpu.CompilerParams(vmem_limit_bytes=24 << 20),
        name="attention",
    )(*mine, *theirs)


def join_kernel(*refs):
    blocks, out = refs[:-1], refs[-1]
    for k, block in enumerate(blocks):
        head = jnp.bitwise_xor(lax.axis_index("ctx") // 2, k)
        out[:, pl.ds(pl.multiple_of(head * HEAD_DIM, LANES), HEAD_DIM)] = block[...]


def join(blocks):
    rows = blocks[0].shape[0]
    return pl.pallas_call(
        join_kernel,
        out_shape=jax.ShapeDtypeStruct((rows, len(blocks) * HEAD_DIM), BF16),
        in_specs=[VMEM] * len(blocks),
        out_specs=VMEM,
        compiler_params=pltpu.CompilerParams(vmem_limit_bytes=4 << 20),
        name="join_heads",
    )(*blocks)


def gathered_attention(message, heads, rows):
    parts = jnp.stack([m.reshape(3, rows, HEAD_DIM) for m in message], axis=2)
    query, keys, values = parts[0], parts[1], parts[2]
    keys = lax.all_gather(keys, "ctx", axis=0, tiled=True)
    values = lax.all_gather(values, "ctx", axis=0, tiled=True)
    query_pos = lax.axis_index("ctx") * rows + jnp.arange(rows, dtype=jnp.int32)
    key_pos = jnp.arange(keys.shape[0], dtype=jnp.int32)
    scores = jnp.einsum("qhd,khd->hqk", query, keys, preferred_element_type=F32)
    allowed = (query_pos[:, None] >= key_pos[None, :])[None]
    scores = jnp.where(allowed, scores / math.sqrt(HEAD_DIM), -1e30)
    expo = jnp.where(allowed, jnp.exp(scores - jnp.max(scores, axis=2, keepdims=True)), 0.0)
    total = jnp.sum(expo, axis=2)
    summed = jnp.einsum("hqk,khd->qhd", expo.astype(BF16), values, preferred_element_type=F32)
    return (summed / total.T[:, :, None]).astype(BF16).reshape(rows, heads * HEAD_DIM)


def body(gate_in, conv_in, value_in, filter_taps, norm_gain, qkv_weight):
    rows, channels = gate_in.shape
    ctx, tp = lax.axis_size("ctx"), lax.axis_size("tp")
    weight = jnp.transpose(qkv_weight, (1, 0, 2))
    heads = weight.shape[2] // HEAD_DIM
    model = weight.shape[1]
    chip_per_head = heads * 2 == ctx and heads & (heads - 1) == 0

    mixed = (conv_in.astype(F32) * value_in.astype(F32)).astype(BF16)
    rim = lax.ppermute(mixed, "ctx", [(i, i + 1) for i in range(ctx - 1)])
    wide = SLAB * LANES

    def widened(value):
        return jnp.pad(value, ((0, 0), (0, wide - channels))) if channels < wide else value

    sums, taps, gate, weight = own_part(
        widened(mixed), widened(filter_taps), widened(gate_in), weight
    )
    sent = rim_part(widened(rim), sums, taps, gate, widened(norm_gain[None]))
    if channels < wide:
        sent = jnp.concatenate([sent[:, :channels], sent[:, wide:]], axis=1)

    def swapped(value, by):
        return lax.ppermute(value, "tp", [(i, i ^ by) for i in range(tp)])

    far = []
    by = tp // 2
    while by > 1:
        far = far + [(o ^ by, swapped(b, by)) for o, b in [(0, sent)] + far]
        by //= 2
    mine = [(0, sent), (1, swapped(sent, 1))]
    others = far + [(o ^ 1, swapped(b, 1)) for o, b in far]
    messages = qkv_messages(mine, others, weight, model, chip_per_head)
    if not chip_per_head:
        return gathered_attention(messages, heads, rows)

    def routed(value, k):
        pairs = []
        for z in range(ctx // 2):
            for y in range(2):
                for x in range(tp // 2):
                    for c in range(2):
                        source = (2 * z + y) * tp + 2 * x + c
                        pairs.append((source, (2 * (z ^ k) + c) * tp + 2 * x + y))
        return lax.ppermute(value, ("ctx", "tp"), pairs)

    held = [routed(messages[k], k) for k in range(heads)]
    theirs = [swapped(value, 1) for value in held]
    parts = attend(held, theirs)
    return join([routed(parts[k], k) for k in range(heads)])


def solution(mesh):
    placed = (
        P("ctx", "tp"),
        P("ctx", "tp"),
        P("ctx", "tp"),
        P(None, "tp"),
        P("tp"),
        P(None, None, "tp"),
    )
    return jax.shard_map(
        body, mesh=mesh, in_specs=placed, out_specs=P("ctx", "tp"), check_vma=False
    )
```

```python
import functools
import math

import jax
import jax.numpy as jnp
from jax import lax
from jax.experimental import pallas as pl
from jax.experimental.pallas import tpu as pltpu
from jax.sharding import PartitionSpec as P

HEAD_DIM = 128
LANES = 128
SLAB = 8
PHASES = 4
SUBS = 9
HELD = 8
EPS = 1e-06
BF16 = jnp.bfloat16
F32 = jnp.float32
VMEM = pl.BlockSpec(memory_space=pltpu.VMEM)
HBM = pl.BlockSpec(memory_space=pltpu.HBM)


def params(mib):
    return pltpu.CompilerParams(vmem_limit_bytes=mib << 20)


LATE = 1 << 28


def cost(weight=1024):
    return pl.CostEstimate(flops=0, bytes_accessed=weight, transcendentals=0)


def slabs(count):
    return jax.ShapeDtypeStruct((count * SLAB, LANES), F32)


def slab_scratch(count):
    return pltpu.VMEM((count * SLAB, LANES), F32)


def at(index):
    if not isinstance(index, int):
        return pl.ds(pl.multiple_of(index * SLAB, SLAB), SLAB)
    return pl.ds(index * SLAB, SLAB)


def to_slabs(source, target):
    for group in range(SLAB):
        target[pl.ds(group, source.shape[0], stride=SLAB), :] = source[
            :, group * LANES : (group + 1) * LANES
        ].astype(F32)


def to_subs(source, count, target):
    for n in range(count):
        x0, x1, x2, x3 = (source[at(PHASES * n + p), :] for p in range(PHASES))
        low, high = x0 + x1, x2 + x3
        for s, value in enumerate((x0, x2, x0 + x2, x1, x3, x1 + x3, low, high, low + high)):
            target[at(s * count + n), :] = value


def accumulate(sums, first, lag, taps, tap_at, x_ref, x_at, x_first, x_count, span):
    sums = list(sums)
    for start in range(x_first, x_first + x_count, HELD):
        places = range(start, min(start + HELD, x_first + x_count))
        used = {}
        for i in places:
            x = x_ref[at(x_at + (i - x_first)), :]
            for k in range(len(sums)):
                j = lag + first + k - i
                if 0 <= j < span:
                    if j not in used:
                        used[j] = taps[at(tap_at + j), :]
                    sums[k] = sums[k] + used[j] * x
    return sums


def finish(z_ref, count, full_ref):
    def z(s, k):
        return z_ref[at(s * (count + 1) + k), :]

    before = [z(s, 0) for s in range(SUBS)]
    for n in range(count):
        now = [z(s, n + 1) for s in range(SUBS)]

        def even(s):
            return now[s] + before[s + 1]

        def odd(s, held):
            return held[s + 2] - held[s] - held[s + 1]

        a_even, a_odd, b_even, b_odd = even(0), odd(0, now), even(3), odd(3, now)
        full_ref[at(PHASES * n), :] = a_even + odd(3, before)
        full_ref[at(PHASES * n + 1), :] = even(6) - a_even - b_even
        full_ref[at(PHASES * n + 2), :] = a_odd + b_even
        full_ref[at(PHASES * n + 3), :] = odd(6, now) - a_odd - b_odd
        before = now


def emit(full_ref, gate_ref, first, gain_ref, sent_ref):
    rows = sent_ref.shape[0]
    squares = jnp.zeros((rows, LANES), F32)
    for group in range(SLAB):
        lanes = slice(group * LANES, (group + 1) * LANES)
        hyena = (
            (
                gate_ref[first : first + rows, lanes].astype(F32)
                * full_ref[pl.ds(group, rows, stride=SLAB), :]
            )
            .astype(BF16)
            .astype(F32)
        )
        squares = squares + hyena * hyena
        sent_ref[:, lanes] = (hyena * gain_ref[:, lanes]).astype(BF16)
    total = jnp.sum(squares, axis=1, keepdims=True)
    pieces = []
    for _ in range(3):
        pieces.append(total.astype(BF16).astype(F32))
        total = total - pieces[-1]
    lane = lax.broadcasted_iota(jnp.int32, (rows, LANES), 1)
    row = jnp.zeros((rows, LANES), F32)
    for place, piece in enumerate(pieces):
        row = jnp.where(lane == place, piece, row)
    sent_ref[:, SLAB * LANES :] = row.astype(BF16)


def own_kernel(
    mixed_ref,
    taps_hbm,
    gate_hbm,
    weight_hbm,
    sums_low,
    sums_high,
    tap_subs,
    gate_ref,
    weight_ref,
    taps_ref,
    slab_ref,
    x_subs,
    sems,
):
    rows, span = mixed_ref.shape[0], taps_ref.shape[0]
    quarter, eighth = rows // PHASES, rows // PHASES // 2
    tap_quarter = span // PHASES
    blocks = lax.axis_size("tp")
    channels = weight_ref.shape[1] // blocks
    copies = [
        pltpu.make_async_copy(taps_hbm, taps_ref, sems.at[0]),
        pltpu.make_async_copy(gate_hbm, gate_ref, sems.at[1]),
    ] + [
        own_weights(weight_hbm, weight_ref, o, channels, sems.at[2 + o]) for o in range(blocks)
    ]
    for copy in copies:
        copy.start()
    to_slabs(mixed_ref, slab_ref)
    to_subs(slab_ref, quarter, x_subs)
    copies[0].wait()
    to_slabs(taps_ref, slab_ref)
    to_subs(slab_ref, tap_quarter, tap_subs)

    def sub(s, _):
        zero = jnp.zeros((SLAB, LANES), F32)
        sums_low[at(s * eighth), :] = zero
        for first in (0, eighth):
            sums = accumulate(
                [zero] * eighth, first, 0, tap_subs, s * tap_quarter, x_subs, s * quarter,
                0, first + eighth, tap_quarter,
            )
            for k, value in enumerate(sums):
                n = first + k
                if n < eighth - 1:
                    sums_low[at(s * eighth + n + 1), :] = value
                else:
                    sums_high[at(s * (eighth + 1) + n + 1 - eighth), :] = value
        return 0

    lax.fori_loop(0, SUBS, sub, 0)
    for copy in copies[1:]:
        copy.wait()


def own_weights(weight_hbm, weight_ref, offset, channels, sem):
    owner = jnp.bitwise_xor(lax.axis_index("tp"), offset)
    return pltpu.make_async_copy(
        weight_hbm.at[:, pl.ds(pl.multiple_of(owner * channels, channels), channels), :],
        weight_ref.at[:, pl.ds(offset * channels, channels), :],
        sem,
    )


def own_part(mixed, taps, gate, weight, tp):
    rows, span = mixed.shape[0], taps.shape[0]
    quarter = rows // PHASES
    eighth = quarter // 2
    return pl.pallas_call(
        own_kernel,
        out_shape=(
            slabs(SUBS * eighth),
            slabs(SUBS * (eighth + 1)),
            slabs(SUBS * span // PHASES),
            jax.ShapeDtypeStruct(gate.shape, BF16),
            jax.ShapeDtypeStruct(weight.shape, BF16),
        ),
        in_specs=[VMEM, HBM, HBM, HBM],
        out_specs=(VMEM,) * 5,
        scratch_shapes=[
            pltpu.VMEM(taps.shape, F32),
            slab_scratch(max(rows, span)),
            slab_scratch(SUBS * quarter),
            pltpu.SemaphoreType.DMA((2 + tp,)),
        ],
        compiler_params=params(24),
        cost_estimate=cost(),
        name="fir_own_rows",
    )(mixed, *(pltpu.with_memory_space_constraint(v, pltpu.HBM) for v in (taps, gate, weight)))


def high_kernel(
    rim_ref, sums_ref, tap_subs, gate_ref, gain_ref, sent_ref, x_subs, last_ref, slab_ref, z_ref
):
    rows = sent_ref.shape[0]
    eighth = rows // PHASES
    tap_quarter = tap_subs.shape[0] // SLAB // SUBS
    to_slabs(rim_ref.at[pl.ds(rows, rows)], slab_ref)
    to_subs(slab_ref, eighth, x_subs)

    def sub(s, _):
        at_z = s * (eighth + 1)
        sums = [sums_ref[at(at_z + k), :] for k in range(eighth + 1)]
        sums = accumulate(
            sums, eighth - 1, 2 * eighth, tap_subs, s * tap_quarter, x_subs, s * eighth,
            eighth, eighth, tap_quarter,
        )
        for k, value in enumerate(sums):
            z_ref[at(at_z + k), :] = value
        last_ref[at(s), :] = sums[0]
        return 0

    lax.fori_loop(0, SUBS, sub, 0)
    finish(z_ref, eighth, slab_ref)
    emit(slab_ref, gate_ref, rows, gain_ref, sent_ref)


def high_part(rim, sums, taps, gate, gain):
    rows = rim.shape[0] // 2
    eighth = rows // PHASES
    return pl.pallas_call(
        high_kernel,
        out_shape=(
            jax.ShapeDtypeStruct((rows, (SLAB + 1) * LANES), BF16),
            slabs(SUBS * eighth),
            slabs(SUBS),
        ),
        in_specs=[VMEM] * 5,
        out_specs=(VMEM,) * 3,
        scratch_shapes=[slab_scratch(rows), slab_scratch(SUBS * (eighth + 1))],
        compiler_params=params(16),
        cost_estimate=cost(),
        name="fir_later_rows",
    )(rim, sums, taps, gate, gain)


def low_kernel(
    rim_ref,
    sums_ref,
    x_high,
    last_ref,
    tap_subs,
    gate_ref,
    gain_ref,
    sent_ref,
    slab_ref,
    x_subs,
    z_ref,
):
    rows = sent_ref.shape[0]
    eighth = rows // PHASES
    tap_quarter = tap_subs.shape[0] // SLAB // SUBS
    to_slabs(rim_ref.at[pl.ds(0, rows)], slab_ref)
    to_subs(slab_ref, eighth, x_subs)

    def sub(s, _):
        sums = [sums_ref[at(s * eighth + k), :] for k in range(eighth)]
        for x_ref, first in ((x_high, eighth), (x_subs, 0)):
            sums = accumulate(
                sums, -1, 2 * eighth, tap_subs, s * tap_quarter, x_ref, s * eighth,
                first, eighth, tap_quarter,
            )
        for k, value in enumerate(sums + [last_ref[at(s), :]]):
            z_ref[at(s * (eighth + 1) + k), :] = value
        return 0

    lax.fori_loop(0, SUBS, sub, 0)
    finish(z_ref, eighth, slab_ref)
    emit(slab_ref, gate_ref, 0, gain_ref, sent_ref)


def low_part(rim, sums, x_high, last, taps, gate, gain):
    rows = rim.shape[0] // 2
    eighth = rows // PHASES
    return pl.pallas_call(
        low_kernel,
        out_shape=jax.ShapeDtypeStruct((rows, (SLAB + 1) * LANES), BF16),
        in_specs=[VMEM] * 7,
        out_specs=VMEM,
        scratch_shapes=[
            slab_scratch(rows),
            slab_scratch(SUBS * eighth),
            slab_scratch(SUBS * (eighth + 1)),
        ],
        compiler_params=params(16),
        cost_estimate=cost(),
        name="fir_earlier_rows",
    )(rim, sums, x_high, last, taps, gate, gain)


def project(blocks, first, weight_ref, acc_ref, ssq_ref):
    width = weight_ref.shape[2]
    whole = [jnp.concatenate([low[...], high[...]], axis=0) for low, high in blocks]
    channels = whole[0].shape[1] - LANES
    for block in whole:
        ssq_ref[...] += block[:, channels:].astype(F32)
    for which in range(3):
        lanes = slice(which * width, (which + 1) * width)
        total = acc_ref[:, lanes]
        for place, block in enumerate(whole, first):
            total = total + jnp.dot(
                block[:, :channels],
                weight_ref[which, place * channels : (place + 1) * channels, :],
                preferred_element_type=F32,
            )
        acc_ref[:, lanes] = total


def first_kernel(*refs):
    blocks = ((refs[0], refs[1]), (refs[2], refs[3]))
    weight_ref, acc_ref, ssq_ref = refs[4:]
    acc_ref[...] = jnp.zeros_like(acc_ref)
    ssq_ref[...] = jnp.zeros_like(ssq_ref)
    project(blocks, 0, weight_ref, acc_ref, ssq_ref)


def first_projection(mine, weight):
    rows = 2 * mine[0][0].shape[0]
    return pl.pallas_call(
        first_kernel,
        out_shape=(
            jax.ShapeDtypeStruct((rows, 3 * weight.shape[2]), F32),
            jax.ShapeDtypeStruct((rows, LANES), F32),
        ),
        in_specs=[VMEM] * 5,
        out_specs=(VMEM,) * 2,
        compiler_params=params(24),
        cost_estimate=cost(),
        name="projections_near",
    )(*mine[0], *mine[1], weight)


def last_kernel(count, model, layout, *refs):
    blocks = [(refs[2 * n], refs[2 * n + 1]) for n in range(count)]
    weight_ref, acc_in, ssq_in = refs[2 * count : 2 * count + 3]
    outs, (acc_ref, ssq_ref) = refs[2 * count + 3 : -2], refs[-2:]
    acc_ref[...] = acc_in[...]
    ssq_ref[...] = ssq_in[...]
    project(blocks, 2, weight_ref, acc_ref, ssq_ref)
    msq = jnp.sum(ssq_ref[...], axis=1, keepdims=True) / model
    scale = lax.rsqrt(msq + EPS)
    rows = acc_ref.shape[0]
    width = weight_ref.shape[2]
    heads = width // HEAD_DIM
    place = lax.axis_index("ctx") % heads
    kept = {}
    for out, parts in zip(outs, layout):
        for spot, (which, k) in enumerate(parts):
            if (which, k) not in kept:
                head = jnp.bitwise_xor(place, k)
                lanes = pl.ds(pl.multiple_of(which * width + head * HEAD_DIM, LANES), HEAD_DIM)
                kept[which, k] = (acc_ref[:, lanes] * scale).astype(BF16)
            out[spot * rows : (spot + 1) * rows, :] = kept[which, k]


def last_projection(others, weight, acc, ssq, model, layout):
    rows = acc.shape[0]
    return pl.pallas_call(
        functools.partial(last_kernel, len(others), model, layout),
        out_shape=tuple(
            jax.ShapeDtypeStruct((len(parts) * rows, HEAD_DIM), BF16) for parts in layout
        ),
        in_specs=[VMEM] * (2 * len(others) + 3),
        out_specs=(VMEM,) * len(layout),
        scratch_shapes=[pltpu.VMEM(acc.shape, F32), pltpu.VMEM(ssq.shape, F32)],
        compiler_params=params(24),
        cost_estimate=cost(),
        name="projections_far",
    )(*[half for pair in others for half in pair], weight, acc, ssq)


def earlier_kernel(*refs):
    blocks, (key_ref, value_ref) = refs[:-2], refs[-2:]
    rows = blocks[0].shape[0] // 2
    for k, block in enumerate(blocks):
        key_ref[k * rows : (k + 1) * rows, :] = block[:rows, :]
        value_ref[k * rows : (k + 1) * rows, :] = block[rows:, :]


def earlier_group(blocks):
    shape = jax.ShapeDtypeStruct((blocks[0].shape[0] // 2 * len(blocks), HEAD_DIM), BF16)
    return pl.pallas_call(
        earlier_kernel,
        out_shape=(shape, shape),
        in_specs=[VMEM] * len(blocks),
        out_specs=(VMEM, VMEM),
        compiler_params=params(4),
        cost_estimate=cost(LATE),
        name="earlier_keys",
    )(*blocks)


def attend_kernel(rows, count, *refs):
    mine, (old_keys, old_values), outs = refs[:count], refs[count : count + 2], refs[count + 2 : -2]
    key_ref, value_ref = refs[-2:]
    place = lax.axis_index("ctx")
    group, p = place // count, place % count
    key_ref[: count * rows, :] = old_keys[...]
    value_ref[: count * rows, :] = old_values[...]
    for k in range(count):
        spot = slice((count + k) * rows, (count + k + 1) * rows)
        key_ref[spot, :] = mine[k][rows : 2 * rows, :]
        value_ref[spot, :] = mine[k][2 * rows : 3 * rows, :]
    column = lax.broadcasted_iota(jnp.int32, (1, 2 * count * rows), 1)
    block = jnp.bitwise_xor(column // rows % count, p)
    first = jnp.where(column < count * rows, jnp.where(group > 0, 0, 2 * count), group * count)
    key_pos = (first + block) * rows + column % rows
    scale = 1.0 / math.sqrt(HEAD_DIM)
    for k in range(count):
        start = (group * count + jnp.bitwise_xor(p, k)) * rows
        query_pos = start + lax.broadcasted_iota(jnp.int32, (rows, 1), 0)
        scores = (
            lax.dot_general(
                mine[k][:rows, :],
                key_ref[...],
                (((1,), (1,)), ((), ())),
                preferred_element_type=F32,
            )
            * scale
        )
        scores = jnp.where(query_pos >= key_pos, scores, -1e30)
        top = jnp.max(scores, axis=1, keepdims=True)
        expo = jnp.exp(scores - top)
        total = jnp.sum(expo, axis=1, keepdims=True)
        summed = jnp.dot(expo.astype(BF16), value_ref[...], preferred_element_type=F32)
        outs[k][...] = (summed / total).astype(BF16)


def attend(mine, earlier):
    count = len(mine)
    rows = mine[0].shape[0] // 3
    return pl.pallas_call(
        functools.partial(attend_kernel, rows, count),
        out_shape=tuple(jax.ShapeDtypeStruct((rows, HEAD_DIM), BF16) for _ in range(count)),
        in_specs=[VMEM] * (count + 2),
        out_specs=(VMEM,) * count,
        scratch_shapes=[pltpu.VMEM((2 * count * rows, HEAD_DIM), BF16)] * 2,
        compiler_params=params(24),
        cost_estimate=cost(),
        name="attention",
    )(*mine, *earlier)


def join_kernel(*refs):
    blocks, out = refs[:-1], refs[-1]
    for k, block in enumerate(blocks):
        head = jnp.bitwise_xor(lax.axis_index("ctx") % len(blocks), k)
        out[:, pl.ds(pl.multiple_of(head * HEAD_DIM, LANES), HEAD_DIM)] = block[...]


def join(blocks):
    rows = blocks[0].shape[0]
    return pl.pallas_call(
        join_kernel,
        out_shape=jax.ShapeDtypeStruct((rows, len(blocks) * HEAD_DIM), BF16),
        in_specs=[VMEM] * len(blocks),
        out_specs=VMEM,
        compiler_params=params(4),
        name="join_heads",
    )(*blocks)


def gathered_attention(message, heads, rows):
    order = jnp.bitwise_xor(lax.axis_index("ctx") % heads, jnp.arange(heads))
    query, keys, values = (
        m.reshape(heads, rows, HEAD_DIM)[order].transpose(1, 0, 2) for m in message
    )
    keys = lax.all_gather(keys, "ctx", axis=0, tiled=True)
    values = lax.all_gather(values, "ctx", axis=0, tiled=True)
    query_pos = lax.axis_index("ctx") * rows + jnp.arange(rows, dtype=jnp.int32)
    key_pos = jnp.arange(keys.shape[0], dtype=jnp.int32)
    scores = jnp.einsum("qhd,khd->hqk", query, keys, preferred_element_type=F32)
    allowed = (query_pos[:, None] >= key_pos[None, :])[None]
    scores = jnp.where(allowed, scores / math.sqrt(HEAD_DIM), -1e30)
    expo = jnp.where(allowed, jnp.exp(scores - jnp.max(scores, axis=2, keepdims=True)), 0.0)
    total = jnp.sum(expo, axis=2)
    summed = jnp.einsum("hqk,khd->qhd", expo.astype(BF16), values, preferred_element_type=F32)
    return (summed / total.T[:, :, None]).astype(BF16).reshape(rows, heads * HEAD_DIM)


def body(gate_in, conv_in, value_in, filter_taps, norm_gain, qkv_weight):
    rows, channels = gate_in.shape
    ctx, tp = lax.axis_size("ctx"), lax.axis_size("tp")
    weight = jnp.transpose(qkv_weight, (1, 0, 2))
    heads = weight.shape[2] // HEAD_DIM
    model = weight.shape[1]
    two_groups = heads == 4 and ctx == 2 * heads

    wide = SLAB * LANES

    def widened(value):
        return jnp.pad(value, ((0, 0), (0, wide - channels))) if channels < wide else value

    def narrowed(sent):
        if channels == wide:
            return sent
        return jnp.concatenate([sent[:, :channels], sent[:, wide:]], axis=1)

    def swapped(value, by):
        return lax.ppermute(value, "tp", [(i, i ^ by) for i in range(tp)])

    mixed = (conv_in.astype(F32) * value_in.astype(F32)).astype(BF16)
    rim = widened(lax.ppermute(mixed, "ctx", [(i, i + 1) for i in range(ctx - 1)]))
    gain = widened(norm_gain[None])
    sums_low, sums_high, taps, gate, weight = own_part(
        widened(mixed), widened(filter_taps), widened(gate_in), weight, tp
    )
    sent_high, x_high, last = high_part(rim, sums_high, taps, gate, gain)
    sent_high = narrowed(sent_high)
    near_high = swapped(sent_high, 1)
    rim, near_high = lax.optimization_barrier((rim, near_high))
    sent_low = narrowed(low_part(rim, sums_low, x_high, last, taps, gate, gain))
    sent = (sent_low, sent_high)

    far = []
    by = tp // 2
    while by > 1:
        far = far + [
            (o ^ by, tuple(swapped(part, by) for part in pair)) for o, pair in [(0, sent)] + far
        ]
        by //= 2
    mine = (sent, (swapped(sent_low, 1), near_high))
    acc, ssq = first_projection(mine, weight)
    places, pairs = [o for o, _ in far], [pair for _, pair in far]
    last_low, acc = lax.optimization_barrier((pairs[-1][0], acc))
    pairs[-1] = (last_low, pairs[-1][1])
    others = []
    for o, pair in sorted(zip(places, pairs), key=lambda item: item[0]):
        others += [pair, tuple(swapped(part, 1) for part in pair)]

    def parts(first, *which):
        return tuple((w, k) for k in which for w in range(first, 3))

    if not two_groups:
        layout = tuple(tuple((w, k) for k in range(heads)) for w in range(3))
        return gathered_attention(
            last_projection(others, weight, acc, ssq, model, layout), heads, rows
        )
    layout = tuple(parts(first, k) for first in (1, 0) for k in range(heads))
    sent = last_projection(others, weight, acc, ssq, model, layout)
    onward, inside = sent[:heads], sent[heads:]

    def within(value, k):
        return lax.ppermute(value, "ctx", [(i, i ^ k) for i in range(ctx)]) if k else value

    earlier = [
        lax.ppermute(onward[k], "ctx", [(i, heads + (i ^ k)) for i in range(heads)])
        for k in range(heads)
    ]
    held = [within(inside[k], k) for k in range(heads)]
    done = attend(held, earlier_group(earlier))
    return join([within(done[k], k) for k in range(heads - 1, -1, -1)][::-1])


def solution(mesh):
    placed = (
        P("ctx", "tp"),
        P("ctx", "tp"),
        P("ctx", "tp"),
        P(None, "tp"),
        P("tp"),
        P(None, None, "tp"),
    )
    return jax.shard_map(
        body, mesh=mesh, in_specs=placed, out_specs=P("ctx", "tp"), check_vma=False
    )
```

```python
import functools
import math

import jax
import jax.numpy as jnp
from jax import lax
from jax.experimental import pallas as pl
from jax.experimental.pallas import tpu as pltpu
from jax.sharding import PartitionSpec as P

HEAD_DIM = 128
LANES = 128
SLAB = 8
PHASES = 4
SUBS = 9
HELD = 8
EPS = 1e-06
BF16 = jnp.bfloat16
F32 = jnp.float32
VMEM = pl.BlockSpec(memory_space=pltpu.VMEM)
HBM = pl.BlockSpec(memory_space=pltpu.HBM)


def params(mib):
    return pltpu.CompilerParams(vmem_limit_bytes=mib << 20)


def cost():
    return pl.CostEstimate(flops=0, bytes_accessed=1024, transcendentals=0)


def slabs(count):
    return jax.ShapeDtypeStruct((count * SLAB, LANES), F32)


def slab_scratch(count):
    return pltpu.VMEM((count * SLAB, LANES), F32)


def at(index):
    if not isinstance(index, int):
        return pl.ds(pl.multiple_of(index * SLAB, SLAB), SLAB)
    return pl.ds(index * SLAB, SLAB)


def to_slabs(source, target):
    for group in range(SLAB):
        target[pl.ds(group, source.shape[0], stride=SLAB), :] = source[
            :, group * LANES : (group + 1) * LANES
        ].astype(F32)


def to_subs(source, count, target):
    for n in range(count):
        x0, x1, x2, x3 = (source[at(PHASES * n + p), :] for p in range(PHASES))
        low, high = x0 + x1, x2 + x3
        for s, value in enumerate((x0, x2, x0 + x2, x1, x3, x1 + x3, low, high, low + high)):
            target[at(s * count + n), :] = value


def accumulate(sums, first, lag, taps, tap_at, x_ref, x_at, x_first, x_count, span):
    sums = list(sums)
    for start in range(x_first, x_first + x_count, HELD):
        places = range(start, min(start + HELD, x_first + x_count))
        used = {}
        for i in places:
            x = x_ref[at(x_at + (i - x_first)), :]
            for k in range(len(sums)):
                j = lag + first + k - i
                if 0 <= j < span:
                    if j not in used:
                        used[j] = taps[at(tap_at + j), :]
                    sums[k] = sums[k] + used[j] * x
    return sums


def finish(z_ref, count, full_ref):
    def z(s, k):
        return z_ref[at(s * (count + 1) + k), :]

    before = [z(s, 0) for s in range(SUBS)]
    for n in range(count):
        now = [z(s, n + 1) for s in range(SUBS)]

        def even(s):
            return now[s] + before[s + 1]

        def odd(s, held):
            return held[s + 2] - held[s] - held[s + 1]

        a_even, a_odd, b_even, b_odd = even(0), odd(0, now), even(3), odd(3, now)
        full_ref[at(PHASES * n), :] = a_even + odd(3, before)
        full_ref[at(PHASES * n + 1), :] = even(6) - a_even - b_even
        full_ref[at(PHASES * n + 2), :] = a_odd + b_even
        full_ref[at(PHASES * n + 3), :] = odd(6, now) - a_odd - b_odd
        before = now


def emit(full_ref, gate_ref, first, gain_ref, sent_ref):
    rows = sent_ref.shape[0]
    squares = jnp.zeros((rows, LANES), F32)
    for group in range(SLAB):
        lanes = slice(group * LANES, (group + 1) * LANES)
        hyena = (
            (
                gate_ref[first : first + rows, lanes].astype(F32)
                * full_ref[pl.ds(group, rows, stride=SLAB), :]
            )
            .astype(BF16)
            .astype(F32)
        )
        squares = squares + hyena * hyena
        sent_ref[:, lanes] = (hyena * gain_ref[:, lanes]).astype(BF16)
    total = jnp.sum(squares, axis=1, keepdims=True)
    pieces = []
    for _ in range(3):
        pieces.append(total.astype(BF16).astype(F32))
        total = total - pieces[-1]
    lane = lax.broadcasted_iota(jnp.int32, (rows, LANES), 1)
    row = jnp.zeros((rows, LANES), F32)
    for place, piece in enumerate(pieces):
        row = jnp.where(lane == place, piece, row)
    sent_ref[:, SLAB * LANES :] = row.astype(BF16)


def own_kernel(
    mixed_ref,
    taps_hbm,
    gate_hbm,
    weight_hbm,
    sums_low,
    sums_high,
    tap_subs,
    gate_ref,
    weight_ref,
    taps_ref,
    slab_ref,
    x_subs,
    sems,
):
    rows, span = mixed_ref.shape[0], taps_ref.shape[0]
    quarter, eighth = rows // PHASES, rows // PHASES // 2
    tap_quarter = span // PHASES
    blocks = lax.axis_size("tp")
    channels = weight_ref.shape[1] // blocks
    copies = [
        pltpu.make_async_copy(taps_hbm, taps_ref, sems.at[0]),
        pltpu.make_async_copy(gate_hbm, gate_ref, sems.at[1]),
    ] + [
        own_weights(weight_hbm, weight_ref, o, channels, sems.at[2 + o]) for o in range(blocks)
    ]
    for copy in copies:
        copy.start()
    to_slabs(mixed_ref, slab_ref)
    to_subs(slab_ref, quarter, x_subs)
    copies[0].wait()
    to_slabs(taps_ref, slab_ref)
    to_subs(slab_ref, tap_quarter, tap_subs)

    def sub(s, _):
        zero = jnp.zeros((SLAB, LANES), F32)
        sums_low[at(s * eighth), :] = zero
        for first in (0, eighth):
            sums = accumulate(
                [zero] * eighth, first, 0, tap_subs, s * tap_quarter, x_subs, s * quarter,
                0, first + eighth, tap_quarter,
            )
            for k, value in enumerate(sums):
                n = first + k
                if n < eighth - 1:
                    sums_low[at(s * eighth + n + 1), :] = value
                else:
                    sums_high[at(s * (eighth + 1) + n + 1 - eighth), :] = value
        return 0

    lax.fori_loop(0, SUBS, sub, 0)
    for copy in copies[1:]:
        copy.wait()


def own_weights(weight_hbm, weight_ref, offset, channels, sem):
    owner = jnp.bitwise_xor(lax.axis_index("tp"), offset)
    return pltpu.make_async_copy(
        weight_hbm.at[:, pl.ds(pl.multiple_of(owner * channels, channels), channels), :],
        weight_ref.at[:, pl.ds(offset * channels, channels), :],
        sem,
    )


def own_part(mixed, taps, gate, weight, tp):
    rows, span = mixed.shape[0], taps.shape[0]
    quarter = rows // PHASES
    eighth = quarter // 2
    return pl.pallas_call(
        own_kernel,
        out_shape=(
            slabs(SUBS * eighth),
            slabs(SUBS * (eighth + 1)),
            slabs(SUBS * span // PHASES),
            jax.ShapeDtypeStruct(gate.shape, BF16),
            jax.ShapeDtypeStruct(weight.shape, BF16),
        ),
        in_specs=[VMEM, HBM, HBM, HBM],
        out_specs=(VMEM,) * 5,
        scratch_shapes=[
            pltpu.VMEM(taps.shape, F32),
            slab_scratch(max(rows, span)),
            slab_scratch(SUBS * quarter),
            pltpu.SemaphoreType.DMA((2 + tp,)),
        ],
        compiler_params=params(24),
        cost_estimate=cost(),
        name="fir_own_rows",
    )(mixed, *(pltpu.with_memory_space_constraint(v, pltpu.HBM) for v in (taps, gate, weight)))


def high_kernel(
    rim_ref, sums_ref, tap_subs, gate_ref, gain_ref, sent_ref, x_subs, last_ref, slab_ref, z_ref
):
    rows = sent_ref.shape[0]
    eighth = rows // PHASES
    tap_quarter = tap_subs.shape[0] // SLAB // SUBS
    to_slabs(rim_ref.at[pl.ds(rows, rows)], slab_ref)
    to_subs(slab_ref, eighth, x_subs)

    def sub(s, _):
        at_z = s * (eighth + 1)
        sums = [sums_ref[at(at_z + k), :] for k in range(eighth + 1)]
        sums = accumulate(
            sums, eighth - 1, 2 * eighth, tap_subs, s * tap_quarter, x_subs, s * eighth,
            eighth, eighth, tap_quarter,
        )
        for k, value in enumerate(sums):
            z_ref[at(at_z + k), :] = value
        last_ref[at(s), :] = sums[0]
        return 0

    lax.fori_loop(0, SUBS, sub, 0)
    finish(z_ref, eighth, slab_ref)
    emit(slab_ref, gate_ref, rows, gain_ref, sent_ref)


def high_part(rim, sums, taps, gate, gain):
    rows = rim.shape[0] // 2
    eighth = rows // PHASES
    return pl.pallas_call(
        high_kernel,
        out_shape=(
            jax.ShapeDtypeStruct((rows, (SLAB + 1) * LANES), BF16),
            slabs(SUBS * eighth),
            slabs(SUBS),
        ),
        in_specs=[VMEM] * 5,
        out_specs=(VMEM,) * 3,
        scratch_shapes=[slab_scratch(rows), slab_scratch(SUBS * (eighth + 1))],
        compiler_params=params(16),
        cost_estimate=cost(),
        name="fir_later_rows",
    )(rim, sums, taps, gate, gain)


def low_kernel(
    rim_ref,
    sums_ref,
    x_high,
    last_ref,
    tap_subs,
    gate_ref,
    gain_ref,
    sent_ref,
    slab_ref,
    x_subs,
    z_ref,
):
    rows = sent_ref.shape[0]
    eighth = rows // PHASES
    tap_quarter = tap_subs.shape[0] // SLAB // SUBS
    to_slabs(rim_ref.at[pl.ds(0, rows)], slab_ref)
    to_subs(slab_ref, eighth, x_subs)

    def sub(s, _):
        sums = [sums_ref[at(s * eighth + k), :] for k in range(eighth)]
        for x_ref, first in ((x_high, eighth), (x_subs, 0)):
            sums = accumulate(
                sums, -1, 2 * eighth, tap_subs, s * tap_quarter, x_ref, s * eighth,
                first, eighth, tap_quarter,
            )
        for k, value in enumerate(sums + [last_ref[at(s), :]]):
            z_ref[at(s * (eighth + 1) + k), :] = value
        return 0

    lax.fori_loop(0, SUBS, sub, 0)
    finish(z_ref, eighth, slab_ref)
    emit(slab_ref, gate_ref, 0, gain_ref, sent_ref)


def low_part(rim, sums, x_high, last, taps, gate, gain):
    rows = rim.shape[0] // 2
    eighth = rows // PHASES
    return pl.pallas_call(
        low_kernel,
        out_shape=jax.ShapeDtypeStruct((rows, (SLAB + 1) * LANES), BF16),
        in_specs=[VMEM] * 7,
        out_specs=VMEM,
        scratch_shapes=[
            slab_scratch(rows),
            slab_scratch(SUBS * eighth),
            slab_scratch(SUBS * (eighth + 1)),
        ],
        compiler_params=params(16),
        cost_estimate=cost(),
        name="fir_earlier_rows",
    )(rim, sums, x_high, last, taps, gate, gain)


def project(blocks, first, weight_ref, acc_ref, ssq_ref):
    width = weight_ref.shape[2]
    whole = [jnp.concatenate([low[...], high[...]], axis=0) for low, high in blocks]
    channels = whole[0].shape[1] - LANES
    for block in whole:
        ssq_ref[...] += block[:, channels:].astype(F32)
    for which in range(3):
        lanes = slice(which * width, (which + 1) * width)
        total = acc_ref[:, lanes]
        for place, block in enumerate(whole, first):
            total = total + jnp.dot(
                block[:, :channels],
                weight_ref[which, place * channels : (place + 1) * channels, :],
                preferred_element_type=F32,
            )
        acc_ref[:, lanes] = total


def first_kernel(*refs):
    blocks = ((refs[0], refs[1]), (refs[2], refs[3]))
    weight_ref, acc_ref, ssq_ref = refs[4:]
    acc_ref[...] = jnp.zeros_like(acc_ref)
    ssq_ref[...] = jnp.zeros_like(ssq_ref)
    project(blocks, 0, weight_ref, acc_ref, ssq_ref)


def first_projection(mine, weight):
    rows = 2 * mine[0][0].shape[0]
    return pl.pallas_call(
        first_kernel,
        out_shape=(
            jax.ShapeDtypeStruct((rows, 3 * weight.shape[2]), F32),
            jax.ShapeDtypeStruct((rows, LANES), F32),
        ),
        in_specs=[VMEM] * 5,
        out_specs=(VMEM,) * 2,
        compiler_params=params(24),
        cost_estimate=cost(),
        name="projections_near",
    )(*mine[0], *mine[1], weight)


def last_kernel(count, model, spread, *refs):
    blocks = [(refs[2 * n], refs[2 * n + 1]) for n in range(count)]
    weight_ref, acc_in, ssq_in = refs[2 * count : 2 * count + 3]
    outs, (acc_ref, ssq_ref) = refs[2 * count + 3 : -2], refs[-2:]
    acc_ref[...] = acc_in[...]
    ssq_ref[...] = ssq_in[...]
    project(blocks, 2, weight_ref, acc_ref, ssq_ref)
    msq = jnp.sum(ssq_ref[...], axis=1, keepdims=True) / model
    scale = lax.rsqrt(msq + EPS)
    rows = acc_ref.shape[0]
    width = weight_ref.shape[2]
    heads = width // HEAD_DIM
    place = lax.axis_index("ctx") // 2 if spread else 0
    for n, out in enumerate(outs):
        head = jnp.bitwise_xor(place, heads - 1 - n)
        for which in range(3):
            lanes = pl.ds(pl.multiple_of(which * width + head * HEAD_DIM, LANES), HEAD_DIM)
            out[which * rows : (which + 1) * rows, :] = (acc_ref[:, lanes] * scale).astype(BF16)


def last_projection(others, weight, acc, ssq, model, spread):
    rows = acc.shape[0]
    heads = weight.shape[2] // HEAD_DIM
    return pl.pallas_call(
        functools.partial(last_kernel, len(others), model, spread),
        out_shape=tuple(
            jax.ShapeDtypeStruct((3 * rows, HEAD_DIM), BF16) for _ in range(heads)
        ),
        in_specs=[VMEM] * (2 * len(others) + 3),
        out_specs=(VMEM,) * heads,
        scratch_shapes=[pltpu.VMEM(acc.shape, F32), pltpu.VMEM(ssq.shape, F32)],
        compiler_params=params(24),
        cost_estimate=cost(),
        name="projections_far",
    )(*[half for pair in others for half in pair], weight, acc, ssq)


def pack_kernel(*refs):
    blocks, out = refs[:-1], refs[-1]
    rows = blocks[0].shape[0] // 3
    half = len(blocks) * rows
    for k, block in enumerate(blocks):
        out[k * rows : (k + 1) * rows, :] = block[rows : 2 * rows, :]
        out[half + k * rows : half + (k + 1) * rows, :] = block[2 * rows :, :]


def packed(blocks):
    rows = blocks[0].shape[0] // 3
    return pl.pallas_call(
        pack_kernel,
        out_shape=jax.ShapeDtypeStruct((2 * len(blocks) * rows, HEAD_DIM), BF16),
        in_specs=[VMEM] * len(blocks),
        out_specs=VMEM,
        compiler_params=params(4),
        cost_estimate=cost(),
        name="pack_keys",
    )(*blocks)


def attend_kernel(count, *refs):
    blocks, sides, outs = refs[:count], refs[count : count + 2], refs[count + 2 :]
    rows = outs[0].shape[0]
    half = count * rows
    z, c = lax.axis_index("ctx") // 2, lax.axis_index("tp") % 2
    column = lax.broadcasted_iota(jnp.int32, (1, half), 1)
    even = 2 * jnp.bitwise_xor(column // rows, z) * rows + column % rows
    scale = 1.0 / math.sqrt(HEAD_DIM)
    for n, block in enumerate(blocks):
        k = count - 1 - n
        start = (2 * jnp.bitwise_xor(z, k) + c) * rows
        query_pos = start + lax.broadcasted_iota(jnp.int32, (rows, 1), 0)
        scores = []
        for side, core in zip(sides, (c, 1 - c)):
            product = lax.dot_general(
                block[:rows, :],
                side[:half, :],
                (((1,), (1,)), ((), ())),
                preferred_element_type=F32,
            )
            allowed = query_pos >= even + core * rows
            scores.append(jnp.where(allowed, product * scale, -1e30))
        top = jnp.maximum(*(jnp.max(part, axis=1, keepdims=True) for part in scores))
        expo = [jnp.exp(part - top) for part in scores]
        total = sum(jnp.sum(part, axis=1, keepdims=True) for part in expo)
        summed = sum(
            jnp.dot(part.astype(BF16), side[half:, :], preferred_element_type=F32)
            for part, side in zip(expo, sides)
        )
        outs[n][...] = (summed / total).astype(BF16)


def attend(blocks, mine, theirs):
    count = len(blocks)
    rows = blocks[0].shape[0] // 3
    return pl.pallas_call(
        functools.partial(attend_kernel, count),
        out_shape=tuple(jax.ShapeDtypeStruct((rows, HEAD_DIM), BF16) for _ in range(count)),
        in_specs=[VMEM] * (count + 2),
        out_specs=(VMEM,) * count,
        compiler_params=params(24),
        cost_estimate=cost(),
        name="attention",
    )(*blocks, mine, theirs)


def join_kernel(*refs):
    blocks, out = refs[:-1], refs[-1]
    for n, block in enumerate(blocks):
        head = jnp.bitwise_xor(lax.axis_index("ctx") // 2, len(blocks) - 1 - n)
        out[:, pl.ds(pl.multiple_of(head * HEAD_DIM, LANES), HEAD_DIM)] = block[...]


def join(blocks):
    rows = blocks[0].shape[0]
    return pl.pallas_call(
        join_kernel,
        out_shape=jax.ShapeDtypeStruct((rows, len(blocks) * HEAD_DIM), BF16),
        in_specs=[VMEM] * len(blocks),
        out_specs=VMEM,
        compiler_params=params(4),
        cost_estimate=cost(),
        name="join_heads",
    )(*blocks)


def gathered_attention(message, heads, rows):
    parts = jnp.stack([m.reshape(3, rows, HEAD_DIM) for m in message], axis=2)
    query, keys, values = parts[0], parts[1], parts[2]
    keys = lax.all_gather(keys, "ctx", axis=0, tiled=True)
    values = lax.all_gather(values, "ctx", axis=0, tiled=True)
    query_pos = lax.axis_index("ctx") * rows + jnp.arange(rows, dtype=jnp.int32)
    key_pos = jnp.arange(keys.shape[0], dtype=jnp.int32)
    scores = jnp.einsum("qhd,khd->hqk", query, keys, preferred_element_type=F32)
    allowed = (query_pos[:, None] >= key_pos[None, :])[None]
    scores = jnp.where(allowed, scores / math.sqrt(HEAD_DIM), -1e30)
    expo = jnp.where(allowed, jnp.exp(scores - jnp.max(scores, axis=2, keepdims=True)), 0.0)
    total = jnp.sum(expo, axis=2)
    summed = jnp.einsum("hqk,khd->qhd", expo.astype(BF16), values, preferred_element_type=F32)
    return (summed / total.T[:, :, None]).astype(BF16).reshape(rows, heads * HEAD_DIM)


def body(gate_in, conv_in, value_in, filter_taps, norm_gain, qkv_weight):
    rows, channels = gate_in.shape
    ctx, tp = lax.axis_size("ctx"), lax.axis_size("tp")
    weight = jnp.transpose(qkv_weight, (1, 0, 2))
    heads = weight.shape[2] // HEAD_DIM
    model = weight.shape[1]
    chip_per_head = heads * 2 == ctx and heads & (heads - 1) == 0

    wide = SLAB * LANES

    def widened(value):
        return jnp.pad(value, ((0, 0), (0, wide - channels))) if channels < wide else value

    def narrowed(sent):
        if channels == wide:
            return sent
        return jnp.concatenate([sent[:, :channels], sent[:, wide:]], axis=1)

    def swapped(value, by):
        return lax.ppermute(value, "tp", [(i, i ^ by) for i in range(tp)])

    mixed = (conv_in.astype(F32) * value_in.astype(F32)).astype(BF16)
    rim = widened(lax.ppermute(mixed, "ctx", [(i, i + 1) for i in range(ctx - 1)]))
    gain = widened(norm_gain[None])
    sums_low, sums_high, taps, gate, weight = own_part(
        widened(mixed), widened(filter_taps), widened(gate_in), weight, tp
    )
    sent_high, x_high, last = high_part(rim, sums_high, taps, gate, gain)
    sent_high = narrowed(sent_high)
    near_high = swapped(sent_high, 1)
    rim, near_high = lax.optimization_barrier((rim, near_high))
    sent_low = narrowed(low_part(rim, sums_low, x_high, last, taps, gate, gain))
    sent = (sent_low, sent_high)

    far = []
    by = tp // 2
    while by > 1:
        far = far + [
            (o ^ by, tuple(swapped(part, by) for part in pair)) for o, pair in [(0, sent)] + far
        ]
        by //= 2
    mine = (sent, (swapped(sent_low, 1), near_high))
    acc, ssq = first_projection(mine, weight)
    places, pairs = [o for o, _ in far], [pair for _, pair in far]
    last_low, acc = lax.optimization_barrier((pairs[-1][0], acc))
    pairs[-1] = (last_low, pairs[-1][1])
    others = []
    for o, pair in sorted(zip(places, pairs), key=lambda item: item[0]):
        others += [pair, tuple(swapped(part, 1) for part in pair)]
    messages = last_projection(others, weight, acc, ssq, model, chip_per_head)
    if not chip_per_head:
        return gathered_attention(messages[::-1], heads, rows)

    def routed(value, k):
        pairs = []
        for z in range(ctx // 2):
            for y in range(2):
                for x in range(tp // 2):
                    for c in range(2):
                        source = (2 * z + y) * tp + 2 * x + c
                        pairs.append((source, (2 * (z ^ k) + c) * tp + 2 * x + y))
        return lax.ppermute(value, ("ctx", "tp"), pairs)

    order = range(heads - 1, -1, -1)
    held = [routed(value, k) for value, k in zip(messages, order)]
    mine = packed(held[::-1])
    done = attend(held, mine, swapped(mine, 1))
    return join([routed(value, k) for value, k in zip(done, order)])


def solution(mesh):
    placed = (
        P("ctx", "tp"),
        P("ctx", "tp"),
        P("ctx", "tp"),
        P(None, "tp"),
        P("tp"),
        P(None, None, "tp"),
    )
    return jax.shard_map(
        body, mesh=mesh, in_specs=placed, out_specs=P("ctx", "tp"), check_vma=False
    )
```

```python
import functools
import math

import jax
import jax.numpy as jnp
from jax import lax
from jax.experimental import pallas as pl
from jax.experimental.pallas import tpu as pltpu
from jax.sharding import PartitionSpec as P

HEAD_DIM = 128
LANES = 128
SLAB = 8
PHASES = 4
SUBS = 9
HELD = 8
EPS = 1e-06
BF16 = jnp.bfloat16
F32 = jnp.float32
VMEM = pl.BlockSpec(memory_space=pltpu.VMEM)
HBM = pl.BlockSpec(memory_space=pltpu.HBM)


def params(mib):
    return pltpu.CompilerParams(vmem_limit_bytes=mib << 20)


def cost():
    return pl.CostEstimate(flops=0, bytes_accessed=1024, transcendentals=0)


def slabs(count):
    return jax.ShapeDtypeStruct((count * SLAB, LANES), F32)


def slab_scratch(count):
    return pltpu.VMEM((count * SLAB, LANES), F32)


def at(index):
    if not isinstance(index, int):
        return pl.ds(pl.multiple_of(index * SLAB, SLAB), SLAB)
    return pl.ds(index * SLAB, SLAB)


def to_slabs(source, target):
    for group in range(SLAB):
        target[pl.ds(group, source.shape[0], stride=SLAB), :] = source[
            :, group * LANES : (group + 1) * LANES
        ].astype(F32)


def to_subs(source, count, target):
    for n in range(count):
        x0, x1, x2, x3 = (source[at(PHASES * n + p), :] for p in range(PHASES))
        low, high = x0 + x1, x2 + x3
        for s, value in enumerate((x0, x2, x0 + x2, x1, x3, x1 + x3, low, high, low + high)):
            target[at(s * count + n), :] = value


def accumulate(sums, first, lag, taps, tap_at, x_ref, x_at, x_first, x_count, span):
    sums = list(sums)
    for start in range(x_first, x_first + x_count, HELD):
        places = range(start, min(start + HELD, x_first + x_count))
        used = {}
        for i in places:
            x = x_ref[at(x_at + (i - x_first)), :]
            for k in range(len(sums)):
                j = lag + first + k - i
                if 0 <= j < span:
                    if j not in used:
                        used[j] = taps[at(tap_at + j), :]
                    sums[k] = sums[k] + used[j] * x
    return sums


def finish(z_ref, count, full_ref):
    def z(s, k):
        return z_ref[at(s * (count + 1) + k), :]

    before = [z(s, 0) for s in range(SUBS)]
    for n in range(count):
        now = [z(s, n + 1) for s in range(SUBS)]

        def even(s):
            return now[s] + before[s + 1]

        def odd(s, held):
            return held[s + 2] - held[s] - held[s + 1]

        a_even, a_odd, b_even, b_odd = even(0), odd(0, now), even(3), odd(3, now)
        full_ref[at(PHASES * n), :] = a_even + odd(3, before)
        full_ref[at(PHASES * n + 1), :] = even(6) - a_even - b_even
        full_ref[at(PHASES * n + 2), :] = a_odd + b_even
        full_ref[at(PHASES * n + 3), :] = odd(6, now) - a_odd - b_odd
        before = now


def emit(full_ref, gate_ref, first, gain_ref, sent_ref):
    rows = sent_ref.shape[0]
    squares = jnp.zeros((rows, LANES), F32)
    for group in range(SLAB):
        lanes = slice(group * LANES, (group + 1) * LANES)
        hyena = (
            (
                gate_ref[first : first + rows, lanes].astype(F32)
                * full_ref[pl.ds(group, rows, stride=SLAB), :]
            )
            .astype(BF16)
            .astype(F32)
        )
        squares = squares + hyena * hyena
        sent_ref[:, lanes] = (hyena * gain_ref[:, lanes]).astype(BF16)
    total = jnp.sum(squares, axis=1, keepdims=True)
    pieces = []
    for _ in range(3):
        pieces.append(total.astype(BF16).astype(F32))
        total = total - pieces[-1]
    lane = lax.broadcasted_iota(jnp.int32, (rows, LANES), 1)
    row = jnp.zeros((rows, LANES), F32)
    for place, piece in enumerate(pieces):
        row = jnp.where(lane == place, piece, row)
    sent_ref[:, SLAB * LANES :] = row.astype(BF16)


def own_kernel(
    mixed_ref,
    taps_hbm,
    gate_hbm,
    weight_hbm,
    sums_low,
    sums_high,
    tap_subs,
    gate_ref,
    weight_ref,
    taps_ref,
    slab_ref,
    x_subs,
    sems,
):
    rows, span = mixed_ref.shape[0], taps_ref.shape[0]
    quarter, eighth = rows // PHASES, rows // PHASES // 2
    tap_quarter = span // PHASES
    blocks = lax.axis_size("tp")
    channels = weight_ref.shape[1] // blocks
    copies = [
        pltpu.make_async_copy(taps_hbm, taps_ref, sems.at[0]),
        pltpu.make_async_copy(gate_hbm, gate_ref, sems.at[1]),
    ] + [
        own_weights(weight_hbm, weight_ref, o, channels, sems.at[2 + o]) for o in range(blocks)
    ]
    for copy in copies:
        copy.start()
    to_slabs(mixed_ref, slab_ref)
    to_subs(slab_ref, quarter, x_subs)
    copies[0].wait()
    to_slabs(taps_ref, slab_ref)
    to_subs(slab_ref, tap_quarter, tap_subs)

    def sub(s, _):
        zero = jnp.zeros((SLAB, LANES), F32)
        sums_low[at(s * eighth), :] = zero
        for first in (0, eighth):
            sums = accumulate(
                [zero] * eighth, first, 0, tap_subs, s * tap_quarter, x_subs, s * quarter,
                0, first + eighth, tap_quarter,
            )
            for k, value in enumerate(sums):
                n = first + k
                if n < eighth - 1:
                    sums_low[at(s * eighth + n + 1), :] = value
                else:
                    sums_high[at(s * (eighth + 1) + n + 1 - eighth), :] = value
        return 0

    lax.fori_loop(0, SUBS, sub, 0)
    for copy in copies[1:]:
        copy.wait()


def own_weights(weight_hbm, weight_ref, offset, channels, sem):
    owner = jnp.bitwise_xor(lax.axis_index("tp"), offset)
    return pltpu.make_async_copy(
        weight_hbm.at[:, pl.ds(pl.multiple_of(owner * channels, channels), channels), :],
        weight_ref.at[:, pl.ds(offset * channels, channels), :],
        sem,
    )


def own_part(mixed, taps, gate, weight, tp):
    rows, span = mixed.shape[0], taps.shape[0]
    quarter = rows // PHASES
    eighth = quarter // 2
    return pl.pallas_call(
        own_kernel,
        out_shape=(
            slabs(SUBS * eighth),
            slabs(SUBS * (eighth + 1)),
            slabs(SUBS * span // PHASES),
            jax.ShapeDtypeStruct(gate.shape, BF16),
            jax.ShapeDtypeStruct(weight.shape, BF16),
        ),
        in_specs=[VMEM, HBM, HBM, HBM],
        out_specs=(VMEM,) * 5,
        scratch_shapes=[
            pltpu.VMEM(taps.shape, F32),
            slab_scratch(max(rows, span)),
            slab_scratch(SUBS * quarter),
            pltpu.SemaphoreType.DMA((2 + tp,)),
        ],
        compiler_params=params(24),
        cost_estimate=cost(),
        name="fir_own_rows",
    )(mixed, *(pltpu.with_memory_space_constraint(v, pltpu.HBM) for v in (taps, gate, weight)))


def high_kernel(
    rim_ref, sums_ref, tap_subs, gate_ref, gain_ref, sent_ref, x_subs, last_ref, slab_ref, z_ref
):
    rows = sent_ref.shape[0]
    eighth = rows // PHASES
    tap_quarter = tap_subs.shape[0] // SLAB // SUBS
    to_slabs(rim_ref.at[pl.ds(rows, rows)], slab_ref)
    to_subs(slab_ref, eighth, x_subs)

    def sub(s, _):
        at_z = s * (eighth + 1)
        sums = [sums_ref[at(at_z + k), :] for k in range(eighth + 1)]
        sums = accumulate(
            sums, eighth - 1, 2 * eighth, tap_subs, s * tap_quarter, x_subs, s * eighth,
            eighth, eighth, tap_quarter,
        )
        for k, value in enumerate(sums):
            z_ref[at(at_z + k), :] = value
        last_ref[at(s), :] = sums[0]
        return 0

    lax.fori_loop(0, SUBS, sub, 0)
    finish(z_ref, eighth, slab_ref)
    emit(slab_ref, gate_ref, rows, gain_ref, sent_ref)


def high_part(rim, sums, taps, gate, gain):
    rows = rim.shape[0] // 2
    eighth = rows // PHASES
    return pl.pallas_call(
        high_kernel,
        out_shape=(
            jax.ShapeDtypeStruct((rows, (SLAB + 1) * LANES), BF16),
            slabs(SUBS * eighth),
            slabs(SUBS),
        ),
        in_specs=[VMEM] * 5,
        out_specs=(VMEM,) * 3,
        scratch_shapes=[slab_scratch(rows), slab_scratch(SUBS * (eighth + 1))],
        compiler_params=params(16),
        cost_estimate=cost(),
        name="fir_later_rows",
    )(rim, sums, taps, gate, gain)


def low_kernel(
    rim_ref,
    sums_ref,
    x_high,
    last_ref,
    tap_subs,
    gate_ref,
    gain_ref,
    sent_ref,
    slab_ref,
    x_subs,
    z_ref,
):
    rows = sent_ref.shape[0]
    eighth = rows // PHASES
    tap_quarter = tap_subs.shape[0] // SLAB // SUBS
    to_slabs(rim_ref.at[pl.ds(0, rows)], slab_ref)
    to_subs(slab_ref, eighth, x_subs)

    def sub(s, _):
        sums = [sums_ref[at(s * eighth + k), :] for k in range(eighth)]
        for x_ref, first in ((x_high, eighth), (x_subs, 0)):
            sums = accumulate(
                sums, -1, 2 * eighth, tap_subs, s * tap_quarter, x_ref, s * eighth,
                first, eighth, tap_quarter,
            )
        for k, value in enumerate(sums + [last_ref[at(s), :]]):
            z_ref[at(s * (eighth + 1) + k), :] = value
        return 0

    lax.fori_loop(0, SUBS, sub, 0)
    finish(z_ref, eighth, slab_ref)
    emit(slab_ref, gate_ref, 0, gain_ref, sent_ref)


def low_part(rim, sums, x_high, last, taps, gate, gain):
    rows = rim.shape[0] // 2
    eighth = rows // PHASES
    return pl.pallas_call(
        low_kernel,
        out_shape=jax.ShapeDtypeStruct((rows, (SLAB + 1) * LANES), BF16),
        in_specs=[VMEM] * 7,
        out_specs=VMEM,
        scratch_shapes=[
            slab_scratch(rows),
            slab_scratch(SUBS * eighth),
            slab_scratch(SUBS * (eighth + 1)),
        ],
        compiler_params=params(16),
        cost_estimate=cost(),
        name="fir_earlier_rows",
    )(rim, sums, x_high, last, taps, gate, gain)


def project(blocks, places, weight_ref, acc_ref, ssq_ref):
    width = weight_ref.shape[2]
    whole = [jnp.concatenate([low[...], high[...]], axis=0) for low, high in blocks]
    channels = whole[0].shape[1] - LANES
    for block in whole:
        ssq_ref[...] += block[:, channels:].astype(F32)
    for which in range(3):
        lanes = slice(which * width, (which + 1) * width)
        total = acc_ref[:, lanes]
        for place, block in zip(places, whole):
            total = total + jnp.dot(
                block[:, :channels],
                weight_ref[which, place * channels : (place + 1) * channels, :],
                preferred_element_type=F32,
            )
        acc_ref[:, lanes] = total


def partial_kernel(places, fresh, *refs):
    count = len(places)
    blocks = [(refs[2 * n], refs[2 * n + 1]) for n in range(count)]
    weight_ref, *before, acc_ref, ssq_ref = refs[2 * count :]
    acc_ref[...] = jnp.zeros_like(acc_ref) if fresh else before[0][...]
    ssq_ref[...] = jnp.zeros_like(ssq_ref) if fresh else before[1][...]
    project(blocks, places, weight_ref, acc_ref, ssq_ref)


def part_projection(blocks, weight, before=()):
    rows = 2 * blocks[0][1][0].shape[0]
    return pl.pallas_call(
        functools.partial(partial_kernel, tuple(place for place, _ in blocks), not before),
        out_shape=(
            jax.ShapeDtypeStruct((rows, 3 * weight.shape[2]), F32),
            jax.ShapeDtypeStruct((rows, LANES), F32),
        ),
        in_specs=[VMEM] * (2 * len(blocks) + 1 + len(before)),
        out_specs=(VMEM,) * 2,
        compiler_params=params(24),
        cost_estimate=cost(),
        name="projections_part",
    )(*[half for _, pair in blocks for half in pair], weight, *before)


def last_kernel(places, model, spread, *refs):
    count = len(places)
    blocks = [(refs[2 * n], refs[2 * n + 1]) for n in range(count)]
    weight_ref, acc_in, ssq_in = refs[2 * count : 2 * count + 3]
    outs, (acc_ref, ssq_ref) = refs[2 * count + 3 : -2], refs[-2:]
    acc_ref[...] = acc_in[...]
    ssq_ref[...] = ssq_in[...]
    project(blocks, places, weight_ref, acc_ref, ssq_ref)
    msq = jnp.sum(ssq_ref[...], axis=1, keepdims=True) / model
    scale = lax.rsqrt(msq + EPS)
    rows = acc_ref.shape[0]
    width = weight_ref.shape[2]
    heads = width // HEAD_DIM
    place = lax.axis_index("ctx") // 2 if spread else 0
    for n, out in enumerate(outs):
        head = jnp.bitwise_xor(place, heads - 1 - n)
        for which in range(3):
            lanes = pl.ds(pl.multiple_of(which * width + head * HEAD_DIM, LANES), HEAD_DIM)
            out[which * rows : (which + 1) * rows, :] = (acc_ref[:, lanes] * scale).astype(BF16)


def last_projection(blocks, weight, acc, ssq, model, spread):
    rows = acc.shape[0]
    heads = weight.shape[2] // HEAD_DIM
    return pl.pallas_call(
        functools.partial(last_kernel, tuple(place for place, _ in blocks), model, spread),
        out_shape=tuple(
            jax.ShapeDtypeStruct((3 * rows, HEAD_DIM), BF16) for _ in range(heads)
        ),
        in_specs=[VMEM] * (2 * len(blocks) + 3),
        out_specs=(VMEM,) * heads,
        scratch_shapes=[pltpu.VMEM(acc.shape, F32), pltpu.VMEM(ssq.shape, F32)],
        compiler_params=params(24),
        cost_estimate=cost(),
        name="projections_last",
    )(*[half for _, pair in blocks for half in pair], weight, acc, ssq)


def scores_of(query, keys, rows, y):
    place = lax.axis_index("ctx")

    def base(shape, axis, of_y):
        index = lax.broadcasted_iota(jnp.int32, shape, axis)
        block = 2 * jnp.bitwise_xor(index // rows, place // 2) + of_y
        return block * rows + index % rows

    product = lax.dot_general(
        query, keys, (((1,), (1,)), ((), ())), preferred_element_type=F32
    ) * (1.0 / math.sqrt(HEAD_DIM))
    query_base = base((query.shape[0], 1), 0, place % 2)
    key_base = base((1, keys.shape[0]), 1, y)
    return jnp.where(query_base >= key_base, product, -1e30)


def own_y_kernel(*refs):
    blocks, outs = refs[:-6], refs[-6:]
    query_ref, top_ref, total_ref, summed_ref, key_ref, value_ref = outs
    rows = blocks[0].shape[0] // 3
    for n, block in enumerate(blocks):
        spot = slice(n * rows, (n + 1) * rows)
        query_ref[spot, :] = block[:rows, :]
        key_ref[spot, :] = block[rows : 2 * rows, :]
        value_ref[spot, :] = block[2 * rows :, :]
    scores = scores_of(query_ref[...], key_ref[...], rows, lax.axis_index("ctx") % 2)
    top = jnp.max(scores, axis=1, keepdims=True)
    expo = jnp.exp(scores - top)
    top_ref[...] = jnp.broadcast_to(top, top_ref.shape)
    total_ref[...] = jnp.broadcast_to(jnp.sum(expo, axis=1, keepdims=True), total_ref.shape)
    summed_ref[...] = jnp.dot(expo.astype(BF16), value_ref[...], preferred_element_type=F32)


def attend_own_y(blocks):
    length = len(blocks) * blocks[0].shape[0] // 3
    query = jax.ShapeDtypeStruct((length, HEAD_DIM), BF16)
    shape = jax.ShapeDtypeStruct((length, LANES), F32)
    return pl.pallas_call(
        own_y_kernel,
        out_shape=(query, shape, shape, shape),
        in_specs=[VMEM] * len(blocks),
        out_specs=(VMEM,) * 4,
        scratch_shapes=[pltpu.VMEM((length, HEAD_DIM), BF16)] * 2,
        compiler_params=params(16),
        cost_estimate=cost(),
        name="attention_own_y",
    )(*blocks)


def other_y_kernel(count, *refs):
    others, (query_ref, top_ref, total_ref, summed_ref) = refs[:count], refs[count : count + 4]
    outs, (key_ref, value_ref) = refs[count + 4 : -2], refs[-2:]
    rows = outs[0].shape[0]
    for n, other in enumerate(others):
        key_ref[n * rows : (n + 1) * rows, :] = other[:rows, :]
        value_ref[n * rows : (n + 1) * rows, :] = other[rows:, :]
    scores = scores_of(query_ref[...], key_ref[...], rows, 1 - lax.axis_index("ctx") % 2)
    before = top_ref[...]
    top = jnp.maximum(before[:, :1], jnp.max(scores, axis=1, keepdims=True))
    expo = jnp.exp(scores - top)
    fade = jnp.exp(before - top)
    total = total_ref[...] * fade + jnp.sum(expo, axis=1, keepdims=True)
    summed = summed_ref[...] * fade + jnp.dot(
        expo.astype(BF16), value_ref[...], preferred_element_type=F32
    )
    attended = (summed / total).astype(BF16)
    for n, out in enumerate(reversed(outs)):
        out[...] = attended[n * rows : (n + 1) * rows, :]


def attend_other_y(others, state):
    count = len(others)
    rows = others[0].shape[0] // 2
    return pl.pallas_call(
        functools.partial(other_y_kernel, count),
        out_shape=tuple(jax.ShapeDtypeStruct((rows, HEAD_DIM), BF16) for _ in range(count)),
        in_specs=[VMEM] * (count + 4),
        out_specs=(VMEM,) * count,
        scratch_shapes=[pltpu.VMEM((count * rows, HEAD_DIM), BF16)] * 2,
        compiler_params=params(16),
        cost_estimate=cost(),
        name="attention_other_y",
    )(*others, *state)


def join_kernel(*refs):
    blocks, out = refs[:-1], refs[-1]
    for n, block in enumerate(blocks):
        head = jnp.bitwise_xor(lax.axis_index("ctx") // 2, len(blocks) - 1 - n)
        out[:, pl.ds(pl.multiple_of(head * HEAD_DIM, LANES), HEAD_DIM)] = block[...]


def join(blocks):
    rows = blocks[0].shape[0]
    return pl.pallas_call(
        join_kernel,
        out_shape=jax.ShapeDtypeStruct((rows, len(blocks) * HEAD_DIM), BF16),
        in_specs=[VMEM] * len(blocks),
        out_specs=VMEM,
        compiler_params=params(4),
        cost_estimate=cost(),
        name="join_heads",
    )(*blocks)


def gathered_attention(message, heads, rows):
    parts = jnp.stack([m.reshape(3, rows, HEAD_DIM) for m in message], axis=2)
    query, keys, values = parts[0], parts[1], parts[2]
    keys = lax.all_gather(keys, "ctx", axis=0, tiled=True)
    values = lax.all_gather(values, "ctx", axis=0, tiled=True)
    query_pos = lax.axis_index("ctx") * rows + jnp.arange(rows, dtype=jnp.int32)
    key_pos = jnp.arange(keys.shape[0], dtype=jnp.int32)
    scores = jnp.einsum("qhd,khd->hqk", query, keys, preferred_element_type=F32)
    allowed = (query_pos[:, None] >= key_pos[None, :])[None]
    scores = jnp.where(allowed, scores / math.sqrt(HEAD_DIM), -1e30)
    expo = jnp.where(allowed, jnp.exp(scores - jnp.max(scores, axis=2, keepdims=True)), 0.0)
    total = jnp.sum(expo, axis=2)
    summed = jnp.einsum("hqk,khd->qhd", expo.astype(BF16), values, preferred_element_type=F32)
    return (summed / total.T[:, :, None]).astype(BF16).reshape(rows, heads * HEAD_DIM)


def body(gate_in, conv_in, value_in, filter_taps, norm_gain, qkv_weight):
    rows, channels = gate_in.shape
    ctx, tp = lax.axis_size("ctx"), lax.axis_size("tp")
    weight = jnp.transpose(qkv_weight, (1, 0, 2))
    heads = weight.shape[2] // HEAD_DIM
    model = weight.shape[1]
    chip_per_head = heads * 2 == ctx and heads & (heads - 1) == 0

    wide = SLAB * LANES

    def widened(value):
        return jnp.pad(value, ((0, 0), (0, wide - channels))) if channels < wide else value

    def narrowed(sent):
        if channels == wide:
            return sent
        return jnp.concatenate([sent[:, :channels], sent[:, wide:]], axis=1)

    def swapped(value, by):
        return lax.ppermute(value, "tp", [(i, i ^ by) for i in range(tp)])

    mixed = (conv_in.astype(F32) * value_in.astype(F32)).astype(BF16)
    rim = widened(lax.ppermute(mixed, "ctx", [(i, i + 1) for i in range(ctx - 1)]))
    gain = widened(norm_gain[None])
    sums_low, sums_high, taps, gate, weight = own_part(
        widened(mixed), widened(filter_taps), widened(gate_in), weight, tp
    )
    sent_high, x_high, last = high_part(rim, sums_high, taps, gate, gain)
    sent_high = narrowed(sent_high)
    near_high = swapped(sent_high, 1)
    rim, near_high = lax.optimization_barrier((rim, near_high))
    sent_low = narrowed(low_part(rim, sums_low, x_high, last, taps, gate, gain))
    sent = (sent_low, sent_high)

    far = []
    by = tp // 2
    while by > 1:
        far = far + [
            (o ^ by ^ 1, tuple(swapped(part, by ^ 1) for part in pair))
            for o, pair in [(0, sent)] + far
        ]
        by //= 2
    acc, ssq = part_projection([(0, sent), (1, (swapped(sent_low, 1), near_high))], weight)
    last_low, acc = lax.optimization_barrier((far[-1][1][0], acc))
    far[-1] = (far[-1][0], (last_low, far[-1][1][1]))
    swaps = [(o ^ 1, tuple(swapped(part, 1) for part in pair)) for o, pair in far]
    acc, ssq = part_projection(far, weight, (acc, ssq))
    messages = last_projection(swaps, weight, acc, ssq, model, chip_per_head)
    if not chip_per_head:
        return gathered_attention(messages[::-1], heads, rows)

    def over_z(value, k):
        pairs = [(i * tp + t, (i ^ (2 * k)) * tp + (t ^ 1)) for i in range(ctx) for t in range(tp)]
        return lax.ppermute(value, ("ctx", "tp"), pairs)

    def over_y(value):
        return lax.ppermute(value, "ctx", [(i, i ^ 1) for i in range(ctx)])

    order = range(heads - 1, -1, -1)
    held = [over_z(value, k) for value, k in zip(messages, order)]
    others = [over_y(value[rows:]) for value in held]
    done = attend_other_y(others[::-1], attend_own_y(held[::-1]))
    return join([over_z(value, k) for value, k in zip(done, order)])


def solution(mesh):
    placed = (
        P("ctx", "tp"),
        P("ctx", "tp"),
        P("ctx", "tp"),
        P(None, "tp"),
        P("tp"),
        P(None, None, "tp"),
    )
    return jax.shard_map(
        body, mesh=mesh, in_specs=placed, out_specs=P("ctx", "tp"), check_vma=False
    )
```

```python
import functools
import math

import jax
import jax.numpy as jnp
from jax import lax
from jax.experimental import pallas as pl
from jax.experimental.pallas import tpu as pltpu
from jax.sharding import PartitionSpec as P

HEAD_DIM = 128
LANES = 128
SLAB = 8
PHASES = 4
SUBS = 9
HELD = 8
EPS = 1e-06
BF16 = jnp.bfloat16
F32 = jnp.float32
VMEM = pl.BlockSpec(memory_space=pltpu.VMEM)
HBM = pl.BlockSpec(memory_space=pltpu.HBM)


def params(mib):
    return pltpu.CompilerParams(vmem_limit_bytes=mib << 20)


def cost():
    return pl.CostEstimate(flops=0, bytes_accessed=1024, transcendentals=0)


def slabs(count):
    return jax.ShapeDtypeStruct((count * SLAB, LANES), F32)


def slab_scratch(count):
    return pltpu.VMEM((count * SLAB, LANES), F32)


def at(index):
    if not isinstance(index, int):
        return pl.ds(pl.multiple_of(index * SLAB, SLAB), SLAB)
    return pl.ds(index * SLAB, SLAB)


def to_slabs(source, target):
    for group in range(SLAB):
        target[pl.ds(group, source.shape[0], stride=SLAB), :] = source[
            :, group * LANES : (group + 1) * LANES
        ].astype(F32)


def to_subs(source, count, target):
    for n in range(count):
        x0, x1, x2, x3 = (source[at(PHASES * n + p), :] for p in range(PHASES))
        low, high = x0 + x1, x2 + x3
        for s, value in enumerate((x0, x2, x0 + x2, x1, x3, x1 + x3, low, high, low + high)):
            target[at(s * count + n), :] = value


def accumulate(sums, first, lag, taps, tap_at, x_ref, x_at, x_first, x_count, span):
    sums = list(sums)
    for start in range(x_first, x_first + x_count, HELD):
        places = range(start, min(start + HELD, x_first + x_count))
        used = {}
        for i in places:
            x = x_ref[at(x_at + (i - x_first)), :]
            for k in range(len(sums)):
                j = lag + first + k - i
                if 0 <= j < span:
                    if j not in used:
                        used[j] = taps[at(tap_at + j), :]
                    sums[k] = sums[k] + used[j] * x
    return sums


def finish(z_ref, count, full_ref):
    def z(s, k):
        return z_ref[at(s * (count + 1) + k), :]

    before = [z(s, 0) for s in range(SUBS)]
    for n in range(count):
        now = [z(s, n + 1) for s in range(SUBS)]

        def even(s):
            return now[s] + before[s + 1]

        def odd(s, held):
            return held[s + 2] - held[s] - held[s + 1]

        a_even, a_odd, b_even, b_odd = even(0), odd(0, now), even(3), odd(3, now)
        full_ref[at(PHASES * n), :] = a_even + odd(3, before)
        full_ref[at(PHASES * n + 1), :] = even(6) - a_even - b_even
        full_ref[at(PHASES * n + 2), :] = a_odd + b_even
        full_ref[at(PHASES * n + 3), :] = odd(6, now) - a_odd - b_odd
        before = now


def emit(full_ref, gate_ref, first, gain_ref, sent_ref):
    rows = sent_ref.shape[0]
    squares = jnp.zeros((rows, LANES), F32)
    for group in range(SLAB):
        lanes = slice(group * LANES, (group + 1) * LANES)
        hyena = (
            (
                gate_ref[first : first + rows, lanes].astype(F32)
                * full_ref[pl.ds(group, rows, stride=SLAB), :]
            )
            .astype(BF16)
            .astype(F32)
        )
        squares = squares + hyena * hyena
        sent_ref[:, lanes] = (hyena * gain_ref[:, lanes]).astype(BF16)
    total = jnp.sum(squares, axis=1, keepdims=True)
    pieces = []
    for _ in range(3):
        pieces.append(total.astype(BF16).astype(F32))
        total = total - pieces[-1]
    lane = lax.broadcasted_iota(jnp.int32, (rows, LANES), 1)
    row = jnp.zeros((rows, LANES), F32)
    for place, piece in enumerate(pieces):
        row = jnp.where(lane == place, piece, row)
    sent_ref[:, SLAB * LANES :] = row.astype(BF16)


def own_kernel(
    mixed_ref,
    taps_hbm,
    gate_hbm,
    weight_hbm,
    sums_low,
    sums_high,
    tap_subs,
    gate_ref,
    weight_ref,
    taps_ref,
    slab_ref,
    x_subs,
    sems,
):
    rows, span = mixed_ref.shape[0], taps_ref.shape[0]
    quarter, eighth = rows // PHASES, rows // PHASES // 2
    tap_quarter = span // PHASES
    blocks = lax.axis_size("tp")
    channels = weight_ref.shape[1] // blocks
    copies = [
        pltpu.make_async_copy(taps_hbm, taps_ref, sems.at[0]),
        pltpu.make_async_copy(gate_hbm, gate_ref, sems.at[1]),
    ] + [
        own_weights(weight_hbm, weight_ref, o, channels, sems.at[2 + o]) for o in range(blocks)
    ]
    for copy in copies:
        copy.start()
    to_slabs(mixed_ref, slab_ref)
    to_subs(slab_ref, quarter, x_subs)
    copies[0].wait()
    to_slabs(taps_ref, slab_ref)
    to_subs(slab_ref, tap_quarter, tap_subs)

    def sub(s, _):
        zero = jnp.zeros((SLAB, LANES), F32)
        sums_low[at(s * eighth), :] = zero
        for first in (0, eighth):
            sums = accumulate(
                [zero] * eighth, first, 0, tap_subs, s * tap_quarter, x_subs, s * quarter,
                0, first + eighth, tap_quarter,
            )
            for k, value in enumerate(sums):
                n = first + k
                if n < eighth - 1:
                    sums_low[at(s * eighth + n + 1), :] = value
                else:
                    sums_high[at(s * (eighth + 1) + n + 1 - eighth), :] = value
        return 0

    lax.fori_loop(0, SUBS, sub, 0)
    for copy in copies[1:]:
        copy.wait()


def own_weights(weight_hbm, weight_ref, offset, channels, sem):
    owner = jnp.bitwise_xor(lax.axis_index("tp"), offset)
    return pltpu.make_async_copy(
        weight_hbm.at[:, pl.ds(pl.multiple_of(owner * channels, channels), channels), :],
        weight_ref.at[:, pl.ds(offset * channels, channels), :],
        sem,
    )


def own_part(mixed, taps, gate, weight, tp):
    rows, span = mixed.shape[0], taps.shape[0]
    quarter = rows // PHASES
    eighth = quarter // 2
    return pl.pallas_call(
        own_kernel,
        out_shape=(
            slabs(SUBS * eighth),
            slabs(SUBS * (eighth + 1)),
            slabs(SUBS * span // PHASES),
            jax.ShapeDtypeStruct(gate.shape, BF16),
            jax.ShapeDtypeStruct(weight.shape, BF16),
        ),
        in_specs=[VMEM, HBM, HBM, HBM],
        out_specs=(VMEM,) * 5,
        scratch_shapes=[
            pltpu.VMEM(taps.shape, F32),
            slab_scratch(max(rows, span)),
            slab_scratch(SUBS * quarter),
            pltpu.SemaphoreType.DMA((2 + tp,)),
        ],
        compiler_params=params(24),
        cost_estimate=cost(),
        name="fir_own_rows",
    )(mixed, *(pltpu.with_memory_space_constraint(v, pltpu.HBM) for v in (taps, gate, weight)))


def high_kernel(
    rim_ref, sums_ref, tap_subs, gate_ref, gain_ref, sent_ref, x_subs, last_ref, slab_ref, z_ref
):
    rows = sent_ref.shape[0]
    eighth = rows // PHASES
    tap_quarter = tap_subs.shape[0] // SLAB // SUBS
    to_slabs(rim_ref.at[pl.ds(rows, rows)], slab_ref)
    to_subs(slab_ref, eighth, x_subs)

    def sub(s, _):
        at_z = s * (eighth + 1)
        sums = [sums_ref[at(at_z + k), :] for k in range(eighth + 1)]
        sums = accumulate(
            sums, eighth - 1, 2 * eighth, tap_subs, s * tap_quarter, x_subs, s * eighth,
            eighth, eighth, tap_quarter,
        )
        for k, value in enumerate(sums):
            z_ref[at(at_z + k), :] = value
        last_ref[at(s), :] = sums[0]
        return 0

    lax.fori_loop(0, SUBS, sub, 0)
    finish(z_ref, eighth, slab_ref)
    emit(slab_ref, gate_ref, rows, gain_ref, sent_ref)


def high_part(rim, sums, taps, gate, gain):
    rows = rim.shape[0] // 2
    eighth = rows // PHASES
    return pl.pallas_call(
        high_kernel,
        out_shape=(
            jax.ShapeDtypeStruct((rows, (SLAB + 1) * LANES), BF16),
            slabs(SUBS * eighth),
            slabs(SUBS),
        ),
        in_specs=[VMEM] * 5,
        out_specs=(VMEM,) * 3,
        scratch_shapes=[slab_scratch(rows), slab_scratch(SUBS * (eighth + 1))],
        compiler_params=params(16),
        cost_estimate=cost(),
        name="fir_later_rows",
    )(rim, sums, taps, gate, gain)


def low_kernel(
    rim_ref,
    sums_ref,
    x_high,
    last_ref,
    tap_subs,
    gate_ref,
    gain_ref,
    sent_ref,
    slab_ref,
    x_subs,
    z_ref,
):
    rows = sent_ref.shape[0]
    eighth = rows // PHASES
    tap_quarter = tap_subs.shape[0] // SLAB // SUBS
    to_slabs(rim_ref.at[pl.ds(0, rows)], slab_ref)
    to_subs(slab_ref, eighth, x_subs)

    def sub(s, _):
        sums = [sums_ref[at(s * eighth + k), :] for k in range(eighth)]
        for x_ref, first in ((x_high, eighth), (x_subs, 0)):
            sums = accumulate(
                sums, -1, 2 * eighth, tap_subs, s * tap_quarter, x_ref, s * eighth,
                first, eighth, tap_quarter,
            )
        for k, value in enumerate(sums + [last_ref[at(s), :]]):
            z_ref[at(s * (eighth + 1) + k), :] = value
        return 0

    lax.fori_loop(0, SUBS, sub, 0)
    finish(z_ref, eighth, slab_ref)
    emit(slab_ref, gate_ref, 0, gain_ref, sent_ref)


def low_part(rim, sums, x_high, last, taps, gate, gain):
    rows = rim.shape[0] // 2
    eighth = rows // PHASES
    return pl.pallas_call(
        low_kernel,
        out_shape=jax.ShapeDtypeStruct((rows, (SLAB + 1) * LANES), BF16),
        in_specs=[VMEM] * 7,
        out_specs=VMEM,
        scratch_shapes=[
            slab_scratch(rows),
            slab_scratch(SUBS * eighth),
            slab_scratch(SUBS * (eighth + 1)),
        ],
        compiler_params=params(16),
        cost_estimate=cost(),
        name="fir_earlier_rows",
    )(rim, sums, x_high, last, taps, gate, gain)


def project(blocks, places, weight_ref, acc_ref, ssq_ref):
    width = weight_ref.shape[2]
    whole = [jnp.concatenate([low[...], high[...]], axis=0) for low, high in blocks]
    channels = whole[0].shape[1] - LANES
    for block in whole:
        ssq_ref[...] += block[:, channels:].astype(F32)
    for which in range(3):
        lanes = slice(which * width, (which + 1) * width)
        total = acc_ref[:, lanes]
        for place, block in zip(places, whole):
            total = total + jnp.dot(
                block[:, :channels],
                weight_ref[which, place * channels : (place + 1) * channels, :],
                preferred_element_type=F32,
            )
        acc_ref[:, lanes] = total


def partial_kernel(places, fresh, *refs):
    count = len(places)
    blocks = [(refs[2 * n], refs[2 * n + 1]) for n in range(count)]
    weight_ref, *before, acc_ref, ssq_ref = refs[2 * count :]
    acc_ref[...] = jnp.zeros_like(acc_ref) if fresh else before[0][...]
    ssq_ref[...] = jnp.zeros_like(ssq_ref) if fresh else before[1][...]
    project(blocks, places, weight_ref, acc_ref, ssq_ref)


def part_projection(blocks, weight, before=()):
    rows = 2 * blocks[0][1][0].shape[0]
    return pl.pallas_call(
        functools.partial(partial_kernel, tuple(place for place, _ in blocks), not before),
        out_shape=(
            jax.ShapeDtypeStruct((rows, 3 * weight.shape[2]), F32),
            jax.ShapeDtypeStruct((rows, LANES), F32),
        ),
        in_specs=[VMEM] * (2 * len(blocks) + 1 + len(before)),
        out_specs=(VMEM,) * 2,
        compiler_params=params(24),
        cost_estimate=cost(),
        name="projections_part",
    )(*[half for _, pair in blocks for half in pair], weight, *before)


def last_kernel(places, model, spread, *refs):
    count = len(places)
    blocks = [(refs[2 * n], refs[2 * n + 1]) for n in range(count)]
    weight_ref, acc_in, ssq_in = refs[2 * count : 2 * count + 3]
    outs, (acc_ref, ssq_ref) = refs[2 * count + 3 : -2], refs[-2:]
    acc_ref[...] = acc_in[...]
    ssq_ref[...] = ssq_in[...]
    project(blocks, places, weight_ref, acc_ref, ssq_ref)
    msq = jnp.sum(ssq_ref[...], axis=1, keepdims=True) / model
    scale = lax.rsqrt(msq + EPS)
    rows = acc_ref.shape[0]
    width = weight_ref.shape[2]
    heads = width // HEAD_DIM
    place = lax.axis_index("ctx") // 2 if spread else 0
    for n, out in enumerate(outs):
        head = jnp.bitwise_xor(place, heads - 1 - n)
        for which in range(3):
            lanes = pl.ds(pl.multiple_of(which * width + head * HEAD_DIM, LANES), HEAD_DIM)
            out[which * rows : (which + 1) * rows, :] = (acc_ref[:, lanes] * scale).astype(BF16)


def last_projection(blocks, weight, acc, ssq, model, spread):
    rows = acc.shape[0]
    heads = weight.shape[2] // HEAD_DIM
    return pl.pallas_call(
        functools.partial(last_kernel, tuple(place for place, _ in blocks), model, spread),
        out_shape=tuple(
            jax.ShapeDtypeStruct((3 * rows, HEAD_DIM), BF16) for _ in range(heads)
        ),
        in_specs=[VMEM] * (2 * len(blocks) + 3),
        out_specs=(VMEM,) * heads,
        scratch_shapes=[pltpu.VMEM(acc.shape, F32), pltpu.VMEM(ssq.shape, F32)],
        compiler_params=params(24),
        cost_estimate=cost(),
        name="projections_last",
    )(*[half for _, pair in blocks for half in pair], weight, acc, ssq)


def base_of(shape, axis, rows, y):
    index = lax.broadcasted_iota(jnp.int32, shape, axis)
    block = 2 * jnp.bitwise_xor(index // rows, lax.axis_index("ctx") // 2) + y
    return block * rows + index % rows


def scores_of(query, keys, rows, key_base):
    product = lax.dot_general(
        query, keys, (((1,), (1,)), ((), ())), preferred_element_type=F32
    ) * (1.0 / math.sqrt(HEAD_DIM))
    query_base = base_of((query.shape[0], 1), 0, rows, lax.axis_index("ctx") % 2)
    return jnp.where(query_base >= key_base, product, -1e30)


def most_kernel(count, *refs):
    blocks, others = refs[:count], refs[count : 2 * count - 1]
    query_ref, top_ref, total_ref, summed_ref, key_ref, value_ref = refs[2 * count - 1 :]
    rows = blocks[0].shape[0] // 3
    for n, block in enumerate(blocks):
        spot = slice(n * rows, (n + 1) * rows)
        query_ref[spot, :] = block[:rows, :]
        key_ref[spot, :] = block[rows : 2 * rows, :]
        value_ref[spot, :] = block[2 * rows :, :]
    for n, other in enumerate(others, count):
        key_ref[n * rows : (n + 1) * rows, :] = other[:rows, :]
        value_ref[n * rows : (n + 1) * rows, :] = other[rows:, :]
    y = lax.axis_index("ctx") % 2
    key_base = jnp.concatenate(
        [
            base_of((1, count * rows), 1, rows, y),
            base_of((1, (count - 1) * rows), 1, rows, 1 - y),
        ],
        axis=1,
    )
    scores = scores_of(query_ref[...], key_ref[...], rows, key_base)
    top = jnp.max(scores, axis=1, keepdims=True)
    expo = jnp.exp(scores - top)
    top_ref[...] = jnp.broadcast_to(top, top_ref.shape)
    total_ref[...] = jnp.broadcast_to(jnp.sum(expo, axis=1, keepdims=True), total_ref.shape)
    summed_ref[...] = jnp.dot(expo.astype(BF16), value_ref[...], preferred_element_type=F32)


def attend_most(blocks, others):
    count = len(blocks)
    rows = blocks[0].shape[0] // 3
    keys = pltpu.VMEM(((2 * count - 1) * rows, HEAD_DIM), BF16)
    shape = jax.ShapeDtypeStruct((count * rows, LANES), F32)
    return pl.pallas_call(
        functools.partial(most_kernel, count),
        out_shape=(jax.ShapeDtypeStruct((count * rows, HEAD_DIM), BF16), shape, shape, shape),
        in_specs=[VMEM] * (2 * count - 1),
        out_specs=(VMEM,) * 4,
        scratch_shapes=[keys, keys],
        compiler_params=params(16),
        cost_estimate=cost(),
        name="attention_most",
    )(*blocks, *others)


def rest_kernel(other_ref, query_ref, top_ref, total_ref, summed_ref, *outs):
    count = len(outs)
    rows = outs[0].shape[0]
    y = lax.axis_index("ctx") % 2
    key_base = base_of((1, count * rows), 1, rows, 1 - y)[:, (count - 1) * rows :]
    scores = scores_of(query_ref[...], other_ref[:rows, :], rows, key_base)
    before = top_ref[...]
    top = jnp.maximum(before[:, :1], jnp.max(scores, axis=1, keepdims=True))
    expo = jnp.exp(scores - top)
    fade = jnp.exp(before - top)
    total = total_ref[...] * fade + jnp.sum(expo, axis=1, keepdims=True)
    summed = summed_ref[...] * fade + jnp.dot(
        expo.astype(BF16), other_ref[rows:, :], preferred_element_type=F32
    )
    attended = (summed / total).astype(BF16)
    for n, out in enumerate(reversed(outs)):
        out[...] = attended[n * rows : (n + 1) * rows, :]


def attend_rest(other, state, count):
    rows = other.shape[0] // 2
    return pl.pallas_call(
        rest_kernel,
        out_shape=tuple(jax.ShapeDtypeStruct((rows, HEAD_DIM), BF16) for _ in range(count)),
        in_specs=[VMEM] * 5,
        out_specs=(VMEM,) * count,
        compiler_params=params(16),
        cost_estimate=cost(),
        name="attention_rest",
    )(other, *state)


def join_kernel(*refs):
    blocks, out = refs[:-1], refs[-1]
    for n, block in enumerate(blocks):
        head = jnp.bitwise_xor(lax.axis_index("ctx") // 2, len(blocks) - 1 - n)
        out[:, pl.ds(pl.multiple_of(head * HEAD_DIM, LANES), HEAD_DIM)] = block[...]


def join(blocks):
    rows = blocks[0].shape[0]
    return pl.pallas_call(
        join_kernel,
        out_shape=jax.ShapeDtypeStruct((rows, len(blocks) * HEAD_DIM), BF16),
        in_specs=[VMEM] * len(blocks),
        out_specs=VMEM,
        compiler_params=params(4),
        cost_estimate=cost(),
        name="join_heads",
    )(*blocks)


def gathered_attention(message, heads, rows):
    parts = jnp.stack([m.reshape(3, rows, HEAD_DIM) for m in message], axis=2)
    query, keys, values = parts[0], parts[1], parts[2]
    keys = lax.all_gather(keys, "ctx", axis=0, tiled=True)
    values = lax.all_gather(values, "ctx", axis=0, tiled=True)
    query_pos = lax.axis_index("ctx") * rows + jnp.arange(rows, dtype=jnp.int32)
    key_pos = jnp.arange(keys.shape[0], dtype=jnp.int32)
    scores = jnp.einsum("qhd,khd->hqk", query, keys, preferred_element_type=F32)
    allowed = (query_pos[:, None] >= key_pos[None, :])[None]
    scores = jnp.where(allowed, scores / math.sqrt(HEAD_DIM), -1e30)
    expo = jnp.where(allowed, jnp.exp(scores - jnp.max(scores, axis=2, keepdims=True)), 0.0)
    total = jnp.sum(expo, axis=2)
    summed = jnp.einsum("hqk,khd->qhd", expo.astype(BF16), values, preferred_element_type=F32)
    return (summed / total.T[:, :, None]).astype(BF16).reshape(rows, heads * HEAD_DIM)


def body(gate_in, conv_in, value_in, filter_taps, norm_gain, qkv_weight):
    rows, channels = gate_in.shape
    ctx, tp = lax.axis_size("ctx"), lax.axis_size("tp")
    weight = jnp.transpose(qkv_weight, (1, 0, 2))
    heads = weight.shape[2] // HEAD_DIM
    model = weight.shape[1]
    chip_per_head = heads * 2 == ctx and heads & (heads - 1) == 0

    wide = SLAB * LANES

    def widened(value):
        return jnp.pad(value, ((0, 0), (0, wide - channels))) if channels < wide else value

    def narrowed(sent):
        if channels == wide:
            return sent
        return jnp.concatenate([sent[:, :channels], sent[:, wide:]], axis=1)

    def swapped(value, by):
        return lax.ppermute(value, "tp", [(i, i ^ by) for i in range(tp)])

    mixed = (conv_in.astype(F32) * value_in.astype(F32)).astype(BF16)
    rim = widened(lax.ppermute(mixed, "ctx", [(i, i + 1) for i in range(ctx - 1)]))
    gain = widened(norm_gain[None])
    sums_low, sums_high, taps, gate, weight = own_part(
        widened(mixed), widened(filter_taps), widened(gate_in), weight, tp
    )
    sent_high, x_high, last = high_part(rim, sums_high, taps, gate, gain)
    sent_high = narrowed(sent_high)
    near_high = swapped(sent_high, 1)
    rim, near_high = lax.optimization_barrier((rim, near_high))
    sent_low = narrowed(low_part(rim, sums_low, x_high, last, taps, gate, gain))
    sent = (sent_low, sent_high)

    far = []
    by = tp // 2
    while by > 1:
        far = far + [
            (o ^ by ^ 1, tuple(swapped(part, by ^ 1) for part in pair))
            for o, pair in [(0, sent)] + far
        ]
        by //= 2
    acc, ssq = part_projection([(0, sent), (1, (swapped(sent_low, 1), near_high))], weight)
    last_low, acc = lax.optimization_barrier((far[-1][1][0], acc))
    far[-1] = (far[-1][0], (last_low, far[-1][1][1]))
    swaps = [(o ^ 1, tuple(swapped(part, 1) for part in pair)) for o, pair in far]
    acc, ssq = part_projection(far, weight, (acc, ssq))
    messages = last_projection(swaps, weight, acc, ssq, model, chip_per_head)
    if not chip_per_head:
        return gathered_attention(messages[::-1], heads, rows)

    def over_z(value, k):
        pairs = [(i * tp + t, (i ^ (2 * k)) * tp + (t ^ 1)) for i in range(ctx) for t in range(tp)]
        return lax.ppermute(value, ("ctx", "tp"), pairs)

    def over_y(value):
        return lax.ppermute(value, "ctx", [(i, i ^ 1) for i in range(ctx)])

    order = range(heads - 1, -1, -1)
    held = [over_z(value, k) for value, k in zip(messages, order)]
    others = [over_y(value[rows:]) for value in held]
    held, others = held[::-1], others[::-1]
    done = attend_rest(others[-1], attend_most(held, others[:-1]), heads)
    return join([over_z(value, k) for value, k in zip(done, order)])


def solution(mesh):
    placed = (
        P("ctx", "tp"),
        P("ctx", "tp"),
        P("ctx", "tp"),
        P(None, "tp"),
        P("tp"),
        P(None, None, "tp"),
    )
    return jax.shard_map(
        body, mesh=mesh, in_specs=placed, out_specs=P("ctx", "tp"), check_vma=False
    )
```

```python
import functools
import math

import jax
import jax.numpy as jnp
from jax import lax
from jax.experimental import pallas as pl
from jax.experimental.pallas import tpu as pltpu
from jax.sharding import PartitionSpec as P

HEAD_DIM = 128
LANES = 128
SLAB = 8
PHASES = 4
SUBS = 9
HELD = 8
PAD = 16
EPS = 1e-06
BF16 = jnp.bfloat16
F32 = jnp.float32
VMEM = pl.BlockSpec(memory_space=pltpu.VMEM)
HBM = pl.BlockSpec(memory_space=pltpu.HBM)


def params(mib):
    return pltpu.CompilerParams(vmem_limit_bytes=mib << 20)


def cost():
    return pl.CostEstimate(flops=0, bytes_accessed=1024, transcendentals=0)


def slabs(count):
    return jax.ShapeDtypeStruct((count * SLAB, LANES), F32)


def slab_scratch(count):
    return pltpu.VMEM((count * SLAB, LANES), F32)


def at(index):
    if not isinstance(index, int):
        return pl.ds(pl.multiple_of(index * SLAB, SLAB), SLAB)
    return pl.ds(index * SLAB, SLAB)


def to_slabs(source, target):
    for group in range(SLAB):
        target[pl.ds(group, source.shape[0], stride=SLAB), :] = source[
            :, group * LANES : (group + 1) * LANES
        ].astype(F32)


def to_subs(source, count, target):
    for n in range(count):
        x0, x1, x2, x3 = (source[at(PHASES * n + p), :] for p in range(PHASES))
        low, high = x0 + x1, x2 + x3
        for s, value in enumerate((x0, x2, x0 + x2, x1, x3, x1 + x3, low, high, low + high)):
            target[at(s * count + n), :] = value


def accumulate(sums, first, lag, taps, tap_at, x_ref, x_at, x_first, x_count, span):
    sums = list(sums)
    for start in range(x_first, x_first + x_count, HELD):
        places = range(start, min(start + HELD, x_first + x_count))
        used = {}
        for i in places:
            x = x_ref[at(x_at + (i - x_first)), :]
            for k in range(len(sums)):
                j = lag + first + k - i
                if 0 <= j < span:
                    if j not in used:
                        used[j] = taps[at(tap_at + j), :]
                    sums[k] = sums[k] + used[j] * x
    return sums


def finish(z_ref, count, full_ref):
    def z(s, k):
        return z_ref[at(s * (count + 1) + k), :]

    before = [z(s, 0) for s in range(SUBS)]
    for n in range(count):
        now = [z(s, n + 1) for s in range(SUBS)]

        def even(s):
            return now[s] + before[s + 1]

        def odd(s, held):
            return held[s + 2] - held[s] - held[s + 1]

        a_even, a_odd, b_even, b_odd = even(0), odd(0, now), even(3), odd(3, now)
        full_ref[at(PHASES * n), :] = a_even + odd(3, before)
        full_ref[at(PHASES * n + 1), :] = even(6) - a_even - b_even
        full_ref[at(PHASES * n + 2), :] = a_odd + b_even
        full_ref[at(PHASES * n + 3), :] = odd(6, now) - a_odd - b_odd
        before = now


def emit(full_ref, gate_ref, first, gain_ref, sent_ref):
    rows = sent_ref.shape[0]
    squares = jnp.zeros((rows, LANES), F32)
    for group in range(SLAB):
        lanes = slice(group * LANES, (group + 1) * LANES)
        hyena = (
            (
                gate_ref[first : first + rows, lanes].astype(F32)
                * full_ref[pl.ds(group, rows, stride=SLAB), :]
            )
            .astype(BF16)
            .astype(F32)
        )
        squares = squares + hyena * hyena
        sent_ref[:, lanes] = (hyena * gain_ref[:, lanes]).astype(BF16)
    total = jnp.sum(squares, axis=1, keepdims=True)
    pieces = []
    for _ in range(3):
        pieces.append(total.astype(BF16).astype(F32))
        total = total - pieces[-1]
    lane = lax.broadcasted_iota(jnp.int32, (rows, LANES), 1)
    row = jnp.zeros((rows, LANES), F32)
    for place, piece in enumerate(pieces):
        row = jnp.where(lane == place, piece, row)
    sent_ref[:, SLAB * LANES :] = row.astype(BF16)


def mixed_kernel(
    conv_hbm,
    value_hbm,
    taps_hbm,
    gate_hbm,
    high_ref,
    low_ref,
    taps_ref,
    gate_ref,
    conv_ref,
    value_ref,
    sems,
):
    half = high_ref.shape[0]
    pairs = (
        (conv_hbm, conv_ref),
        (value_hbm, value_ref),
        (taps_hbm, taps_ref),
        (gate_hbm, gate_ref),
    )
    copies = [
        pltpu.make_async_copy(source, target, sems.at[n])
        for n, (source, target) in enumerate(pairs)
    ]
    for copy in copies:
        copy.start()
    for copy in copies[:2]:
        copy.wait()
    mixed = (conv_ref[...].astype(F32) * value_ref[...].astype(F32)).astype(BF16)
    high_ref[...] = mixed[half:, :]
    low_ref[...] = mixed[: low_ref.shape[0], :]
    for copy in copies[2:]:
        copy.wait()


def mixed_halves(conv, value, taps, gate):
    rows, channels = conv.shape
    half = rows // 2
    arrays = (conv, value, taps, gate)
    return pl.pallas_call(
        mixed_kernel,
        out_shape=(
            jax.ShapeDtypeStruct((half, channels), BF16),
            jax.ShapeDtypeStruct((half + PAD, channels), BF16),
            jax.ShapeDtypeStruct(taps.shape, F32),
            jax.ShapeDtypeStruct(gate.shape, BF16),
        ),
        in_specs=[HBM] * 4,
        out_specs=(VMEM,) * 4,
        scratch_shapes=[
            pltpu.VMEM(conv.shape, BF16),
            pltpu.VMEM(conv.shape, BF16),
            pltpu.SemaphoreType.DMA((4,)),
        ],
        compiler_params=params(8),
        cost_estimate=cost(),
        name="conv_times_value",
    )(*(pltpu.with_memory_space_constraint(v, pltpu.HBM) for v in arrays))


def own_kernel(
    low_ref,
    high_ref,
    taps_ref,
    weight_hbm,
    sums_low,
    sums_high,
    tap_subs,
    weight_ref,
    slab_ref,
    x_subs,
    sems,
):
    half, span = high_ref.shape[0], taps_ref.shape[0]
    quarter, eighth = 2 * half // PHASES, half // PHASES
    tap_quarter = span // PHASES
    copies = weight_copies(weight_hbm, weight_ref, (0,), sems)
    for copy in copies:
        copy.start()
    to_slabs(low_ref.at[pl.ds(0, half)], slab_ref.at[pl.ds(0, half * SLAB)])
    to_slabs(high_ref, slab_ref.at[pl.ds(half * SLAB, half * SLAB)])
    to_subs(slab_ref, quarter, x_subs)
    to_slabs(taps_ref, slab_ref)
    to_subs(slab_ref, tap_quarter, tap_subs)

    def sub(s, _):
        zero = jnp.zeros((SLAB, LANES), F32)
        sums_low[at(s * eighth), :] = zero
        for first in (0, eighth):
            sums = accumulate(
                [zero] * eighth, first, 0, tap_subs, s * tap_quarter, x_subs, s * quarter,
                0, first + eighth, tap_quarter,
            )
            for k, value in enumerate(sums):
                n = first + k
                if n < eighth - 1:
                    sums_low[at(s * eighth + n + 1), :] = value
                else:
                    sums_high[at(s * (eighth + 1) + n + 1 - eighth), :] = value
        return 0

    lax.fori_loop(0, SUBS, sub, 0)
    for copy in copies:
        copy.wait()


def weight_copies(weight_hbm, weight_ref, offsets, sems):
    copies = []
    channels = weight_ref.shape[1] // len(offsets)
    for n, offset in enumerate(offsets):
        owner = jnp.bitwise_xor(lax.axis_index("tp"), offset)
        copies.append(
            pltpu.make_async_copy(
                weight_hbm.at[:, pl.ds(pl.multiple_of(owner * channels, channels), channels), :],
                weight_ref.at[:, pl.ds(n * channels, channels), :],
                sems.at[n],
            )
        )
    return copies


def weight_rows(weight, count, channels):
    return jax.ShapeDtypeStruct((3, count * channels, weight.shape[2]), BF16)


def own_part(low, high, taps, weight, channels):
    rows, span = 2 * high.shape[0], taps.shape[0]
    quarter = rows // PHASES
    eighth = quarter // 2
    return pl.pallas_call(
        own_kernel,
        out_shape=(
            slabs(SUBS * eighth),
            slabs(SUBS * (eighth + 1)),
            slabs(SUBS * span // PHASES),
            weight_rows(weight, 1, channels),
        ),
        in_specs=[VMEM] * 3 + [HBM],
        out_specs=(VMEM,) * 4,
        scratch_shapes=[
            slab_scratch(max(rows, span)),
            slab_scratch(SUBS * quarter),
            pltpu.SemaphoreType.DMA((1,)),
        ],
        compiler_params=params(16),
        cost_estimate=cost(),
        name="fir_own_rows",
    )(low, high, taps, pltpu.with_memory_space_constraint(weight, pltpu.HBM))


def high_kernel(
    rim_ref, sums_ref, tap_subs, gate_ref, gain_ref, sent_ref, x_subs, last_ref, slab_ref, z_ref
):
    rows = sent_ref.shape[0]
    eighth = rows // PHASES
    tap_quarter = tap_subs.shape[0] // SLAB // SUBS
    to_slabs(rim_ref, slab_ref)
    to_subs(slab_ref, eighth, x_subs)

    def sub(s, _):
        at_z = s * (eighth + 1)
        sums = [sums_ref[at(at_z + k), :] for k in range(eighth + 1)]
        sums = accumulate(
            sums, eighth - 1, 2 * eighth, tap_subs, s * tap_quarter, x_subs, s * eighth,
            eighth, eighth, tap_quarter,
        )
        for k, value in enumerate(sums):
            z_ref[at(at_z + k), :] = value
        last_ref[at(s), :] = sums[0]
        return 0

    lax.fori_loop(0, SUBS, sub, 0)
    finish(z_ref, eighth, slab_ref)
    emit(slab_ref, gate_ref, rows, gain_ref, sent_ref)


def high_part(rim, sums, taps, gate, gain):
    rows = rim.shape[0]
    eighth = rows // PHASES
    return pl.pallas_call(
        high_kernel,
        out_shape=(
            jax.ShapeDtypeStruct((rows, (SLAB + 1) * LANES), BF16),
            slabs(SUBS * eighth),
            slabs(SUBS),
        ),
        in_specs=[VMEM] * 5,
        out_specs=(VMEM,) * 3,
        scratch_shapes=[slab_scratch(rows), slab_scratch(SUBS * (eighth + 1))],
        compiler_params=params(16),
        cost_estimate=cost(),
        name="fir_later_rows",
    )(rim, sums, taps, gate, gain)


def low_kernel(
    offsets,
    rim_ref,
    sums_ref,
    x_high,
    last_ref,
    tap_subs,
    gate_ref,
    gain_ref,
    weight_hbm,
    sent_ref,
    weight_ref,
    slab_ref,
    x_subs,
    z_ref,
    sems,
):
    copies = weight_copies(weight_hbm, weight_ref, offsets, sems)
    for copy in copies:
        copy.start()
    rows = sent_ref.shape[0]
    eighth = rows // PHASES
    tap_quarter = tap_subs.shape[0] // SLAB // SUBS
    to_slabs(rim_ref.at[pl.ds(0, rows)], slab_ref)
    to_subs(slab_ref, eighth, x_subs)

    def sub(s, _):
        sums = [sums_ref[at(s * eighth + k), :] for k in range(eighth)]
        for x_ref, first in ((x_high, eighth), (x_subs, 0)):
            sums = accumulate(
                sums, -1, 2 * eighth, tap_subs, s * tap_quarter, x_ref, s * eighth,
                first, eighth, tap_quarter,
            )
        for k, value in enumerate(sums + [last_ref[at(s), :]]):
            z_ref[at(s * (eighth + 1) + k), :] = value
        return 0

    lax.fori_loop(0, SUBS, sub, 0)
    finish(z_ref, eighth, slab_ref)
    emit(slab_ref, gate_ref, 0, gain_ref, sent_ref)
    for copy in copies:
        copy.wait()


def low_part(rim, sums, x_high, last, taps, gate, gain, weight, offsets, channels):
    rows = gate.shape[0] // 2
    eighth = rows // PHASES
    return pl.pallas_call(
        functools.partial(low_kernel, offsets),
        out_shape=(
            jax.ShapeDtypeStruct((rows, (SLAB + 1) * LANES), BF16),
            weight_rows(weight, len(offsets), channels),
        ),
        in_specs=[VMEM] * 7 + [HBM],
        out_specs=(VMEM, VMEM),
        scratch_shapes=[
            slab_scratch(rows),
            slab_scratch(SUBS * eighth),
            slab_scratch(SUBS * (eighth + 1)),
            pltpu.SemaphoreType.DMA((len(offsets),)),
        ],
        compiler_params=params(16),
        cost_estimate=cost(),
        name="fir_earlier_rows",
    )(
        rim,
        sums,
        x_high,
        last,
        taps,
        gate,
        gain,
        pltpu.with_memory_space_constraint(weight, pltpu.HBM),
    )


def project(blocks, weight_refs, acc_ref, ssq_ref):
    width = weight_refs[0].shape[2]
    whole = [jnp.concatenate([low[...], high[...]], axis=0) for low, high in blocks]
    channels = whole[0].shape[1] - LANES
    for block in whole:
        ssq_ref[...] += block[:, channels:].astype(F32)
    for which in range(3):
        lanes = slice(which * width, (which + 1) * width)
        total = acc_ref[:, lanes]
        for ref, block in zip(weight_refs, whole):
            total = total + jnp.dot(
                block[:, :channels],
                ref[which],
                preferred_element_type=F32,
            )
        acc_ref[:, lanes] = total


def split_rows(weight_ref, count):
    channels = weight_ref.shape[1] // count
    return [weight_ref.at[:, pl.ds(n * channels, channels), :] for n in range(count)]


def near_kernel(far, last, *refs):
    blocks = [(refs[0], refs[1]), (refs[2], refs[3])]
    own_ref, beside_ref, weight_hbm, acc_ref, ssq_ref, far_ref, last_ref, far_sems, last_sems = (
        refs[4:]
    )
    copies = weight_copies(weight_hbm, far_ref, far, far_sems)
    copies += weight_copies(weight_hbm, last_ref, last, last_sems)
    for copy in copies:
        copy.start()
    acc_ref[...] = jnp.zeros_like(acc_ref)
    ssq_ref[...] = jnp.zeros_like(ssq_ref)
    project(blocks, [own_ref, beside_ref], acc_ref, ssq_ref)
    for copy in copies:
        copy.wait()


def near_projection(mine, beside, own_weight, beside_weight, weight, far, last):
    rows = 2 * mine[0].shape[0]
    channels, width = own_weight.shape[1:]
    return pl.pallas_call(
        functools.partial(near_kernel, far, last),
        out_shape=(
            jax.ShapeDtypeStruct((rows, 3 * width), F32),
            jax.ShapeDtypeStruct((rows, LANES), F32),
            weight_rows(weight, len(far), channels),
            weight_rows(weight, len(last), channels),
        ),
        in_specs=[VMEM] * 6 + [HBM],
        out_specs=(VMEM,) * 4,
        scratch_shapes=[
            pltpu.SemaphoreType.DMA((len(far),)),
            pltpu.SemaphoreType.DMA((len(last),)),
        ],
        compiler_params=params(16),
        cost_estimate=cost(),
        name="projections_near",
    )(
        *mine,
        *beside,
        own_weight,
        beside_weight,
        pltpu.with_memory_space_constraint(weight, pltpu.HBM),
    )


def partial_kernel(count, *refs):
    blocks = [(refs[2 * n], refs[2 * n + 1]) for n in range(count)]
    weight_ref, acc_in, ssq_in, acc_ref, ssq_ref = refs[2 * count :]
    acc_ref[...] = acc_in[...]
    ssq_ref[...] = ssq_in[...]
    project(blocks, split_rows(weight_ref, count), acc_ref, ssq_ref)


def part_projection(blocks, weight, acc, ssq):
    return pl.pallas_call(
        functools.partial(partial_kernel, len(blocks)),
        out_shape=(
            jax.ShapeDtypeStruct(acc.shape, F32),
            jax.ShapeDtypeStruct(ssq.shape, F32),
        ),
        in_specs=[VMEM] * (2 * len(blocks) + 3),
        out_specs=(VMEM,) * 2,
        compiler_params=params(24),
        cost_estimate=cost(),
        name="projections_far",
    )(*[half for pair in blocks for half in pair], weight, acc, ssq)


def last_kernel(count, model, spread, *refs):
    blocks = [(refs[2 * n], refs[2 * n + 1]) for n in range(count)]
    weight_ref, acc_in, ssq_in = refs[2 * count : 2 * count + 3]
    outs, (acc_ref, ssq_ref) = refs[2 * count + 3 : -2], refs[-2:]
    acc_ref[...] = acc_in[...]
    ssq_ref[...] = ssq_in[...]
    project(blocks, split_rows(weight_ref, count), acc_ref, ssq_ref)
    msq = jnp.sum(ssq_ref[...], axis=1, keepdims=True) / model
    scale = lax.rsqrt(msq + EPS)
    rows = acc_ref.shape[0]
    width = weight_ref.shape[2]
    heads = width // HEAD_DIM
    place = lax.axis_index("ctx") // 2 if spread else 0
    for n, out in enumerate(outs):
        head = jnp.bitwise_xor(place, heads - 1 - n)
        for which in range(3):
            lanes = pl.ds(pl.multiple_of(which * width + head * HEAD_DIM, LANES), HEAD_DIM)
            out[which * rows : (which + 1) * rows, :] = (acc_ref[:, lanes] * scale).astype(BF16)


def last_projection(blocks, weight, acc, ssq, model, spread):
    rows = acc.shape[0]
    heads = weight.shape[2] // HEAD_DIM
    return pl.pallas_call(
        functools.partial(last_kernel, len(blocks), model, spread),
        out_shape=tuple(
            jax.ShapeDtypeStruct((3 * rows, HEAD_DIM), BF16) for _ in range(heads)
        ),
        in_specs=[VMEM] * (2 * len(blocks) + 3),
        out_specs=(VMEM,) * heads,
        scratch_shapes=[pltpu.VMEM(acc.shape, F32), pltpu.VMEM(ssq.shape, F32)],
        compiler_params=params(24),
        cost_estimate=cost(),
        name="projections_last",
    )(*[half for pair in blocks for half in pair], weight, acc, ssq)


def base_of(shape, axis, rows, y):
    index = lax.broadcasted_iota(jnp.int32, shape, axis)
    block = 2 * jnp.bitwise_xor(index // rows, lax.axis_index("ctx") // 2) + y
    return block * rows + index % rows


def scores_of(query, keys, rows, key_base):
    product = lax.dot_general(
        query, keys, (((1,), (1,)), ((), ())), preferred_element_type=F32
    ) * (1.0 / math.sqrt(HEAD_DIM))
    query_base = base_of((query.shape[0], 1), 0, rows, lax.axis_index("ctx") % 2)
    return jnp.where(query_base >= key_base, product, -1e30)


def most_kernel(count, *refs):
    blocks, others = refs[:count], refs[count : 2 * count - 1]
    query_ref, top_ref, total_ref, summed_ref, key_ref, value_ref = refs[2 * count - 1 :]
    rows = blocks[0].shape[0] // 3
    for n, block in enumerate(blocks):
        spot = slice(n * rows, (n + 1) * rows)
        query_ref[spot, :] = block[:rows, :]
        key_ref[spot, :] = block[rows : 2 * rows, :]
        value_ref[spot, :] = block[2 * rows :, :]
    for n, other in enumerate(others, count):
        key_ref[n * rows : (n + 1) * rows, :] = other[:rows, :]
        value_ref[n * rows : (n + 1) * rows, :] = other[rows:, :]
    y = lax.axis_index("ctx") % 2
    key_base = jnp.concatenate(
        [
            base_of((1, count * rows), 1, rows, y),
            base_of((1, (count - 1) * rows), 1, rows, 1 - y),
        ],
        axis=1,
    )
    scores = scores_of(query_ref[...], key_ref[...], rows, key_base)
    top = jnp.max(scores, axis=1, keepdims=True)
    expo = jnp.exp(scores - top)
    top_ref[...] = jnp.broadcast_to(top, top_ref.shape)
    total_ref[...] = jnp.broadcast_to(jnp.sum(expo, axis=1, keepdims=True), total_ref.shape)
    summed_ref[...] = jnp.dot(expo.astype(BF16), value_ref[...], preferred_element_type=F32)


def attend_most(blocks, others):
    count = len(blocks)
    rows = blocks[0].shape[0] // 3
    keys = pltpu.VMEM(((2 * count - 1) * rows, HEAD_DIM), BF16)
    shape = jax.ShapeDtypeStruct((count * rows, LANES), F32)
    return pl.pallas_call(
        functools.partial(most_kernel, count),
        out_shape=(jax.ShapeDtypeStruct((count * rows, HEAD_DIM), BF16), shape, shape, shape),
        in_specs=[VMEM] * (2 * count - 1),
        out_specs=(VMEM,) * 4,
        scratch_shapes=[keys, keys],
        compiler_params=params(16),
        cost_estimate=cost(),
        name="attention_most",
    )(*blocks, *others)


def rest_kernel(other_ref, query_ref, top_ref, total_ref, summed_ref, *outs):
    count = len(outs)
    rows = outs[0].shape[0]
    y = lax.axis_index("ctx") % 2
    key_base = base_of((1, count * rows), 1, rows, 1 - y)[:, (count - 1) * rows :]
    scores = scores_of(query_ref[...], other_ref[:rows, :], rows, key_base)
    before = top_ref[...]
    top = jnp.maximum(before[:, :1], jnp.max(scores, axis=1, keepdims=True))
    expo = jnp.exp(scores - top)
    fade = jnp.exp(before - top)
    total = total_ref[...] * fade + jnp.sum(expo, axis=1, keepdims=True)
    summed = summed_ref[...] * fade + jnp.dot(
        expo.astype(BF16), other_ref[rows:, :], preferred_element_type=F32
    )
    attended = (summed / total).astype(BF16)
    for n, out in enumerate(reversed(outs)):
        out[...] = attended[n * rows : (n + 1) * rows, :]


def attend_rest(other, state, count):
    rows = other.shape[0] // 2
    return pl.pallas_call(
        rest_kernel,
        out_shape=tuple(jax.ShapeDtypeStruct((rows, HEAD_DIM), BF16) for _ in range(count)),
        in_specs=[VMEM] * 5,
        out_specs=(VMEM,) * count,
        compiler_params=params(16),
        cost_estimate=cost(),
        name="attention_rest",
    )(other, *state)


def join_kernel(*refs):
    blocks, out = refs[:-1], refs[-1]
    for n, block in enumerate(blocks):
        head = jnp.bitwise_xor(lax.axis_index("ctx") // 2, len(blocks) - 1 - n)
        out[:, pl.ds(pl.multiple_of(head * HEAD_DIM, LANES), HEAD_DIM)] = block[...]


def join(blocks):
    rows = blocks[0].shape[0]
    return pl.pallas_call(
        join_kernel,
        out_shape=jax.ShapeDtypeStruct((rows, len(blocks) * HEAD_DIM), BF16),
        in_specs=[VMEM] * len(blocks),
        out_specs=VMEM,
        compiler_params=params(4),
        cost_estimate=cost(),
        name="join_heads",
    )(*blocks)


def gathered_attention(message, heads, rows):
    parts = jnp.stack([m.reshape(3, rows, HEAD_DIM) for m in message], axis=2)
    query, keys, values = parts[0], parts[1], parts[2]
    keys = lax.all_gather(keys, "ctx", axis=0, tiled=True)
    values = lax.all_gather(values, "ctx", axis=0, tiled=True)
    query_pos = lax.axis_index("ctx") * rows + jnp.arange(rows, dtype=jnp.int32)
    key_pos = jnp.arange(keys.shape[0], dtype=jnp.int32)
    scores = jnp.einsum("qhd,khd->hqk", query, keys, preferred_element_type=F32)
    allowed = (query_pos[:, None] >= key_pos[None, :])[None]
    scores = jnp.where(allowed, scores / math.sqrt(HEAD_DIM), -1e30)
    expo = jnp.where(allowed, jnp.exp(scores - jnp.max(scores, axis=2, keepdims=True)), 0.0)
    total = jnp.sum(expo, axis=2)
    summed = jnp.einsum("hqk,khd->qhd", expo.astype(BF16), values, preferred_element_type=F32)
    return (summed / total.T[:, :, None]).astype(BF16).reshape(rows, heads * HEAD_DIM)


def body(gate_in, conv_in, value_in, filter_taps, norm_gain, qkv_weight):
    rows, channels = gate_in.shape
    ctx, tp = lax.axis_size("ctx"), lax.axis_size("tp")
    weight = jnp.transpose(qkv_weight, (1, 0, 2))
    heads = weight.shape[2] // HEAD_DIM
    model = weight.shape[1]
    chip_per_head = heads * 2 == ctx and heads & (heads - 1) == 0

    wide = SLAB * LANES

    def widened(value):
        return jnp.pad(value, ((0, 0), (0, wide - channels))) if channels < wide else value

    def narrowed(sent):
        if channels == wide:
            return sent
        return jnp.concatenate([sent[:, :channels], sent[:, wide:]], axis=1)

    def swapped(value, by):
        return lax.ppermute(value, "tp", [(i, i ^ by) for i in range(tp)])

    high, low, taps, gate = mixed_halves(
        *(widened(v) for v in (conv_in, value_in, filter_taps, gate_in))
    )
    rim_high, rim_low = (
        lax.ppermute(part, "ctx", [(i, i + 1) for i in range(ctx - 1)]) for part in (high, low)
    )
    gain = widened(norm_gain[None])
    sums_low, sums_high, taps, own_weight = own_part(low, high, taps, weight, channels)
    sent_high, x_high, last = high_part(rim_high, sums_high, taps, gate, gain)
    steps = [(tp >> n) ^ 1 for n in range(1, tp.bit_length() - 1)]
    offsets = []
    for by in steps:
        offsets += [o ^ by for o in [0] + offsets]
    sent_high = narrowed(sent_high)
    near_high = swapped(sent_high, 1)
    x_high, near_high = lax.optimization_barrier((x_high, near_high))
    sent_low, beside_weight = low_part(
        rim_low, sums_low, x_high, last, taps, gate, gain, weight, (1,), channels
    )
    sent_low = narrowed(sent_low)
    sent = (sent_low, sent_high)
    far = []
    for by in steps:
        far += [tuple(swapped(part, by) for part in pair) for pair in [sent] + far]
    acc, ssq, far_weight, last_weight = near_projection(
        sent,
        (swapped(sent_low, 1), near_high),
        own_weight,
        beside_weight,
        weight,
        tuple(offsets),
        tuple(o ^ 1 for o in offsets),
    )
    last_low, acc = lax.optimization_barrier((far[-1][0], acc))
    far[-1] = (last_low, far[-1][1])
    swaps = [tuple(swapped(part, 1) for part in pair) for pair in far]
    acc, ssq = part_projection(far, far_weight, acc, ssq)
    messages = last_projection(swaps, last_weight, acc, ssq, model, chip_per_head)
    if not chip_per_head:
        return gathered_attention(messages[::-1], heads, rows)

    def over_z(value, k):
        pairs = [(i * tp + t, (i ^ (2 * k)) * tp + (t ^ 1)) for i in range(ctx) for t in range(tp)]
        return lax.ppermute(value, ("ctx", "tp"), pairs)

    def over_y(value):
        return lax.ppermute(value, "ctx", [(i, i ^ 1) for i in range(ctx)])

    order = range(heads - 1, -1, -1)
    held = [over_z(value, k) for value, k in zip(messages, order)]
    others = [over_y(value[rows:]) for value in held]
    held, others = held[::-1], others[::-1]
    done = attend_rest(others[-1], attend_most(held, others[:-1]), heads)
    return join([over_z(value, k) for value, k in zip(done, order)])


def solution(mesh):
    placed = (
        P("ctx", "tp"),
        P("ctx", "tp"),
        P("ctx", "tp"),
        P(None, "tp"),
        P("tp"),
        P(None, None, "tp"),
    )
    return jax.shard_map(
        body, mesh=mesh, in_specs=placed, out_specs=P("ctx", "tp"), check_vma=False
    )
```

```python
import functools
import math

import jax
import jax.numpy as jnp
from jax import lax
from jax.experimental import pallas as pl
from jax.experimental.pallas import tpu as pltpu
from jax.sharding import PartitionSpec as P

HEAD_DIM = 128
LANES = 128
SLAB = 8
PHASES = 4
SUBS = 9
HELD = 8
EPS = 1e-06
BF16 = jnp.bfloat16
F32 = jnp.float32
VMEM = pl.BlockSpec(memory_space=pltpu.VMEM)
HBM = pl.BlockSpec(memory_space=pltpu.HBM)


def params(mib):
    return pltpu.CompilerParams(vmem_limit_bytes=mib << 20)


def cost():
    return pl.CostEstimate(flops=0, bytes_accessed=1024, transcendentals=0)


def slabs(count):
    return jax.ShapeDtypeStruct((count * SLAB, LANES), F32)


def slab_scratch(count):
    return pltpu.VMEM((count * SLAB, LANES), F32)


def at(index):
    if not isinstance(index, int):
        return pl.ds(pl.multiple_of(index * SLAB, SLAB), SLAB)
    return pl.ds(index * SLAB, SLAB)


def to_slabs(source, target):
    for group in range(SLAB):
        target[pl.ds(group, source.shape[0], stride=SLAB), :] = source[
            :, group * LANES : (group + 1) * LANES
        ].astype(F32)


def to_subs(source, count, target):
    for n in range(count):
        x0, x1, x2, x3 = (source[at(PHASES * n + p), :] for p in range(PHASES))
        low, high = x0 + x1, x2 + x3
        for s, value in enumerate((x0, x2, x0 + x2, x1, x3, x1 + x3, low, high, low + high)):
            target[at(s * count + n), :] = value


def accumulate(sums, first, lag, taps, tap_at, x_ref, x_at, x_first, x_count, span):
    sums = list(sums)
    for start in range(x_first, x_first + x_count, HELD):
        places = range(start, min(start + HELD, x_first + x_count))
        used = {}
        for i in places:
            x = x_ref[at(x_at + (i - x_first)), :]
            for k in range(len(sums)):
                j = lag + first + k - i
                if 0 <= j < span:
                    if j not in used:
                        used[j] = taps[at(tap_at + j), :]
                    sums[k] = sums[k] + used[j] * x
    return sums


def finish(z_ref, count, full_ref):
    def z(s, k):
        return z_ref[at(s * (count + 1) + k), :]

    before = [z(s, 0) for s in range(SUBS)]
    for n in range(count):
        now = [z(s, n + 1) for s in range(SUBS)]

        def even(s):
            return now[s] + before[s + 1]

        def odd(s, held):
            return held[s + 2] - held[s] - held[s + 1]

        a_even, a_odd, b_even, b_odd = even(0), odd(0, now), even(3), odd(3, now)
        full_ref[at(PHASES * n), :] = a_even + odd(3, before)
        full_ref[at(PHASES * n + 1), :] = even(6) - a_even - b_even
        full_ref[at(PHASES * n + 2), :] = a_odd + b_even
        full_ref[at(PHASES * n + 3), :] = odd(6, now) - a_odd - b_odd
        before = now


def emit(full_ref, gate_ref, first, gain_ref, sent_ref, first_half, second_half):
    rows = sent_ref.shape[0]
    squares = jnp.zeros((rows, LANES), F32)
    for group in range(SLAB):
        lanes = slice(group * LANES, (group + 1) * LANES)
        hyena = (
            (
                gate_ref[first : first + rows, lanes].astype(F32)
                * full_ref[pl.ds(group, rows, stride=SLAB), :]
            )
            .astype(BF16)
            .astype(F32)
        )
        squares = squares + hyena * hyena
        sent_ref[:, lanes] = (hyena * gain_ref[:, lanes]).astype(BF16)
    total = jnp.sum(squares, axis=1, keepdims=True)
    pieces = []
    for _ in range(3):
        pieces.append(total.astype(BF16).astype(F32))
        total = total - pieces[-1]
    lane = lax.broadcasted_iota(jnp.int32, (rows, LANES), 1)
    row = jnp.zeros((rows, LANES), F32)
    for place, piece in enumerate(pieces):
        row = jnp.where(lane == place, piece, row)
    sent_ref[:, SLAB * LANES :] = row.astype(BF16)
    first_half[...] = sent_ref[: rows // 2, :]
    second_half[...] = sent_ref[rows // 2 :, :]


def mixed_kernel(
    conv_hbm,
    value_hbm,
    taps_hbm,
    gate_hbm,
    high_ref,
    low_ref,
    taps_ref,
    gate_ref,
    conv_ref,
    value_ref,
    sems,
):
    half = high_ref.shape[0]
    pairs = (
        (conv_hbm, conv_ref),
        (value_hbm, value_ref),
        (taps_hbm, taps_ref),
        (gate_hbm, gate_ref),
    )
    copies = [
        pltpu.make_async_copy(source, target, sems.at[n])
        for n, (source, target) in enumerate(pairs)
    ]
    for copy in copies:
        copy.start()
    for copy in copies[:2]:
        copy.wait()
    mixed = (conv_ref[...].astype(F32) * value_ref[...].astype(F32)).astype(BF16)
    high_ref[...] = mixed[half:, :]
    low_ref[...] = mixed[: low_ref.shape[0], :]
    for copy in copies[2:]:
        copy.wait()


def mixed_halves(conv, value, taps, gate):
    rows, channels = conv.shape
    half = rows // 2
    arrays = (conv, value, taps, gate)
    return pl.pallas_call(
        mixed_kernel,
        out_shape=(
            jax.ShapeDtypeStruct((half, channels), BF16),
            jax.ShapeDtypeStruct((half, channels), BF16),
            jax.ShapeDtypeStruct(taps.shape, F32),
            jax.ShapeDtypeStruct(gate.shape, BF16),
        ),
        in_specs=[HBM] * 4,
        out_specs=(VMEM,) * 4,
        scratch_shapes=[
            pltpu.VMEM(conv.shape, BF16),
            pltpu.VMEM(conv.shape, BF16),
            pltpu.SemaphoreType.DMA((4,)),
        ],
        compiler_params=params(8),
        cost_estimate=cost(),
        name="conv_times_value",
    )(*(pltpu.with_memory_space_constraint(v, pltpu.HBM) for v in arrays))


def own_kernel(
    low_ref,
    high_ref,
    taps_ref,
    weight_hbm,
    sums_low,
    sums_high,
    tap_subs,
    weight_ref,
    slab_ref,
    x_subs,
    sems,
):
    half, span = high_ref.shape[0], taps_ref.shape[0]
    quarter, eighth = 2 * half // PHASES, half // PHASES
    tap_quarter = span // PHASES
    copies = weight_copies(weight_hbm, weight_ref, (0,), sems)
    for copy in copies:
        copy.start()
    to_slabs(low_ref.at[pl.ds(0, half)], slab_ref.at[pl.ds(0, half * SLAB)])
    to_slabs(high_ref, slab_ref.at[pl.ds(half * SLAB, half * SLAB)])
    to_subs(slab_ref, quarter, x_subs)
    to_slabs(taps_ref, slab_ref)
    to_subs(slab_ref, tap_quarter, tap_subs)

    def sub(s, _):
        zero = jnp.zeros((SLAB, LANES), F32)
        sums_low[at(s * eighth), :] = zero
        for first in (0, eighth):
            sums = accumulate(
                [zero] * eighth, first, 0, tap_subs, s * tap_quarter, x_subs, s * quarter,
                0, first + eighth, tap_quarter,
            )
            for k, value in enumerate(sums):
                n = first + k
                if n < eighth - 1:
                    sums_low[at(s * eighth + n + 1), :] = value
                else:
                    sums_high[at(s * (eighth + 1) + n + 1 - eighth), :] = value
        return 0

    lax.fori_loop(0, SUBS, sub, 0)
    for copy in copies:
        copy.wait()


def weight_copies(weight_hbm, weight_ref, offsets, sems):
    copies = []
    channels = weight_ref.shape[1] // len(offsets)
    for n, offset in enumerate(offsets):
        owner = jnp.bitwise_xor(lax.axis_index("tp"), offset)
        copies.append(
            pltpu.make_async_copy(
                weight_hbm.at[:, pl.ds(pl.multiple_of(owner * channels, channels), channels), :],
                weight_ref.at[:, pl.ds(n * channels, channels), :],
                sems.at[n],
            )
        )
    return copies


def weight_rows(weight, count, channels):
    return jax.ShapeDtypeStruct((3, count * channels, weight.shape[2]), BF16)


def own_part(low, high, taps, weight, channels):
    rows, span = 2 * high.shape[0], taps.shape[0]
    quarter = rows // PHASES
    eighth = quarter // 2
    return pl.pallas_call(
        own_kernel,
        out_shape=(
            slabs(SUBS * eighth),
            slabs(SUBS * (eighth + 1)),
            slabs(SUBS * span // PHASES),
            weight_rows(weight, 1, channels),
        ),
        in_specs=[VMEM] * 3 + [HBM],
        out_specs=(VMEM,) * 4,
        scratch_shapes=[
            slab_scratch(max(rows, span)),
            slab_scratch(SUBS * quarter),
            pltpu.SemaphoreType.DMA((1,)),
        ],
        compiler_params=params(16),
        cost_estimate=cost(),
        name="fir_own_rows",
    )(low, high, taps, pltpu.with_memory_space_constraint(weight, pltpu.HBM))


def high_kernel(
    rim_ref,
    sums_ref,
    tap_subs,
    gate_ref,
    gain_ref,
    sent_ref,
    first_ref,
    second_ref,
    x_subs,
    last_ref,
    slab_ref,
    z_ref,
):
    rows = sent_ref.shape[0]
    eighth = rows // PHASES
    tap_quarter = tap_subs.shape[0] // SLAB // SUBS
    to_slabs(rim_ref, slab_ref)
    to_subs(slab_ref, eighth, x_subs)

    def sub(s, _):
        at_z = s * (eighth + 1)
        sums = [sums_ref[at(at_z + k), :] for k in range(eighth + 1)]
        sums = accumulate(
            sums, eighth - 1, 2 * eighth, tap_subs, s * tap_quarter, x_subs, s * eighth,
            eighth, eighth, tap_quarter,
        )
        for k, value in enumerate(sums):
            z_ref[at(at_z + k), :] = value
        last_ref[at(s), :] = sums[0]
        return 0

    lax.fori_loop(0, SUBS, sub, 0)
    finish(z_ref, eighth, slab_ref)
    emit(slab_ref, gate_ref, rows, gain_ref, sent_ref, first_ref, second_ref)


def sent_shapes(rows):
    return tuple(
        jax.ShapeDtypeStruct((length, (SLAB + 1) * LANES), BF16)
        for length in (rows, rows // 2, rows // 2)
    )


def high_part(rim, sums, taps, gate, gain):
    rows = rim.shape[0]
    eighth = rows // PHASES
    return pl.pallas_call(
        high_kernel,
        out_shape=sent_shapes(rows) + (slabs(SUBS * eighth), slabs(SUBS)),
        in_specs=[VMEM] * 5,
        out_specs=(VMEM,) * 5,
        scratch_shapes=[slab_scratch(rows), slab_scratch(SUBS * (eighth + 1))],
        compiler_params=params(16),
        cost_estimate=cost(),
        name="fir_later_rows",
    )(rim, sums, taps, gate, gain)


def low_kernel(
    offsets,
    rim_ref,
    sums_ref,
    x_high,
    last_ref,
    tap_subs,
    gate_ref,
    gain_ref,
    weight_hbm,
    sent_ref,
    first_ref,
    second_ref,
    weight_ref,
    slab_ref,
    x_subs,
    z_ref,
    sems,
):
    copies = weight_copies(weight_hbm, weight_ref, offsets, sems)
    for copy in copies:
        copy.start()
    rows = sent_ref.shape[0]
    eighth = rows // PHASES
    tap_quarter = tap_subs.shape[0] // SLAB // SUBS
    to_slabs(rim_ref.at[pl.ds(0, rows)], slab_ref)
    to_subs(slab_ref, eighth, x_subs)

    def sub(s, _):
        sums = [sums_ref[at(s * eighth + k), :] for k in range(eighth)]
        for x_ref, first in ((x_high, eighth), (x_subs, 0)):
            sums = accumulate(
                sums, -1, 2 * eighth, tap_subs, s * tap_quarter, x_ref, s * eighth,
                first, eighth, tap_quarter,
            )
        for k, value in enumerate(sums + [last_ref[at(s), :]]):
            z_ref[at(s * (eighth + 1) + k), :] = value
        return 0

    lax.fori_loop(0, SUBS, sub, 0)
    finish(z_ref, eighth, slab_ref)
    emit(slab_ref, gate_ref, 0, gain_ref, sent_ref, first_ref, second_ref)
    for copy in copies:
        copy.wait()


def low_part(rim, sums, x_high, last, taps, gate, gain, weight, offsets, channels):
    rows = gate.shape[0] // 2
    eighth = rows // PHASES
    return pl.pallas_call(
        functools.partial(low_kernel, offsets),
        out_shape=sent_shapes(rows) + (weight_rows(weight, len(offsets), channels),),
        in_specs=[VMEM] * 7 + [HBM],
        out_specs=(VMEM,) * 4,
        scratch_shapes=[
            slab_scratch(rows),
            slab_scratch(SUBS * eighth),
            slab_scratch(SUBS * (eighth + 1)),
            pltpu.SemaphoreType.DMA((len(offsets),)),
        ],
        compiler_params=params(16),
        cost_estimate=cost(),
        name="fir_earlier_rows",
    )(
        rim,
        sums,
        x_high,
        last,
        taps,
        gate,
        gain,
        pltpu.with_memory_space_constraint(weight, pltpu.HBM),
    )


def project(blocks, weight_refs, acc_ref, ssq_ref):
    width = weight_refs[0].shape[2]
    whole = [jnp.concatenate([piece[...] for piece in pieces], axis=0) for pieces in blocks]
    channels = whole[0].shape[1] - LANES
    for block in whole:
        ssq_ref[...] += block[:, channels:].astype(F32)
    for which in range(3):
        lanes = slice(which * width, (which + 1) * width)
        total = acc_ref[:, lanes]
        for ref, block in zip(weight_refs, whole):
            total = total + jnp.dot(
                block[:, :channels],
                ref[which],
                preferred_element_type=F32,
            )
        acc_ref[:, lanes] = total


def split_rows(weight_ref, count):
    channels = weight_ref.shape[1] // count
    return [weight_ref.at[:, pl.ds(n * channels, channels), :] for n in range(count)]


def near_kernel(far, last, low_ref, high_ref, own_ref, weight_hbm, *refs):
    acc_ref, ssq_ref, far_ref, last_ref, far_sems, last_sems = refs
    copies = weight_copies(weight_hbm, far_ref, far, far_sems)
    copies += weight_copies(weight_hbm, last_ref, last, last_sems)
    for copy in copies:
        copy.start()
    acc_ref[...] = jnp.zeros_like(acc_ref)
    ssq_ref[...] = jnp.zeros_like(ssq_ref)
    project([(low_ref, high_ref)], [own_ref], acc_ref, ssq_ref)
    for copy in copies:
        copy.wait()


def near_projection(mine, own_weight, weight, far, last):
    rows = 2 * mine[0].shape[0]
    channels, width = own_weight.shape[1:]
    return pl.pallas_call(
        functools.partial(near_kernel, far, last),
        out_shape=(
            jax.ShapeDtypeStruct((rows, 3 * width), F32),
            jax.ShapeDtypeStruct((rows, LANES), F32),
            weight_rows(weight, len(far), channels),
            weight_rows(weight, len(last), channels),
        ),
        in_specs=[VMEM] * 3 + [HBM],
        out_specs=(VMEM,) * 4,
        scratch_shapes=[
            pltpu.SemaphoreType.DMA((len(far),)),
            pltpu.SemaphoreType.DMA((len(last),)),
        ],
        compiler_params=params(16),
        cost_estimate=cost(),
        name="projections_near",
    )(*mine, own_weight, pltpu.with_memory_space_constraint(weight, pltpu.HBM))


def partial_kernel(sizes, *refs):
    blocks, rest = [], list(refs)
    for size in sizes:
        blocks.append(rest[:size])
        del rest[:size]
    weight_ref, acc_in, ssq_in, acc_ref, ssq_ref = rest
    acc_ref[...] = acc_in[...]
    ssq_ref[...] = ssq_in[...]
    project(blocks, split_rows(weight_ref, len(blocks)), acc_ref, ssq_ref)


def part_projection(blocks, weight, acc, ssq):
    sizes = tuple(len(pieces) for pieces in blocks)
    return pl.pallas_call(
        functools.partial(partial_kernel, sizes),
        out_shape=(
            jax.ShapeDtypeStruct(acc.shape, F32),
            jax.ShapeDtypeStruct(ssq.shape, F32),
        ),
        in_specs=[VMEM] * (sum(sizes) + 3),
        out_specs=(VMEM,) * 2,
        compiler_params=params(24),
        cost_estimate=cost(),
        name="projections_part",
    )(*[piece for pieces in blocks for piece in pieces], weight, acc, ssq)


def last_kernel(count, model, spread, *refs):
    blocks = [(refs[2 * n], refs[2 * n + 1]) for n in range(count)]
    weight_ref, acc_in, ssq_in = refs[2 * count : 2 * count + 3]
    outs, (acc_ref, ssq_ref) = refs[2 * count + 3 : -2], refs[-2:]
    acc_ref[...] = acc_in[...]
    ssq_ref[...] = ssq_in[...]
    project(blocks, split_rows(weight_ref, count), acc_ref, ssq_ref)
    msq = jnp.sum(ssq_ref[...], axis=1, keepdims=True) / model
    scale = lax.rsqrt(msq + EPS)
    rows = acc_ref.shape[0]
    width = weight_ref.shape[2]
    heads = width // HEAD_DIM
    place = lax.axis_index("ctx") // 2 if spread else 0
    for n, out in enumerate(outs):
        head = jnp.bitwise_xor(place, heads - 1 - n)
        for which in range(3):
            lanes = pl.ds(pl.multiple_of(which * width + head * HEAD_DIM, LANES), HEAD_DIM)
            out[which * rows : (which + 1) * rows, :] = (acc_ref[:, lanes] * scale).astype(BF16)


def last_projection(blocks, weight, acc, ssq, model, spread):
    rows = acc.shape[0]
    heads = weight.shape[2] // HEAD_DIM
    return pl.pallas_call(
        functools.partial(last_kernel, len(blocks), model, spread),
        out_shape=tuple(
            jax.ShapeDtypeStruct((3 * rows, HEAD_DIM), BF16) for _ in range(heads)
        ),
        in_specs=[VMEM] * (2 * len(blocks) + 3),
        out_specs=(VMEM,) * heads,
        scratch_shapes=[pltpu.VMEM(acc.shape, F32), pltpu.VMEM(ssq.shape, F32)],
        compiler_params=params(24),
        cost_estimate=cost(),
        name="projections_last",
    )(*[half for pair in blocks for half in pair], weight, acc, ssq)


def base_of(shape, axis, rows, y):
    index = lax.broadcasted_iota(jnp.int32, shape, axis)
    block = 2 * jnp.bitwise_xor(index // rows, lax.axis_index("ctx") // 2) + y
    return block * rows + index % rows


def scores_of(query, keys, rows, key_base):
    product = lax.dot_general(
        query, keys, (((1,), (1,)), ((), ())), preferred_element_type=F32
    ) * (1.0 / math.sqrt(HEAD_DIM))
    query_base = base_of((query.shape[0], 1), 0, rows, lax.axis_index("ctx") % 2)
    return jnp.where(query_base >= key_base, product, -1e30)


def most_kernel(count, *refs):
    blocks, others = refs[:count], refs[count : 2 * count - 1]
    query_ref, top_ref, total_ref, summed_ref, key_ref, value_ref = refs[2 * count - 1 :]
    rows = blocks[0].shape[0] // 3
    for n, block in enumerate(blocks):
        spot = slice(n * rows, (n + 1) * rows)
        query_ref[spot, :] = block[:rows, :]
        key_ref[spot, :] = block[rows : 2 * rows, :]
        value_ref[spot, :] = block[2 * rows :, :]
    for n, other in enumerate(others, count):
        key_ref[n * rows : (n + 1) * rows, :] = other[:rows, :]
        value_ref[n * rows : (n + 1) * rows, :] = other[rows:, :]
    y = lax.axis_index("ctx") % 2
    key_base = jnp.concatenate(
        [
            base_of((1, count * rows), 1, rows, y),
            base_of((1, (count - 1) * rows), 1, rows, 1 - y),
        ],
        axis=1,
    )
    scores = scores_of(query_ref[...], key_ref[...], rows, key_base)
    top = jnp.max(scores, axis=1, keepdims=True)
    expo = jnp.exp(scores - top)
    top_ref[...] = jnp.broadcast_to(top, top_ref.shape)
    total_ref[...] = jnp.broadcast_to(jnp.sum(expo, axis=1, keepdims=True), total_ref.shape)
    summed_ref[...] = jnp.dot(expo.astype(BF16), value_ref[...], preferred_element_type=F32)


def attend_most(blocks, others):
    count = len(blocks)
    rows = blocks[0].shape[0] // 3
    keys = pltpu.VMEM(((2 * count - 1) * rows, HEAD_DIM), BF16)
    shape = jax.ShapeDtypeStruct((count * rows, LANES), F32)
    return pl.pallas_call(
        functools.partial(most_kernel, count),
        out_shape=(jax.ShapeDtypeStruct((count * rows, HEAD_DIM), BF16), shape, shape, shape),
        in_specs=[VMEM] * (2 * count - 1),
        out_specs=(VMEM,) * 4,
        scratch_shapes=[keys, keys],
        compiler_params=params(16),
        cost_estimate=cost(),
        name="attention_most",
    )(*blocks, *others)


def rest_kernel(other_ref, query_ref, top_ref, total_ref, summed_ref, *outs):
    count = len(outs)
    rows = outs[0].shape[0]
    y = lax.axis_index("ctx") % 2
    key_base = base_of((1, count * rows), 1, rows, 1 - y)[:, (count - 1) * rows :]
    scores = scores_of(query_ref[...], other_ref[:rows, :], rows, key_base)
    before = top_ref[...]
    top = jnp.maximum(before[:, :1], jnp.max(scores, axis=1, keepdims=True))
    expo = jnp.exp(scores - top)
    fade = jnp.exp(before - top)
    total = total_ref[...] * fade + jnp.sum(expo, axis=1, keepdims=True)
    summed = summed_ref[...] * fade + jnp.dot(
        expo.astype(BF16), other_ref[rows:, :], preferred_element_type=F32
    )
    attended = (summed / total).astype(BF16)
    for n, out in enumerate(reversed(outs)):
        out[...] = attended[n * rows : (n + 1) * rows, :]


def attend_rest(other, state, count):
    rows = other.shape[0] // 2
    return pl.pallas_call(
        rest_kernel,
        out_shape=tuple(jax.ShapeDtypeStruct((rows, HEAD_DIM), BF16) for _ in range(count)),
        in_specs=[VMEM] * 5,
        out_specs=(VMEM,) * count,
        compiler_params=params(16),
        cost_estimate=cost(),
        name="attention_rest",
    )(other, *state)


def join_kernel(*refs):
    blocks, out = refs[:-1], refs[-1]
    for n, block in enumerate(blocks):
        head = jnp.bitwise_xor(lax.axis_index("ctx") // 2, len(blocks) - 1 - n)
        out[:, pl.ds(pl.multiple_of(head * HEAD_DIM, LANES), HEAD_DIM)] = block[...]


def join(blocks):
    rows = blocks[0].shape[0]
    return pl.pallas_call(
        join_kernel,
        out_shape=jax.ShapeDtypeStruct((rows, len(blocks) * HEAD_DIM), BF16),
        in_specs=[VMEM] * len(blocks),
        out_specs=VMEM,
        compiler_params=params(4),
        cost_estimate=cost(),
        name="join_heads",
    )(*blocks)


def gathered_attention(message, heads, rows):
    parts = jnp.stack([m.reshape(3, rows, HEAD_DIM) for m in message], axis=2)
    query, keys, values = parts[0], parts[1], parts[2]
    keys = lax.all_gather(keys, "ctx", axis=0, tiled=True)
    values = lax.all_gather(values, "ctx", axis=0, tiled=True)
    query_pos = lax.axis_index("ctx") * rows + jnp.arange(rows, dtype=jnp.int32)
    key_pos = jnp.arange(keys.shape[0], dtype=jnp.int32)
    scores = jnp.einsum("qhd,khd->hqk", query, keys, preferred_element_type=F32)
    allowed = (query_pos[:, None] >= key_pos[None, :])[None]
    scores = jnp.where(allowed, scores / math.sqrt(HEAD_DIM), -1e30)
    expo = jnp.where(allowed, jnp.exp(scores - jnp.max(scores, axis=2, keepdims=True)), 0.0)
    total = jnp.sum(expo, axis=2)
    summed = jnp.einsum("hqk,khd->qhd", expo.astype(BF16), values, preferred_element_type=F32)
    return (summed / total.T[:, :, None]).astype(BF16).reshape(rows, heads * HEAD_DIM)


def body(gate_in, conv_in, value_in, filter_taps, norm_gain, qkv_weight):
    rows, channels = gate_in.shape
    ctx, tp = lax.axis_size("ctx"), lax.axis_size("tp")
    weight = jnp.transpose(qkv_weight, (1, 0, 2))
    heads = weight.shape[2] // HEAD_DIM
    model = weight.shape[1]
    chip_per_head = heads * 2 == ctx and heads & (heads - 1) == 0

    wide = SLAB * LANES

    def widened(value):
        return jnp.pad(value, ((0, 0), (0, wide - channels))) if channels < wide else value

    def narrowed(sent):
        if channels == wide:
            return sent
        return jnp.concatenate([sent[:, :channels], sent[:, wide:]], axis=1)

    def swapped(value, by):
        return lax.ppermute(value, "tp", [(i, i ^ by) for i in range(tp)])

    high, low, taps, gate = mixed_halves(
        *(widened(v) for v in (conv_in, value_in, filter_taps, gate_in))
    )
    rim_high, rim_low = (
        lax.ppermute(part, "ctx", [(i, i + 1) for i in range(ctx - 1)]) for part in (high, low)
    )
    gain = widened(norm_gain[None])
    sums_low, sums_high, taps, own_weight = own_part(low, high, taps, weight, channels)
    *high, x_high, last = high_part(rim_high, sums_high, taps, gate, gain)
    steps = [(tp >> n) ^ 1 for n in range(1, tp.bit_length() - 1)]
    offsets = []
    for by in steps:
        offsets += [o ^ by for o in [0] + offsets]
    sent_high, *halves = map(narrowed, high)
    near_high = [swapped(half, 1) for half in halves]
    x_high, near_high[0] = lax.optimization_barrier((x_high, near_high[0]))
    *low, beside_weight = low_part(
        rim_low, sums_low, x_high, last, taps, gate, gain, weight, (1,), channels
    )
    sent_low, *halves = map(narrowed, low)
    near_low = [swapped(half, 1) for half in halves]
    sent = (sent_low, sent_high)
    far = []
    for by in steps:
        far += [tuple(swapped(part, by) for part in pair) for pair in [sent] + far]
    acc, ssq, far_weight, last_weight = near_projection(
        sent, own_weight, weight, tuple(offsets), tuple(o ^ 1 for o in offsets)
    )
    acc, ssq = part_projection([near_low + near_high], beside_weight, acc, ssq)
    last_low, acc = lax.optimization_barrier((far[-1][0], acc))
    far[-1] = (last_low, far[-1][1])
    swaps = [tuple(swapped(part, 1) for part in pair) for pair in far]
    acc, ssq = part_projection(far, far_weight, acc, ssq)
    messages = last_projection(swaps, last_weight, acc, ssq, model, chip_per_head)
    if not chip_per_head:
        return gathered_attention(messages[::-1], heads, rows)

    def over_z(value, k):
        pairs = [(i * tp + t, (i ^ (2 * k)) * tp + (t ^ 1)) for i in range(ctx) for t in range(tp)]
        return lax.ppermute(value, ("ctx", "tp"), pairs)

    def over_y(value):
        return lax.ppermute(value, "ctx", [(i, i ^ 1) for i in range(ctx)])

    order = range(heads - 1, -1, -1)
    held = [over_z(value, k) for value, k in zip(messages, order)]
    others = [over_y(value[rows:]) for value in held]
    held, others = held[::-1], others[::-1]
    done = attend_rest(others[-1], attend_most(held, others[:-1]), heads)
    return join([over_z(value, k) for value, k in zip(done, order)])


def solution(mesh):
    placed = (
        P("ctx", "tp"),
        P("ctx", "tp"),
        P("ctx", "tp"),
        P(None, "tp"),
        P("tp"),
        P(None, None, "tp"),
    )
    return jax.shard_map(
        body, mesh=mesh, in_specs=placed, out_specs=P("ctx", "tp"), check_vma=False
    )
```

```python
import functools
import math

import jax
import jax.numpy as jnp
from jax import lax
from jax.experimental import pallas as pl
from jax.experimental.pallas import tpu as pltpu
from jax.sharding import PartitionSpec as P

HEAD_DIM = 128
LANES = 128
SLAB = 8
TAKEN = {4: (0, 3, 1, 2)}
GIVEN = {4: (2, 3, 1, 0)}
PHASES = 4
SUBS = 9
HELD = 8
EPS = 1e-06
BF16 = jnp.bfloat16
F32 = jnp.float32
VMEM = pl.BlockSpec(memory_space=pltpu.VMEM)
HBM = pl.BlockSpec(memory_space=pltpu.HBM)


def params(mib):
    return pltpu.CompilerParams(vmem_limit_bytes=mib << 20)


def cost():
    return pl.CostEstimate(flops=0, bytes_accessed=1024, transcendentals=0)


def slabs(count):
    return jax.ShapeDtypeStruct((count * SLAB, LANES), F32)


def slab_scratch(count):
    return pltpu.VMEM((count * SLAB, LANES), F32)


def at(index):
    if not isinstance(index, int):
        return pl.ds(pl.multiple_of(index * SLAB, SLAB), SLAB)
    return pl.ds(index * SLAB, SLAB)


def to_slabs(source, target):
    for group in range(SLAB):
        target[pl.ds(group, source.shape[0], stride=SLAB), :] = source[
            :, group * LANES : (group + 1) * LANES
        ].astype(F32)


def to_subs(source, count, target):
    for n in range(count):
        x0, x1, x2, x3 = (source[at(PHASES * n + p), :] for p in range(PHASES))
        low, high = x0 + x1, x2 + x3
        for s, value in enumerate((x0, x2, x0 + x2, x1, x3, x1 + x3, low, high, low + high)):
            target[at(s * count + n), :] = value


def accumulate(sums, first, lag, taps, tap_at, x_ref, x_at, x_first, x_count, span):
    sums = list(sums)
    for start in range(x_first, x_first + x_count, HELD):
        places = range(start, min(start + HELD, x_first + x_count))
        used = {}
        for i in places:
            x = x_ref[at(x_at + (i - x_first)), :]
            for k in range(len(sums)):
                j = lag + first + k - i
                if 0 <= j < span:
                    if j not in used:
                        used[j] = taps[at(tap_at + j), :]
                    sums[k] = sums[k] + used[j] * x
    return sums


def finish(z_ref, count, full_ref):
    def z(s, k):
        return z_ref[at(s * (count + 1) + k), :]

    before = [z(s, 0) for s in range(SUBS)]
    for n in range(count):
        now = [z(s, n + 1) for s in range(SUBS)]

        def even(s):
            return now[s] + before[s + 1]

        def odd(s, held):
            return held[s + 2] - held[s] - held[s + 1]

        a_even, a_odd, b_even, b_odd = even(0), odd(0, now), even(3), odd(3, now)
        full_ref[at(PHASES * n), :] = a_even + odd(3, before)
        full_ref[at(PHASES * n + 1), :] = even(6) - a_even - b_even
        full_ref[at(PHASES * n + 2), :] = a_odd + b_even
        full_ref[at(PHASES * n + 3), :] = odd(6, now) - a_odd - b_odd
        before = now


def emit(full_ref, gate_ref, first, gain_ref, sent_ref, first_half, second_half):
    rows = sent_ref.shape[0]
    squares = jnp.zeros((rows, LANES), F32)
    for group in range(SLAB):
        lanes = slice(group * LANES, (group + 1) * LANES)
        hyena = (
            (
                gate_ref[first : first + rows, lanes].astype(F32)
                * full_ref[pl.ds(group, rows, stride=SLAB), :]
            )
            .astype(BF16)
            .astype(F32)
        )
        squares = squares + hyena * hyena
        sent_ref[:, lanes] = (hyena * gain_ref[:, lanes]).astype(BF16)
    total = jnp.sum(squares, axis=1, keepdims=True)
    pieces = []
    for _ in range(3):
        pieces.append(total.astype(BF16).astype(F32))
        total = total - pieces[-1]
    lane = lax.broadcasted_iota(jnp.int32, (rows, LANES), 1)
    row = jnp.zeros((rows, LANES), F32)
    for place, piece in enumerate(pieces):
        row = jnp.where(lane == place, piece, row)
    sent_ref[:, SLAB * LANES :] = row.astype(BF16)
    first_half[...] = sent_ref[: rows // 2, :]
    second_half[...] = sent_ref[rows // 2 :, :]


def mixed_kernel(
    conv_hbm,
    value_hbm,
    taps_hbm,
    gate_hbm,
    high_ref,
    low_ref,
    taps_ref,
    gate_ref,
    conv_ref,
    value_ref,
    sems,
):
    half = high_ref.shape[0]
    pairs = (
        (conv_hbm, conv_ref),
        (value_hbm, value_ref),
        (taps_hbm, taps_ref),
        (gate_hbm, gate_ref),
    )
    copies = [
        pltpu.make_async_copy(source, target, sems.at[n])
        for n, (source, target) in enumerate(pairs)
    ]
    for copy in copies:
        copy.start()
    for copy in copies[:2]:
        copy.wait()
    mixed = (conv_ref[...].astype(F32) * value_ref[...].astype(F32)).astype(BF16)
    high_ref[...] = mixed[half:, :]
    low_ref[...] = mixed[: low_ref.shape[0], :]
    for copy in copies[2:]:
        copy.wait()


def mixed_halves(conv, value, taps, gate):
    rows, channels = conv.shape
    half = rows // 2
    arrays = (conv, value, taps, gate)
    return pl.pallas_call(
        mixed_kernel,
        out_shape=(
            jax.ShapeDtypeStruct((half, channels), BF16),
            jax.ShapeDtypeStruct((half, channels), BF16),
            jax.ShapeDtypeStruct(taps.shape, F32),
            jax.ShapeDtypeStruct(gate.shape, BF16),
        ),
        in_specs=[HBM] * 4,
        out_specs=(VMEM,) * 4,
        scratch_shapes=[
            pltpu.VMEM(conv.shape, BF16),
            pltpu.VMEM(conv.shape, BF16),
            pltpu.SemaphoreType.DMA((4,)),
        ],
        compiler_params=params(8),
        cost_estimate=cost(),
        name="conv_times_value",
    )(*(pltpu.with_memory_space_constraint(v, pltpu.HBM) for v in arrays))


def own_kernel(
    low_ref,
    high_ref,
    taps_ref,
    weight_hbm,
    sums_low,
    sums_high,
    tap_subs,
    weight_ref,
    slab_ref,
    x_subs,
    sems,
):
    half, span = high_ref.shape[0], taps_ref.shape[0]
    quarter, eighth = 2 * half // PHASES, half // PHASES
    tap_quarter = span // PHASES
    copies = weight_copies(weight_hbm, weight_ref, (0,), sems)
    for copy in copies:
        copy.start()
    to_slabs(low_ref.at[pl.ds(0, half)], slab_ref.at[pl.ds(0, half * SLAB)])
    to_slabs(high_ref, slab_ref.at[pl.ds(half * SLAB, half * SLAB)])
    to_subs(slab_ref, quarter, x_subs)
    to_slabs(taps_ref, slab_ref)
    to_subs(slab_ref, tap_quarter, tap_subs)

    def sub(s, _):
        zero = jnp.zeros((SLAB, LANES), F32)
        sums_low[at(s * eighth), :] = zero
        for first in (0, eighth):
            sums = accumulate(
                [zero] * eighth, first, 0, tap_subs, s * tap_quarter, x_subs, s * quarter,
                0, first + eighth, tap_quarter,
            )
            for k, value in enumerate(sums):
                n = first + k
                if n < eighth - 1:
                    sums_low[at(s * eighth + n + 1), :] = value
                else:
                    sums_high[at(s * (eighth + 1) + n + 1 - eighth), :] = value
        return 0

    lax.fori_loop(0, SUBS, sub, 0)
    for copy in copies:
        copy.wait()


def weight_copies(weight_hbm, weight_ref, offsets, sems):
    copies = []
    channels = weight_ref.shape[1] // len(offsets)
    for n, offset in enumerate(offsets):
        owner = jnp.bitwise_xor(lax.axis_index("tp"), offset)
        copies.append(
            pltpu.make_async_copy(
                weight_hbm.at[:, pl.ds(pl.multiple_of(owner * channels, channels), channels), :],
                weight_ref.at[:, pl.ds(n * channels, channels), :],
                sems.at[n],
            )
        )
    return copies


def weight_rows(weight, count, channels):
    return jax.ShapeDtypeStruct((3, count * channels, weight.shape[2]), BF16)


def own_part(low, high, taps, weight, channels):
    rows, span = 2 * high.shape[0], taps.shape[0]
    quarter = rows // PHASES
    eighth = quarter // 2
    return pl.pallas_call(
        own_kernel,
        out_shape=(
            slabs(SUBS * eighth),
            slabs(SUBS * (eighth + 1)),
            slabs(SUBS * span // PHASES),
            weight_rows(weight, 1, channels),
        ),
        in_specs=[VMEM] * 3 + [HBM],
        out_specs=(VMEM,) * 4,
        scratch_shapes=[
            slab_scratch(max(rows, span)),
            slab_scratch(SUBS * quarter),
            pltpu.SemaphoreType.DMA((1,)),
        ],
        compiler_params=params(16),
        cost_estimate=cost(),
        name="fir_own_rows",
    )(low, high, taps, pltpu.with_memory_space_constraint(weight, pltpu.HBM))


def high_kernel(
    rim_ref,
    sums_ref,
    tap_subs,
    gate_ref,
    gain_ref,
    sent_ref,
    first_ref,
    second_ref,
    x_subs,
    last_ref,
    slab_ref,
    z_ref,
):
    rows = sent_ref.shape[0]
    eighth = rows // PHASES
    tap_quarter = tap_subs.shape[0] // SLAB // SUBS
    to_slabs(rim_ref, slab_ref)
    to_subs(slab_ref, eighth, x_subs)

    def sub(s, _):
        at_z = s * (eighth + 1)
        sums = [sums_ref[at(at_z + k), :] for k in range(eighth + 1)]
        sums = accumulate(
            sums, eighth - 1, 2 * eighth, tap_subs, s * tap_quarter, x_subs, s * eighth,
            eighth, eighth, tap_quarter,
        )
        for k, value in enumerate(sums):
            z_ref[at(at_z + k), :] = value
        last_ref[at(s), :] = sums[0]
        return 0

    lax.fori_loop(0, SUBS, sub, 0)
    finish(z_ref, eighth, slab_ref)
    emit(slab_ref, gate_ref, rows, gain_ref, sent_ref, first_ref, second_ref)


def sent_shapes(rows):
    return tuple(
        jax.ShapeDtypeStruct((length, (SLAB + 1) * LANES), BF16)
        for length in (rows, rows // 2, rows // 2)
    )


def high_part(rim, sums, taps, gate, gain):
    rows = rim.shape[0]
    eighth = rows // PHASES
    return pl.pallas_call(
        high_kernel,
        out_shape=sent_shapes(rows) + (slabs(SUBS * eighth), slabs(SUBS)),
        in_specs=[VMEM] * 5,
        out_specs=(VMEM,) * 5,
        scratch_shapes=[slab_scratch(rows), slab_scratch(SUBS * (eighth + 1))],
        compiler_params=params(16),
        cost_estimate=cost(),
        name="fir_later_rows",
    )(rim, sums, taps, gate, gain)


def low_kernel(
    offsets,
    rim_ref,
    sums_ref,
    x_high,
    last_ref,
    tap_subs,
    gate_ref,
    gain_ref,
    weight_hbm,
    sent_ref,
    first_ref,
    second_ref,
    weight_ref,
    slab_ref,
    x_subs,
    z_ref,
    sems,
):
    copies = weight_copies(weight_hbm, weight_ref, offsets, sems)
    for copy in copies:
        copy.start()
    rows = sent_ref.shape[0]
    eighth = rows // PHASES
    tap_quarter = tap_subs.shape[0] // SLAB // SUBS
    to_slabs(rim_ref.at[pl.ds(0, rows)], slab_ref)
    to_subs(slab_ref, eighth, x_subs)

    def sub(s, _):
        sums = [sums_ref[at(s * eighth + k), :] for k in range(eighth)]
        for x_ref, first in ((x_high, eighth), (x_subs, 0)):
            sums = accumulate(
                sums, -1, 2 * eighth, tap_subs, s * tap_quarter, x_ref, s * eighth,
                first, eighth, tap_quarter,
            )
        for k, value in enumerate(sums + [last_ref[at(s), :]]):
            z_ref[at(s * (eighth + 1) + k), :] = value
        return 0

    lax.fori_loop(0, SUBS, sub, 0)
    finish(z_ref, eighth, slab_ref)
    emit(slab_ref, gate_ref, 0, gain_ref, sent_ref, first_ref, second_ref)
    for copy in copies:
        copy.wait()


def low_part(rim, sums, x_high, last, taps, gate, gain, weight, offsets, channels):
    rows = gate.shape[0] // 2
    eighth = rows // PHASES
    return pl.pallas_call(
        functools.partial(low_kernel, offsets),
        out_shape=sent_shapes(rows) + (weight_rows(weight, len(offsets), channels),),
        in_specs=[VMEM] * 7 + [HBM],
        out_specs=(VMEM,) * 4,
        scratch_shapes=[
            slab_scratch(rows),
            slab_scratch(SUBS * eighth),
            slab_scratch(SUBS * (eighth + 1)),
            pltpu.SemaphoreType.DMA((len(offsets),)),
        ],
        compiler_params=params(16),
        cost_estimate=cost(),
        name="fir_earlier_rows",
    )(
        rim,
        sums,
        x_high,
        last,
        taps,
        gate,
        gain,
        pltpu.with_memory_space_constraint(weight, pltpu.HBM),
    )


def project(blocks, weight_refs, acc_ref, ssq_ref):
    width = weight_refs[0].shape[2]
    whole = [jnp.concatenate([piece[...] for piece in pieces], axis=0) for pieces in blocks]
    channels = whole[0].shape[1] - LANES
    for block in whole:
        ssq_ref[...] += block[:, channels:].astype(F32)
    for which in range(3):
        lanes = slice(which * width, (which + 1) * width)
        total = acc_ref[:, lanes]
        for ref, block in zip(weight_refs, whole):
            total = total + jnp.dot(
                block[:, :channels],
                ref[which],
                preferred_element_type=F32,
            )
        acc_ref[:, lanes] = total


def split_rows(weight_ref, count):
    channels = weight_ref.shape[1] // count
    return [weight_ref.at[:, pl.ds(n * channels, channels), :] for n in range(count)]


def near_kernel(far, last, low_ref, high_ref, own_ref, weight_hbm, *refs):
    acc_ref, ssq_ref, far_ref, last_ref, far_sems, last_sems = refs
    copies = weight_copies(weight_hbm, far_ref, far, far_sems)
    copies += weight_copies(weight_hbm, last_ref, last, last_sems)
    for copy in copies:
        copy.start()
    acc_ref[...] = jnp.zeros_like(acc_ref)
    ssq_ref[...] = jnp.zeros_like(ssq_ref)
    project([(low_ref, high_ref)], [own_ref], acc_ref, ssq_ref)
    for copy in copies:
        copy.wait()


def near_projection(mine, own_weight, weight, far, last):
    rows = 2 * mine[0].shape[0]
    channels, width = own_weight.shape[1:]
    return pl.pallas_call(
        functools.partial(near_kernel, far, last),
        out_shape=(
            jax.ShapeDtypeStruct((rows, 3 * width), F32),
            jax.ShapeDtypeStruct((rows, LANES), F32),
            weight_rows(weight, len(far), channels),
            weight_rows(weight, len(last), channels),
        ),
        in_specs=[VMEM] * 3 + [HBM],
        out_specs=(VMEM,) * 4,
        scratch_shapes=[
            pltpu.SemaphoreType.DMA((len(far),)),
            pltpu.SemaphoreType.DMA((len(last),)),
        ],
        compiler_params=params(16),
        cost_estimate=cost(),
        name="projections_near",
    )(*mine, own_weight, pltpu.with_memory_space_constraint(weight, pltpu.HBM))


def partial_kernel(sizes, *refs):
    blocks, rest = [], list(refs)
    for size in sizes:
        blocks.append(rest[:size])
        del rest[:size]
    weight_ref, acc_in, ssq_in, acc_ref, ssq_ref = rest
    acc_ref[...] = acc_in[...]
    ssq_ref[...] = ssq_in[...]
    project(blocks, split_rows(weight_ref, len(blocks)), acc_ref, ssq_ref)


def part_projection(blocks, weight, acc, ssq):
    sizes = tuple(len(pieces) for pieces in blocks)
    return pl.pallas_call(
        functools.partial(partial_kernel, sizes),
        out_shape=(
            jax.ShapeDtypeStruct(acc.shape, F32),
            jax.ShapeDtypeStruct(ssq.shape, F32),
        ),
        in_specs=[VMEM] * (sum(sizes) + 3),
        out_specs=(VMEM,) * 2,
        compiler_params=params(24),
        cost_estimate=cost(),
        name="projections_part",
    )(*[piece for pieces in blocks for piece in pieces], weight, acc, ssq)


def last_kernel(count, model, spread, *refs):
    blocks = [(refs[2 * n], refs[2 * n + 1]) for n in range(count)]
    weight_ref, acc_in, ssq_in = refs[2 * count : 2 * count + 3]
    outs, (acc_ref, ssq_ref) = refs[2 * count + 3 : -2], refs[-2:]
    acc_ref[...] = acc_in[...]
    ssq_ref[...] = ssq_in[...]
    project(blocks, split_rows(weight_ref, count), acc_ref, ssq_ref)
    msq = jnp.sum(ssq_ref[...], axis=1, keepdims=True) / model
    scale = lax.rsqrt(msq + EPS)
    rows = acc_ref.shape[0]
    width = weight_ref.shape[2]
    heads = width // HEAD_DIM
    place = lax.axis_index("ctx") // 2 if spread else 0
    for n, out in enumerate(outs):
        head = jnp.bitwise_xor(place, heads - 1 - n)
        for which in range(3):
            lanes = pl.ds(pl.multiple_of(which * width + head * HEAD_DIM, LANES), HEAD_DIM)
            out[which * rows : (which + 1) * rows, :] = (acc_ref[:, lanes] * scale).astype(BF16)


def last_projection(blocks, weight, acc, ssq, model, spread):
    rows = acc.shape[0]
    heads = weight.shape[2] // HEAD_DIM
    return pl.pallas_call(
        functools.partial(last_kernel, len(blocks), model, spread),
        out_shape=tuple(
            jax.ShapeDtypeStruct((3 * rows, HEAD_DIM), BF16) for _ in range(heads)
        ),
        in_specs=[VMEM] * (2 * len(blocks) + 3),
        out_specs=(VMEM,) * heads,
        scratch_shapes=[pltpu.VMEM(acc.shape, F32), pltpu.VMEM(ssq.shape, F32)],
        compiler_params=params(24),
        cost_estimate=cost(),
        name="projections_last",
    )(*[half for pair in blocks for half in pair], weight, acc, ssq)


def base_of(shape, axis, rows, y):
    index = lax.broadcasted_iota(jnp.int32, shape, axis)
    block = 2 * jnp.bitwise_xor(index // rows, lax.axis_index("ctx") // 2) + y
    return block * rows + index % rows


def scores_of(query, keys, rows, key_base):
    product = lax.dot_general(
        query, keys, (((1,), (1,)), ((), ())), preferred_element_type=F32
    ) * (1.0 / math.sqrt(HEAD_DIM))
    query_base = base_of((query.shape[0], 1), 0, rows, lax.axis_index("ctx") % 2)
    return jnp.where(query_base >= key_base, product, -1e30)


def most_kernel(count, taken, *refs):
    blocks, others = refs[:count], refs[count : 2 * count - 1]
    query_ref, top_ref, total_ref, summed_ref, key_ref, value_ref = refs[2 * count - 1 :]
    rows = blocks[0].shape[0] // 3
    for n, block in enumerate(blocks):
        spot = slice(n * rows, (n + 1) * rows)
        query_ref[spot, :] = block[:rows, :]
        key_ref[spot, :] = block[rows : 2 * rows, :]
        value_ref[spot, :] = block[2 * rows :, :]
    for n, other in enumerate(others, count):
        key_ref[n * rows : (n + 1) * rows, :] = other[:rows, :]
        value_ref[n * rows : (n + 1) * rows, :] = other[rows:, :]
    y = lax.axis_index("ctx") % 2
    key_base = jnp.concatenate(
        [
            base_of((1, count * rows), 1, rows, y),
            *(base_of((1, count * rows), 1, rows, 1 - y)[:, k * rows : (k + 1) * rows] for k in taken),
        ],
        axis=1,
    )
    scores = scores_of(query_ref[...], key_ref[...], rows, key_base)
    top = jnp.max(scores, axis=1, keepdims=True)
    expo = jnp.exp(scores - top)
    top_ref[...] = jnp.broadcast_to(top, top_ref.shape)
    total_ref[...] = jnp.broadcast_to(jnp.sum(expo, axis=1, keepdims=True), total_ref.shape)
    summed_ref[...] = jnp.dot(expo.astype(BF16), value_ref[...], preferred_element_type=F32)


def attend_most(blocks, others, taken):
    count = len(blocks)
    rows = blocks[0].shape[0] // 3
    keys = pltpu.VMEM(((2 * count - 1) * rows, HEAD_DIM), BF16)
    shape = jax.ShapeDtypeStruct((count * rows, LANES), F32)
    return pl.pallas_call(
        functools.partial(most_kernel, count, taken),
        out_shape=(jax.ShapeDtypeStruct((count * rows, HEAD_DIM), BF16), shape, shape, shape),
        in_specs=[VMEM] * (2 * count - 1),
        out_specs=(VMEM,) * 4,
        scratch_shapes=[keys, keys],
        compiler_params=params(16),
        cost_estimate=cost(),
        name="attention_most",
    )(*blocks, *others)


def rest_kernel(last, other_ref, query_ref, top_ref, total_ref, summed_ref, *outs):
    count = len(outs)
    rows = outs[0].shape[0]
    y = lax.axis_index("ctx") % 2
    key_base = base_of((1, count * rows), 1, rows, 1 - y)[:, last * rows : (last + 1) * rows]
    scores = scores_of(query_ref[...], other_ref[:rows, :], rows, key_base)
    before = top_ref[...]
    top = jnp.maximum(before[:, :1], jnp.max(scores, axis=1, keepdims=True))
    expo = jnp.exp(scores - top)
    fade = jnp.exp(before - top)
    total = total_ref[...] * fade + jnp.sum(expo, axis=1, keepdims=True)
    summed = summed_ref[...] * fade + jnp.dot(
        expo.astype(BF16), other_ref[rows:, :], preferred_element_type=F32
    )
    attended = (summed / total).astype(BF16)
    for n, out in enumerate(reversed(outs)):
        out[...] = attended[n * rows : (n + 1) * rows, :]


def attend_rest(other, state, count, last):
    rows = other.shape[0] // 2
    return pl.pallas_call(
        functools.partial(rest_kernel, last),
        out_shape=tuple(jax.ShapeDtypeStruct((rows, HEAD_DIM), BF16) for _ in range(count)),
        in_specs=[VMEM] * 5,
        out_specs=(VMEM,) * count,
        compiler_params=params(16),
        cost_estimate=cost(),
        name="attention_rest",
    )(other, *state)


def join_kernel(given, *refs):
    blocks, out = refs[:-1], refs[-1]
    for n, block in enumerate(blocks):
        head = jnp.bitwise_xor(lax.axis_index("ctx") // 2, given[n])
        out[:, pl.ds(pl.multiple_of(head * HEAD_DIM, LANES), HEAD_DIM)] = block[...]


def join(blocks, given):
    rows = blocks[0].shape[0]
    return pl.pallas_call(
        functools.partial(join_kernel, given),
        out_shape=jax.ShapeDtypeStruct((rows, len(blocks) * HEAD_DIM), BF16),
        in_specs=[VMEM] * len(blocks),
        out_specs=VMEM,
        compiler_params=params(4),
        cost_estimate=cost(),
        name="join_heads",
    )(*blocks)


def gathered_attention(message, heads, rows):
    parts = jnp.stack([m.reshape(3, rows, HEAD_DIM) for m in message], axis=2)
    query, keys, values = parts[0], parts[1], parts[2]
    keys = lax.all_gather(keys, "ctx", axis=0, tiled=True)
    values = lax.all_gather(values, "ctx", axis=0, tiled=True)
    query_pos = lax.axis_index("ctx") * rows + jnp.arange(rows, dtype=jnp.int32)
    key_pos = jnp.arange(keys.shape[0], dtype=jnp.int32)
    scores = jnp.einsum("qhd,khd->hqk", query, keys, preferred_element_type=F32)
    allowed = (query_pos[:, None] >= key_pos[None, :])[None]
    scores = jnp.where(allowed, scores / math.sqrt(HEAD_DIM), -1e30)
    expo = jnp.where(allowed, jnp.exp(scores - jnp.max(scores, axis=2, keepdims=True)), 0.0)
    total = jnp.sum(expo, axis=2)
    summed = jnp.einsum("hqk,khd->qhd", expo.astype(BF16), values, preferred_element_type=F32)
    return (summed / total.T[:, :, None]).astype(BF16).reshape(rows, heads * HEAD_DIM)


def body(gate_in, conv_in, value_in, filter_taps, norm_gain, qkv_weight):
    rows, channels = gate_in.shape
    ctx, tp = lax.axis_size("ctx"), lax.axis_size("tp")
    weight = jnp.transpose(qkv_weight, (1, 0, 2))
    heads = weight.shape[2] // HEAD_DIM
    model = weight.shape[1]
    chip_per_head = heads * 2 == ctx and heads & (heads - 1) == 0

    wide = SLAB * LANES

    def widened(value):
        return jnp.pad(value, ((0, 0), (0, wide - channels))) if channels < wide else value

    def narrowed(sent):
        if channels == wide:
            return sent
        return jnp.concatenate([sent[:, :channels], sent[:, wide:]], axis=1)

    def swapped(value, by):
        return lax.ppermute(value, "tp", [(i, i ^ by) for i in range(tp)])

    high, low, taps, gate = mixed_halves(
        *(widened(v) for v in (conv_in, value_in, filter_taps, gate_in))
    )
    rim_high, rim_low = (
        lax.ppermute(part, "ctx", [(i, i + 1) for i in range(ctx - 1)]) for part in (high, low)
    )
    gain = widened(norm_gain[None])
    sums_low, sums_high, taps, own_weight = own_part(low, high, taps, weight, channels)
    *high, x_high, last = high_part(rim_high, sums_high, taps, gate, gain)
    steps = [(tp >> n) ^ 1 for n in range(1, tp.bit_length() - 1)]
    offsets = []
    for by in steps:
        offsets += [o ^ by for o in [0] + offsets]
    sent_high, *halves = map(narrowed, high)
    near_high = [swapped(half, 1) for half in halves]
    x_high, near_high[0] = lax.optimization_barrier((x_high, near_high[0]))
    *low, beside_weight = low_part(
        rim_low, sums_low, x_high, last, taps, gate, gain, weight, (1,), channels
    )
    sent_low, *halves = map(narrowed, low)
    near_low = [swapped(half, 1) for half in halves]
    sent = (sent_low, sent_high)
    far = []
    for by in steps:
        far += [tuple(swapped(part, by) for part in pair) for pair in [sent] + far]
    acc, ssq, far_weight, last_weight = near_projection(
        sent, own_weight, weight, tuple(offsets), tuple(o ^ 1 for o in offsets)
    )
    acc, ssq = part_projection([near_low + near_high], beside_weight, acc, ssq)
    last_low, acc = lax.optimization_barrier((far[-1][0], acc))
    far[-1] = (last_low, far[-1][1])
    swaps = [tuple(swapped(part, 1) for part in pair) for pair in far]
    acc, ssq = part_projection(far, far_weight, acc, ssq)
    messages = last_projection(swaps, last_weight, acc, ssq, model, chip_per_head)
    if not chip_per_head:
        return gathered_attention(messages[::-1], heads, rows)

    def over_z(value, k):
        pairs = [(i * tp + t, (i ^ (2 * k)) * tp + (t ^ 1)) for i in range(ctx) for t in range(tp)]
        return lax.ppermute(value, ("ctx", "tp"), pairs)

    def over_y(value):
        return lax.ppermute(value, "ctx", [(i, i ^ 1) for i in range(ctx)])

    order = range(heads - 1, -1, -1)
    held = [over_z(value, k) for value, k in zip(messages, order)]
    others = [over_y(value[rows:]) for value in held]
    taken = TAKEN.get(heads, tuple(range(heads)))
    given = GIVEN.get(heads, tuple(order))
    held, others = held[::-1], [others[heads - 1 - k] for k in taken]
    state = attend_most(held, others[:-1], taken[:-1])
    done = attend_rest(others[-1], state, heads, taken[-1])
    return join([over_z(done[heads - 1 - k], k) for k in given], given)


def solution(mesh):
    placed = (
        P("ctx", "tp"),
        P("ctx", "tp"),
        P("ctx", "tp"),
        P(None, "tp"),
        P("tp"),
        P(None, None, "tp"),
    )
    return jax.shard_map(
        body, mesh=mesh, in_specs=placed, out_specs=P("ctx", "tp"), check_vma=False
    )
```

```python
import functools
import math

import jax
import jax.numpy as jnp
from jax import lax
from jax.experimental import pallas as pl
from jax.experimental.pallas import tpu as pltpu
from jax.sharding import PartitionSpec as P

HEAD_DIM = 128
LANES = 128
SLAB = 8
TAKEN = {4: (0, 3, 1, 2)}
GIVEN = {4: (2, 3, 1, 0)}
PHASES = 4
SUBS = 9
HELD = 8
EPS = 1e-06
BF16 = jnp.bfloat16
F32 = jnp.float32
VMEM = pl.BlockSpec(memory_space=pltpu.VMEM)
HBM = pl.BlockSpec(memory_space=pltpu.HBM)


def params(mib):
    return pltpu.CompilerParams(vmem_limit_bytes=mib << 20)


def cost():
    return pl.CostEstimate(flops=0, bytes_accessed=1024, transcendentals=0)


def slabs(count):
    return jax.ShapeDtypeStruct((count * SLAB, LANES), F32)


def slab_scratch(count):
    return pltpu.VMEM((count * SLAB, LANES), F32)


def at(index):
    if not isinstance(index, int):
        return pl.ds(pl.multiple_of(index * SLAB, SLAB), SLAB)
    return pl.ds(index * SLAB, SLAB)


def to_slabs(source, target):
    for group in range(SLAB):
        target[pl.ds(group, source.shape[0], stride=SLAB), :] = source[
            :, group * LANES : (group + 1) * LANES
        ].astype(F32)


def to_subs(source, count, target):
    for n in range(count):
        x0, x1, x2, x3 = (source[at(PHASES * n + p), :] for p in range(PHASES))
        low, high = x0 + x1, x2 + x3
        for s, value in enumerate((x0, x2, x0 + x2, x1, x3, x1 + x3, low, high, low + high)):
            target[at(s * count + n), :] = value


def accumulate(sums, first, lag, taps, tap_at, x_ref, x_at, x_first, x_count, span):
    sums = list(sums)
    for start in range(x_first, x_first + x_count, HELD):
        places = range(start, min(start + HELD, x_first + x_count))
        used = {}
        for i in places:
            x = x_ref[at(x_at + (i - x_first)), :]
            for k in range(len(sums)):
                j = lag + first + k - i
                if 0 <= j < span:
                    if j not in used:
                        used[j] = taps[at(tap_at + j), :]
                    sums[k] = sums[k] + used[j] * x
    return sums


def finish(z_ref, count, full_ref):
    def z(s, k):
        return z_ref[at(s * (count + 1) + k), :]

    before = [z(s, 0) for s in range(SUBS)]
    for n in range(count):
        now = [z(s, n + 1) for s in range(SUBS)]

        def even(s):
            return now[s] + before[s + 1]

        def odd(s, held):
            return held[s + 2] - held[s] - held[s + 1]

        a_even, a_odd, b_even, b_odd = even(0), odd(0, now), even(3), odd(3, now)
        full_ref[at(PHASES * n), :] = a_even + odd(3, before)
        full_ref[at(PHASES * n + 1), :] = even(6) - a_even - b_even
        full_ref[at(PHASES * n + 2), :] = a_odd + b_even
        full_ref[at(PHASES * n + 3), :] = odd(6, now) - a_odd - b_odd
        before = now


def emit(full_ref, gate_ref, first, gain_ref, sent_ref, first_half, second_half):
    rows = sent_ref.shape[0]
    squares = jnp.zeros((rows, LANES), F32)
    for group in range(SLAB):
        lanes = slice(group * LANES, (group + 1) * LANES)
        hyena = (
            (
                gate_ref[first : first + rows, lanes].astype(F32)
                * full_ref[pl.ds(group, rows, stride=SLAB), :]
            )
            .astype(BF16)
            .astype(F32)
        )
        squares = squares + hyena * hyena
        sent_ref[:, lanes] = (hyena * gain_ref[:, lanes]).astype(BF16)
    total = jnp.sum(squares, axis=1, keepdims=True)
    pieces = []
    for _ in range(3):
        pieces.append(total.astype(BF16).astype(F32))
        total = total - pieces[-1]
    lane = lax.broadcasted_iota(jnp.int32, (rows, LANES), 1)
    row = jnp.zeros((rows, LANES), F32)
    for place, piece in enumerate(pieces):
        row = jnp.where(lane == place, piece, row)
    sent_ref[:, SLAB * LANES :] = row.astype(BF16)
    first_half[...] = sent_ref[: rows // 2, :]
    second_half[...] = sent_ref[rows // 2 :, :]


def mixed_kernel(
    conv_hbm,
    value_hbm,
    taps_hbm,
    gate_hbm,
    high_ref,
    low_ref,
    taps_ref,
    gate_ref,
    conv_ref,
    value_ref,
    sems,
):
    half = high_ref.shape[0]
    pairs = (
        (conv_hbm, conv_ref),
        (value_hbm, value_ref),
        (taps_hbm, taps_ref),
        (gate_hbm, gate_ref),
    )
    copies = [
        pltpu.make_async_copy(source, target, sems.at[n])
        for n, (source, target) in enumerate(pairs)
    ]
    for copy in copies:
        copy.start()
    for copy in copies[:2]:
        copy.wait()
    mixed = (conv_ref[...].astype(F32) * value_ref[...].astype(F32)).astype(BF16)
    high_ref[...] = mixed[half:, :]
    low_ref[...] = mixed[: low_ref.shape[0], :]
    for copy in copies[2:]:
        copy.wait()


def mixed_halves(conv, value, taps, gate):
    rows, channels = conv.shape
    half = rows // 2
    arrays = (conv, value, taps, gate)
    return pl.pallas_call(
        mixed_kernel,
        out_shape=(
            jax.ShapeDtypeStruct((half, channels), BF16),
            jax.ShapeDtypeStruct((half, channels), BF16),
            jax.ShapeDtypeStruct(taps.shape, F32),
            jax.ShapeDtypeStruct(gate.shape, BF16),
        ),
        in_specs=[HBM] * 4,
        out_specs=(VMEM,) * 4,
        scratch_shapes=[
            pltpu.VMEM(conv.shape, BF16),
            pltpu.VMEM(conv.shape, BF16),
            pltpu.SemaphoreType.DMA((4,)),
        ],
        compiler_params=params(8),
        cost_estimate=cost(),
        name="conv_times_value",
    )(*(pltpu.with_memory_space_constraint(v, pltpu.HBM) for v in arrays))


def own_kernel(
    low_ref,
    high_ref,
    taps_ref,
    weight_hbm,
    sums_low,
    sums_high,
    tap_subs,
    weight_ref,
    slab_ref,
    x_subs,
    sems,
):
    half, span = high_ref.shape[0], taps_ref.shape[0]
    quarter, eighth = 2 * half // PHASES, half // PHASES
    tap_quarter = span // PHASES
    copies = weight_copies(weight_hbm, weight_ref, (0,), sems)
    for copy in copies:
        copy.start()
    to_slabs(low_ref.at[pl.ds(0, half)], slab_ref.at[pl.ds(0, half * SLAB)])
    to_slabs(high_ref, slab_ref.at[pl.ds(half * SLAB, half * SLAB)])
    to_subs(slab_ref, quarter, x_subs)
    to_slabs(taps_ref, slab_ref)
    to_subs(slab_ref, tap_quarter, tap_subs)

    def sub(s, _):
        zero = jnp.zeros((SLAB, LANES), F32)
        sums_low[at(s * eighth), :] = zero
        for first in (0, eighth):
            sums = accumulate(
                [zero] * eighth, first, 0, tap_subs, s * tap_quarter, x_subs, s * quarter,
                0, first + eighth, tap_quarter,
            )
            for k, value in enumerate(sums):
                n = first + k
                if n < eighth - 1:
                    sums_low[at(s * eighth + n + 1), :] = value
                else:
                    sums_high[at(s * (eighth + 1) + n + 1 - eighth), :] = value
        return 0

    lax.fori_loop(0, SUBS, sub, 0)
    for copy in copies:
        copy.wait()


def weight_copies(weight_hbm, weight_ref, offsets, sems, first=0):
    copies = []
    channels = weight_ref.shape[1] // len(offsets)
    for n, offset in enumerate(offsets):
        owner = jnp.bitwise_xor(lax.axis_index("tp"), offset)
        copies.append(
            pltpu.make_async_copy(
                weight_hbm.at[
                    pl.ds(first, weight_ref.shape[0]),
                    pl.ds(pl.multiple_of(owner * channels, channels), channels),
                    :,
                ],
                weight_ref.at[:, pl.ds(n * channels, channels), :],
                sems.at[n],
            )
        )
    return copies


def weight_rows(weight, count, channels, kinds=3):
    return jax.ShapeDtypeStruct((kinds, count * channels, weight.shape[2]), BF16)


def own_part(low, high, taps, weight, channels):
    rows, span = 2 * high.shape[0], taps.shape[0]
    quarter = rows // PHASES
    eighth = quarter // 2
    return pl.pallas_call(
        own_kernel,
        out_shape=(
            slabs(SUBS * eighth),
            slabs(SUBS * (eighth + 1)),
            slabs(SUBS * span // PHASES),
            weight_rows(weight, 1, channels),
        ),
        in_specs=[VMEM] * 3 + [HBM],
        out_specs=(VMEM,) * 4,
        scratch_shapes=[
            slab_scratch(max(rows, span)),
            slab_scratch(SUBS * quarter),
            pltpu.SemaphoreType.DMA((1,)),
        ],
        compiler_params=params(16),
        cost_estimate=cost(),
        name="fir_own_rows",
    )(low, high, taps, pltpu.with_memory_space_constraint(weight, pltpu.HBM))


def high_kernel(
    rim_ref,
    sums_ref,
    tap_subs,
    gate_ref,
    gain_ref,
    sent_ref,
    first_ref,
    second_ref,
    x_subs,
    last_ref,
    slab_ref,
    z_ref,
):
    rows = sent_ref.shape[0]
    eighth = rows // PHASES
    tap_quarter = tap_subs.shape[0] // SLAB // SUBS
    to_slabs(rim_ref, slab_ref)
    to_subs(slab_ref, eighth, x_subs)

    def sub(s, _):
        at_z = s * (eighth + 1)
        sums = [sums_ref[at(at_z + k), :] for k in range(eighth + 1)]
        sums = accumulate(
            sums, eighth - 1, 2 * eighth, tap_subs, s * tap_quarter, x_subs, s * eighth,
            eighth, eighth, tap_quarter,
        )
        for k, value in enumerate(sums):
            z_ref[at(at_z + k), :] = value
        last_ref[at(s), :] = sums[0]
        return 0

    lax.fori_loop(0, SUBS, sub, 0)
    finish(z_ref, eighth, slab_ref)
    emit(slab_ref, gate_ref, rows, gain_ref, sent_ref, first_ref, second_ref)


def sent_shapes(rows):
    return tuple(
        jax.ShapeDtypeStruct((length, (SLAB + 1) * LANES), BF16)
        for length in (rows, rows // 2, rows // 2)
    )


def high_part(rim, sums, taps, gate, gain):
    rows = rim.shape[0]
    eighth = rows // PHASES
    return pl.pallas_call(
        high_kernel,
        out_shape=sent_shapes(rows) + (slabs(SUBS * eighth), slabs(SUBS)),
        in_specs=[VMEM] * 5,
        out_specs=(VMEM,) * 5,
        scratch_shapes=[slab_scratch(rows), slab_scratch(SUBS * (eighth + 1))],
        compiler_params=params(16),
        cost_estimate=cost(),
        name="fir_later_rows",
    )(rim, sums, taps, gate, gain)


def low_kernel(
    offsets,
    rim_ref,
    sums_ref,
    x_high,
    last_ref,
    tap_subs,
    gate_ref,
    gain_ref,
    weight_hbm,
    sent_ref,
    first_ref,
    second_ref,
    weight_ref,
    slab_ref,
    x_subs,
    z_ref,
    sems,
):
    copies = weight_copies(weight_hbm, weight_ref, offsets, sems)
    for copy in copies:
        copy.start()
    rows = sent_ref.shape[0]
    eighth = rows // PHASES
    tap_quarter = tap_subs.shape[0] // SLAB // SUBS
    to_slabs(rim_ref.at[pl.ds(0, rows)], slab_ref)
    to_subs(slab_ref, eighth, x_subs)

    def sub(s, _):
        sums = [sums_ref[at(s * eighth + k), :] for k in range(eighth)]
        for x_ref, first in ((x_high, eighth), (x_subs, 0)):
            sums = accumulate(
                sums, -1, 2 * eighth, tap_subs, s * tap_quarter, x_ref, s * eighth,
                first, eighth, tap_quarter,
            )
        for k, value in enumerate(sums + [last_ref[at(s), :]]):
            z_ref[at(s * (eighth + 1) + k), :] = value
        return 0

    lax.fori_loop(0, SUBS, sub, 0)
    finish(z_ref, eighth, slab_ref)
    emit(slab_ref, gate_ref, 0, gain_ref, sent_ref, first_ref, second_ref)
    for copy in copies:
        copy.wait()


def low_part(rim, sums, x_high, last, taps, gate, gain, weight, offsets, channels):
    rows = gate.shape[0] // 2
    eighth = rows // PHASES
    return pl.pallas_call(
        functools.partial(low_kernel, offsets),
        out_shape=sent_shapes(rows) + (weight_rows(weight, len(offsets), channels, 2),),
        in_specs=[VMEM] * 7 + [HBM],
        out_specs=(VMEM,) * 4,
        scratch_shapes=[
            slab_scratch(rows),
            slab_scratch(SUBS * eighth),
            slab_scratch(SUBS * (eighth + 1)),
            pltpu.SemaphoreType.DMA((len(offsets),)),
        ],
        compiler_params=params(16),
        cost_estimate=cost(),
        name="fir_earlier_rows",
    )(
        rim,
        sums,
        x_high,
        last,
        taps,
        gate,
        gain,
        pltpu.with_memory_space_constraint(weight, pltpu.HBM),
    )


def project(blocks, weight_refs, acc_ref, ssq_ref):
    width = weight_refs[0][0].shape[1]
    whole = [jnp.concatenate([piece[...] for piece in pieces], axis=0) for pieces in blocks]
    channels = whole[0].shape[1] - LANES
    for block in whole:
        ssq_ref[...] += block[:, channels:].astype(F32)
    for which in range(3):
        lanes = slice(which * width, (which + 1) * width)
        total = acc_ref[:, lanes]
        for ref, block in zip(weight_refs, whole):
            total = total + jnp.dot(
                block[:, :channels],
                ref[which][...],
                preferred_element_type=F32,
            )
        acc_ref[:, lanes] = total


def split_rows(weight_ref, count):
    channels = weight_ref.shape[1] // count
    return [weight_ref.at[:, pl.ds(n * channels, channels), :] for n in range(count)]


def near_kernel(far, last, low_ref, high_ref, own_ref, weight_hbm, *refs):
    acc_ref, ssq_ref, beside_ref, far_ref, last_ref, beside_sems, far_sems, last_sems = refs
    copies = weight_copies(weight_hbm, beside_ref, (1,), beside_sems, 2)
    copies += weight_copies(weight_hbm, far_ref, far, far_sems)
    copies += weight_copies(weight_hbm, last_ref, last, last_sems)
    for copy in copies:
        copy.start()
    acc_ref[...] = jnp.zeros_like(acc_ref)
    ssq_ref[...] = jnp.zeros_like(ssq_ref)
    project([(low_ref, high_ref)], [own_ref], acc_ref, ssq_ref)
    for copy in copies:
        copy.wait()


def near_projection(mine, own_weight, weight, far, last):
    rows = 2 * mine[0].shape[0]
    channels, width = own_weight.shape[1:]
    return pl.pallas_call(
        functools.partial(near_kernel, far, last),
        out_shape=(
            jax.ShapeDtypeStruct((rows, 3 * width), F32),
            jax.ShapeDtypeStruct((rows, LANES), F32),
            weight_rows(weight, 1, channels, 1),
            weight_rows(weight, len(far), channels),
            weight_rows(weight, len(last), channels),
        ),
        in_specs=[VMEM] * 3 + [HBM],
        out_specs=(VMEM,) * 5,
        scratch_shapes=[
            pltpu.SemaphoreType.DMA((1,)),
            pltpu.SemaphoreType.DMA((len(far),)),
            pltpu.SemaphoreType.DMA((len(last),)),
        ],
        compiler_params=params(16),
        cost_estimate=cost(),
        name="projections_near",
    )(*mine, own_weight, pltpu.with_memory_space_constraint(weight, pltpu.HBM))


def partial_kernel(sizes, *refs):
    blocks, rest = [], list(refs)
    for size in sizes:
        blocks.append(rest[:size])
        del rest[:size]
    *weight_refs, acc_in, ssq_in, acc_ref, ssq_ref = rest
    acc_ref[...] = acc_in[...]
    ssq_ref[...] = ssq_in[...]
    parts = [split_rows(ref, len(blocks)) for ref in weight_refs]
    kinds = [
        [part[n].at[i] for part in parts for i in range(part[n].shape[0])]
        for n in range(len(blocks))
    ]
    project(blocks, kinds, acc_ref, ssq_ref)


def part_projection(blocks, weights, acc, ssq):
    sizes = tuple(len(pieces) for pieces in blocks)
    return pl.pallas_call(
        functools.partial(partial_kernel, sizes),
        out_shape=(
            jax.ShapeDtypeStruct(acc.shape, F32),
            jax.ShapeDtypeStruct(ssq.shape, F32),
        ),
        in_specs=[VMEM] * (sum(sizes) + len(weights) + 2),
        out_specs=(VMEM,) * 2,
        compiler_params=params(24),
        cost_estimate=cost(),
        name="projections_part",
    )(*[piece for pieces in blocks for piece in pieces], *weights, acc, ssq)


def last_kernel(count, model, spread, *refs):
    blocks = [(refs[2 * n], refs[2 * n + 1]) for n in range(count)]
    weight_ref, acc_in, ssq_in = refs[2 * count : 2 * count + 3]
    outs, (acc_ref, ssq_ref) = refs[2 * count + 3 : -2], refs[-2:]
    acc_ref[...] = acc_in[...]
    ssq_ref[...] = ssq_in[...]
    project(blocks, split_rows(weight_ref, count), acc_ref, ssq_ref)
    msq = jnp.sum(ssq_ref[...], axis=1, keepdims=True) / model
    scale = lax.rsqrt(msq + EPS)
    rows = acc_ref.shape[0]
    width = weight_ref.shape[2]
    heads = width // HEAD_DIM
    place = lax.axis_index("ctx") // 2 if spread else 0
    for n, out in enumerate(outs):
        head = jnp.bitwise_xor(place, heads - 1 - n)
        for which in range(3):
            lanes = pl.ds(pl.multiple_of(which * width + head * HEAD_DIM, LANES), HEAD_DIM)
            out[which * rows : (which + 1) * rows, :] = (acc_ref[:, lanes] * scale).astype(BF16)


def last_projection(blocks, weight, acc, ssq, model, spread):
    rows = acc.shape[0]
    heads = weight.shape[2] // HEAD_DIM
    return pl.pallas_call(
        functools.partial(last_kernel, len(blocks), model, spread),
        out_shape=tuple(
            jax.ShapeDtypeStruct((3 * rows, HEAD_DIM), BF16) for _ in range(heads)
        ),
        in_specs=[VMEM] * (2 * len(blocks) + 3),
        out_specs=(VMEM,) * heads,
        scratch_shapes=[pltpu.VMEM(acc.shape, F32), pltpu.VMEM(ssq.shape, F32)],
        compiler_params=params(24),
        cost_estimate=cost(),
        name="projections_last",
    )(*[half for pair in blocks for half in pair], weight, acc, ssq)


def base_of(shape, axis, rows, y):
    index = lax.broadcasted_iota(jnp.int32, shape, axis)
    block = 2 * jnp.bitwise_xor(index // rows, lax.axis_index("ctx") // 2) + y
    return block * rows + index % rows


def scores_of(query, keys, rows, key_base):
    product = lax.dot_general(
        query, keys, (((1,), (1,)), ((), ())), preferred_element_type=F32
    ) * (1.0 / math.sqrt(HEAD_DIM))
    query_base = base_of((query.shape[0], 1), 0, rows, lax.axis_index("ctx") % 2)
    return jnp.where(query_base >= key_base, product, -1e30)


def most_kernel(count, taken, *refs):
    blocks, others = refs[:count], refs[count : 2 * count - 1]
    query_ref, top_ref, total_ref, summed_ref, key_ref, value_ref = refs[2 * count - 1 :]
    rows = blocks[0].shape[0] // 3
    for n, block in enumerate(blocks):
        spot = slice(n * rows, (n + 1) * rows)
        query_ref[spot, :] = block[:rows, :]
        key_ref[spot, :] = block[rows : 2 * rows, :]
        value_ref[spot, :] = block[2 * rows :, :]
    for n, other in enumerate(others, count):
        key_ref[n * rows : (n + 1) * rows, :] = other[:rows, :]
        value_ref[n * rows : (n + 1) * rows, :] = other[rows:, :]
    y = lax.axis_index("ctx") % 2
    key_base = jnp.concatenate(
        [
            base_of((1, count * rows), 1, rows, y),
            *(base_of((1, count * rows), 1, rows, 1 - y)[:, k * rows : (k + 1) * rows] for k in taken),
        ],
        axis=1,
    )
    scores = scores_of(query_ref[...], key_ref[...], rows, key_base)
    top = jnp.max(scores, axis=1, keepdims=True)
    expo = jnp.exp(scores - top)
    top_ref[...] = jnp.broadcast_to(top, top_ref.shape)
    total_ref[...] = jnp.broadcast_to(jnp.sum(expo, axis=1, keepdims=True), total_ref.shape)
    summed_ref[...] = jnp.dot(expo.astype(BF16), value_ref[...], preferred_element_type=F32)


def attend_most(blocks, others, taken):
    count = len(blocks)
    rows = blocks[0].shape[0] // 3
    keys = pltpu.VMEM(((2 * count - 1) * rows, HEAD_DIM), BF16)
    shape = jax.ShapeDtypeStruct((count * rows, LANES), F32)
    return pl.pallas_call(
        functools.partial(most_kernel, count, taken),
        out_shape=(jax.ShapeDtypeStruct((count * rows, HEAD_DIM), BF16), shape, shape, shape),
        in_specs=[VMEM] * (2 * count - 1),
        out_specs=(VMEM,) * 4,
        scratch_shapes=[keys, keys],
        compiler_params=params(16),
        cost_estimate=cost(),
        name="attention_most",
    )(*blocks, *others)


def rest_kernel(last, other_ref, query_ref, top_ref, total_ref, summed_ref, *outs):
    count = len(outs)
    rows = outs[0].shape[0]
    y = lax.axis_index("ctx") % 2
    key_base = base_of((1, count * rows), 1, rows, 1 - y)[:, last * rows : (last + 1) * rows]
    scores = scores_of(query_ref[...], other_ref[:rows, :], rows, key_base)
    before = top_ref[...]
    top = jnp.maximum(before[:, :1], jnp.max(scores, axis=1, keepdims=True))
    expo = jnp.exp(scores - top)
    fade = jnp.exp(before - top)
    total = total_ref[...] * fade + jnp.sum(expo, axis=1, keepdims=True)
    summed = summed_ref[...] * fade + jnp.dot(
        expo.astype(BF16), other_ref[rows:, :], preferred_element_type=F32
    )
    attended = (summed / total).astype(BF16)
    for n, out in enumerate(reversed(outs)):
        out[...] = attended[n * rows : (n + 1) * rows, :]


def attend_rest(other, state, count, last):
    rows = other.shape[0] // 2
    return pl.pallas_call(
        functools.partial(rest_kernel, last),
        out_shape=tuple(jax.ShapeDtypeStruct((rows, HEAD_DIM), BF16) for _ in range(count)),
        in_specs=[VMEM] * 5,
        out_specs=(VMEM,) * count,
        compiler_params=params(16),
        cost_estimate=cost(),
        name="attention_rest",
    )(other, *state)


def join_kernel(given, *refs):
    blocks, out = refs[:-1], refs[-1]
    for n, block in enumerate(blocks):
        head = jnp.bitwise_xor(lax.axis_index("ctx") // 2, given[n])
        out[:, pl.ds(pl.multiple_of(head * HEAD_DIM, LANES), HEAD_DIM)] = block[...]


def join(blocks, given):
    rows = blocks[0].shape[0]
    return pl.pallas_call(
        functools.partial(join_kernel, given),
        out_shape=jax.ShapeDtypeStruct((rows, len(blocks) * HEAD_DIM), BF16),
        in_specs=[VMEM] * len(blocks),
        out_specs=VMEM,
        compiler_params=params(4),
        cost_estimate=cost(),
        name="join_heads",
    )(*blocks)


def gathered_attention(message, heads, rows):
    parts = jnp.stack([m.reshape(3, rows, HEAD_DIM) for m in message], axis=2)
    query, keys, values = parts[0], parts[1], parts[2]
    keys = lax.all_gather(keys, "ctx", axis=0, tiled=True)
    values = lax.all_gather(values, "ctx", axis=0, tiled=True)
    query_pos = lax.axis_index("ctx") * rows + jnp.arange(rows, dtype=jnp.int32)
    key_pos = jnp.arange(keys.shape[0], dtype=jnp.int32)
    scores = jnp.einsum("qhd,khd->hqk", query, keys, preferred_element_type=F32)
    allowed = (query_pos[:, None] >= key_pos[None, :])[None]
    scores = jnp.where(allowed, scores / math.sqrt(HEAD_DIM), -1e30)
    expo = jnp.where(allowed, jnp.exp(scores - jnp.max(scores, axis=2, keepdims=True)), 0.0)
    total = jnp.sum(expo, axis=2)
    summed = jnp.einsum("hqk,khd->qhd", expo.astype(BF16), values, preferred_element_type=F32)
    return (summed / total.T[:, :, None]).astype(BF16).reshape(rows, heads * HEAD_DIM)


def body(gate_in, conv_in, value_in, filter_taps, norm_gain, qkv_weight):
    rows, channels = gate_in.shape
    ctx, tp = lax.axis_size("ctx"), lax.axis_size("tp")
    weight = jnp.transpose(qkv_weight, (1, 0, 2))
    heads = weight.shape[2] // HEAD_DIM
    model = weight.shape[1]
    chip_per_head = heads * 2 == ctx and heads & (heads - 1) == 0

    wide = SLAB * LANES

    def widened(value):
        return jnp.pad(value, ((0, 0), (0, wide - channels))) if channels < wide else value

    def narrowed(sent):
        if channels == wide:
            return sent
        return jnp.concatenate([sent[:, :channels], sent[:, wide:]], axis=1)

    def swapped(value, by):
        return lax.ppermute(value, "tp", [(i, i ^ by) for i in range(tp)])

    high, low, taps, gate = mixed_halves(
        *(widened(v) for v in (conv_in, value_in, filter_taps, gate_in))
    )
    rim_high, rim_low = (
        lax.ppermute(part, "ctx", [(i, i + 1) for i in range(ctx - 1)]) for part in (high, low)
    )
    gain = widened(norm_gain[None])
    sums_low, sums_high, taps, own_weight = own_part(low, high, taps, weight, channels)
    *high, x_high, last = high_part(rim_high, sums_high, taps, gate, gain)
    steps = [(tp >> n) ^ 1 for n in range(1, tp.bit_length() - 1)]
    offsets = []
    for by in steps:
        offsets += [o ^ by for o in [0] + offsets]
    sent_high, *halves = map(narrowed, high)
    near_high = [swapped(half, 1) for half in halves]
    x_high, near_high[0] = lax.optimization_barrier((x_high, near_high[0]))
    *low, beside_weight = low_part(
        rim_low, sums_low, x_high, last, taps, gate, gain, weight, (1,), channels
    )
    sent_low, *halves = map(narrowed, low)
    near_low = [swapped(half, 1) for half in halves]
    sent = (sent_low, sent_high)
    far = []
    for by in steps:
        far += [tuple(swapped(part, by) for part in pair) for pair in [sent] + far]
    acc, ssq, beside_value, far_weight, last_weight = near_projection(
        sent, own_weight, weight, tuple(offsets), tuple(o ^ 1 for o in offsets)
    )
    acc, ssq = part_projection([near_low + near_high], (beside_weight, beside_value), acc, ssq)
    last_low, acc = lax.optimization_barrier((far[-1][0], acc))
    far[-1] = (last_low, far[-1][1])
    swaps = [tuple(swapped(part, 1) for part in pair) for pair in far]
    acc, ssq = part_projection(far, (far_weight,), acc, ssq)
    messages = last_projection(swaps, last_weight, acc, ssq, model, chip_per_head)
    if not chip_per_head:
        return gathered_attention(messages[::-1], heads, rows)

    def over_z(value, k):
        pairs = [(i * tp + t, (i ^ (2 * k)) * tp + (t ^ 1)) for i in range(ctx) for t in range(tp)]
        return lax.ppermute(value, ("ctx", "tp"), pairs)

    def over_y(value):
        return lax.ppermute(value, "ctx", [(i, i ^ 1) for i in range(ctx)])

    order = range(heads - 1, -1, -1)
    held = [over_z(value, k) for value, k in zip(messages, order)]
    others = [over_y(value[rows:]) for value in held]
    taken = TAKEN.get(heads, tuple(range(heads)))
    given = GIVEN.get(heads, tuple(order))
    held, others = held[::-1], [others[heads - 1 - k] for k in taken]
    state = attend_most(held, others[:-1], taken[:-1])
    done = attend_rest(others[-1], state, heads, taken[-1])
    return join([over_z(done[heads - 1 - k], k) for k in given], given)


def solution(mesh):
    placed = (
        P("ctx", "tp"),
        P("ctx", "tp"),
        P("ctx", "tp"),
        P(None, "tp"),
        P("tp"),
        P(None, None, "tp"),
    )
    return jax.shard_map(
        body, mesh=mesh, in_specs=placed, out_specs=P("ctx", "tp"), check_vma=False
    )
```
